128 devices in a mesh: fsdp: 2 (over z_lo), ctx: 8 (over z_hi, y), tp: 8 (over x, core).
Axes of the slice: x: 4, y: 4, z: 4 (z_hi: 2, z_lo: 2; z = z_hi * 2 + z_lo), core: 2. Of those that a mesh axis runs over, the one named last changes fastest.
Arguments:
- tokens: bfloat16 [2, 3072, 2048], P('fsdp', 'ctx'), may hold values from -6 to 6
- norm_in: float32 [2048], replicated, may hold values from 0.5 to 1.5
- norm_mid: float32 [2048], replicated, may hold values from 0.5 to 1.5
- router_att: float32 [2048, 8], replicated, may hold values from -0.09375 to 0.09375
- router_mlp: float32 [2048, 8], replicated, may hold values from -0.09375 to 0.09375
- kv_weight: bfloat16 [2, 2048, 2048], P(None, ('fsdp', 'ctx'), 'tp'), may hold values from -0.1875 to 0.1875
- query_weight: bfloat16 [8, 2048, 2048], P('ctx', 'fsdp', 'tp'), may hold values from -0.1875 to 0.1875
- output_weight: bfloat16 [8, 2048, 2048], P('ctx', 'tp', 'fsdp'), may hold values from -0.5 to 0.5
- gate_up_weight: bfloat16 [8, 2, 2048, 5632], P('ctx', None, 'fsdp', 'tp'), may hold values from -0.125 to 0.125
- down_weight: bfloat16 [8, 5632, 2048], P('ctx', 'tp', 'fsdp'), may hold values from -0.109375 to 0.109375
- routes_att: int32 [2, 3072, 2], P('fsdp', 'ctx'), may hold values from 0 to 7, all different within a row
- routes_mlp: int32 [2, 3072, 2], P('fsdp', 'ctx'), may hold values from 0 to 7, all different within a row
- cotangent: bfloat16 [2, 3072, 2048], P('fsdp', 'ctx'), may hold values from -6 to 6
Outputs:
- output: bfloat16 [2, 3072, 2048], P('fsdp', 'ctx')
- input_grad: float32 [2, 3072, 2048], P('fsdp', 'ctx')
- norm_in_grad: float32 [2048], P(('fsdp', 'ctx'))
- norm_mid_grad: float32 [2048], P(('fsdp', 'ctx'))
- router_att_grad: float32 [2048, 8], P(('fsdp', 'ctx'))
- router_mlp_grad: float32 [2048, 8], P(('fsdp', 'ctx'))
- kv_weight_grad: float32 [2, 2048, 2048], P(None, ('fsdp', 'ctx'), 'tp')
- query_weight_grad: float32 [8, 2048, 2048], P('ctx', 'fsdp', 'tp')
- output_weight_grad: float32 [8, 2048, 2048], P('ctx', 'tp', 'fsdp')
- gate_up_weight_grad: float32 [8, 2, 2048, 5632], P('ctx', None, 'fsdp', 'tp')
- down_weight_grad: float32 [8, 5632, 2048], P('ctx', 'tp', 'fsdp')
The draws below stay inside these ranges and needn't reach their ends.
Inputs may be any that keep to these rules, and one draw needn't show every extreme that they name: `routes_att`: each position names two different experts. `routes_mlp`: each position names two different experts.
All inputs are finite; a program needn't handle non-finite values.
Results may differ from the reference program's by a relative error of at most 0.025.
Values may be sent and summed in bfloat16 or wider, within the bound.
A program may use at most 256 MiB of HBM per device.

```python
from functools import partial
import jax
import jax.numpy as jnp
from jax import lax

D = 2048
HEADS = 16
HD = 128
FF = 5632
TOPK = 2
TOK = 384
EXPERTS = 8
SEQ = 3072
SEQS = 2
CAP = 96
QW = 2048
N_CTX = 8


def block_scale(stream_key, extent, cuts, low, largest):
    loudness, own = 1.0, jax.random.fold_in(stream_key, 6)
    for axis_at, blocks in cuts:
        heights = jnp.exp(jax.random.uniform(jax.random.fold_in(own, axis_at), (blocks,), jnp.float32, low / len(cuts), largest / len(cuts)))
        loudness = loudness * jnp.repeat(heights, extent[axis_at] // blocks).reshape([-1 if axis == axis_at else 1 for axis in range(len(extent))])
    return loudness


def different_ones(key, rows, count, top, lift):
    order = jax.random.permutation(jax.random.fold_in(key, 1), count)
    favour = order
    for power in range(3):
        favour = favour * favour // count
    favour = favour * lift // count
    lots = jax.random.randint(jax.random.fold_in(key, 2), (rows, count), 0, 4096) + favour
    sure = jax.random.permutation(jax.random.fold_in(key, 3), rows)[jnp.arange(count) % rows]
    lots = jnp.where(jnp.arange(rows)[:, None] == sure[None, :], 1 << 14, lots)
    merit = lots * count + jnp.arange(count)
    return lax.top_k(merit.astype(jnp.int32), top)[1].astype(jnp.int32)


def scatter_about(key, dims, scale, most, shards=(), kind=jnp.bfloat16):
    values = scale * jax.random.normal(key, dims, jnp.float32)
    if shards:
        values = values * block_scale(key, dims, shards, -0.22, 0.18)
    return jnp.clip(values, -most, most).astype(kind)


def setup_inputs(seed: int = 0) -> dict:
    keys = jax.random.split(jax.random.key(seed), 14)
    tokens = scatter_about(keys[0], (SEQS, SEQ, D), 1.0, 6.0, ((0, 2), (1, 8)))
    norm_in = jnp.clip(1.0 + 0.1 * jax.random.normal(keys[1], (D,), jnp.float32), 0.5, 1.5)
    norm_mid = jnp.clip(1.0 + 0.1 * jax.random.normal(keys[2], (D,), jnp.float32), 0.5, 1.5)
    router_att = scatter_about(keys[3], (D, EXPERTS), (2 * D) ** -0.5, 0.09375, (), jnp.float32)
    router_mlp = scatter_about(keys[4], (D, EXPERTS), (2 * D) ** -0.5, 0.09375, (), jnp.float32)
    kv_weight = scatter_about(keys[5], (2, D, QW), (D // 2) ** -0.5, 0.1875, ((1, 16), (2, 8)))
    query_weight = scatter_about(keys[6], (EXPERTS, D, QW), (D // 2) ** -0.5, 0.1875, ((0, 8), (1, 2), (2, 8)))
    output_weight = scatter_about(keys[7], (EXPERTS, QW, D), (QW // 16) ** -0.5, 0.5, ((0, 8), (1, 8), (2, 2)))
    gate_up_weight = scatter_about(keys[8], (EXPERTS, 2, D, FF), D ** -0.5, 0.125, ((0, 8), (2, 2), (3, 8)))
    down_weight = scatter_about(keys[9], (EXPERTS, FF, D), (FF // 2) ** -0.5, 0.109375, ((0, 8), (1, 8), (2, 2)))
    routes_att = different_ones(keys[10], SEQS * SEQ, EXPERTS, TOPK, 2048).reshape((SEQS, SEQ, TOPK))
    routes_mlp = different_ones(keys[11], SEQS * SEQ, EXPERTS, TOPK, 2048).reshape((SEQS, SEQ, TOPK))
    cotangent = scatter_about(keys[12], (SEQS, SEQ, D), 1.0, 6.0, ((0, 2), (1, 8)))
    return dict(tokens=tokens, norm_in=norm_in, norm_mid=norm_mid, router_att=router_att, router_mlp=router_mlp, kv_weight=kv_weight, query_weight=query_weight, output_weight=output_weight, gate_up_weight=gate_up_weight, down_weight=down_weight, routes_att=routes_att, routes_mlp=routes_mlp, cotangent=cotangent)


@jax.custom_vjp
def low(v):
    return lax.optimization_barrier(v.astype(jnp.bfloat16)).astype(jnp.float32)

@jax.custom_vjp
def low_back(v):
    return v

def low_keep(v):
    return (low(v), None)

def low_pass(kept, grad):
    return (grad,)

def back_keep(v):
    return (v, None)

def back_low(kept, grad):
    return (low(grad),)
low.defvjp(low_keep, low_pass)
low_back.defvjp(back_keep, back_low)
precise = lax.Precision.HIGHEST
epsilon = 1e-06
masked_score = -1e+30

def route_slots(routes_block, experts, capacity):
    count_rows, chosen = routes_block.shape
    flattened = routes_block.reshape(-1).astype(jnp.int32)
    labels = jnp.arange(experts, dtype=jnp.int32)
    onehot = (flattened[:, None] == labels[None, :]).astype(jnp.int32)
    before = jnp.cumsum(onehot, axis=0, dtype=jnp.int32) - onehot
    placed = lax.optimization_barrier(jnp.sum(before * onehot, axis=1, dtype=jnp.int32))
    retained = placed < capacity
    dumped = experts * capacity
    target = jnp.where(retained, flattened * capacity + placed, dumped).astype(jnp.int32)
    source = (jnp.arange(count_rows * chosen, dtype=jnp.int32) // chosen).astype(jnp.int32)
    slot_token = jnp.zeros((dumped,), jnp.int32).at[target].set(source, mode='drop')
    filled = jnp.zeros((dumped,), jnp.float32).at[target].set(1.0, mode='drop')
    return (target.reshape(count_rows, chosen), retained.reshape(count_rows, chosen), slot_token, filled)

def build_tables(routes):
    seqs = routes.shape[0]
    blocked = routes.reshape(seqs * N_CTX, TOK, TOPK)
    target, retained, slot_token, filled = jax.vmap(partial(route_slots, experts=EXPERTS, capacity=CAP))(blocked)
    offsets = (jnp.arange(N_CTX, dtype=jnp.int32) * TOK)[None, :, None, None]
    positions = slot_token.reshape(seqs, N_CTX, EXPERTS, CAP) + offsets
    positions = positions.transpose(0, 2, 1, 3).reshape(seqs * EXPERTS, N_CTX * CAP)
    return (target.reshape(seqs, N_CTX, TOK, TOPK), retained.reshape(seqs, N_CTX, TOK, TOPK).astype(jnp.float32), slot_token.reshape(seqs, N_CTX, EXPERTS * CAP), filled.reshape(seqs, N_CTX, EXPERTS * CAP), positions)

def rms_norm(values, gain_vector):
    row_scale = lax.rsqrt(lax.optimization_barrier(jnp.mean(values * values, axis=-1, keepdims=True)) + epsilon)
    return values * row_scale * gain_vector

def softmax_chosen(logits, routes):
    picked = jnp.take_along_axis(logits, routes, axis=-1)
    return jax.nn.softmax(picked, axis=-1)

def take_rows(matrix_rows, indices):
    return jnp.take(matrix_rows, indices, axis=0)

def take_blocks(matrix_rows, indices):
    return jax.vmap(jax.vmap(take_rows))(matrix_rows, indices)

def combine_blocks(returned, target, weight):
    seqs = target.shape[0]
    clipped = jnp.minimum(target, EXPERTS * CAP - 1)
    picked = take_blocks(returned, clipped.reshape(seqs, N_CTX, TOK * TOPK))
    picked = picked.reshape(seqs, N_CTX, TOK, TOPK, -1)
    return lax.optimization_barrier(jnp.sum(picked * weight[..., None], axis=3)).reshape(seqs, N_CTX * TOK, -1)

def expert_attention(slot_rows, positions, keys_seq, values_seq, query_matrix, output_matrix):
    row_count = slot_rows.shape[0]
    queries = low_back(low(jnp.dot(slot_rows, query_matrix, precision=precise))).reshape(row_count, HEADS, HD)
    keys_heads = keys_seq.reshape(-1, HEADS, HD)
    values_heads = values_seq.reshape(-1, HEADS, HD)
    scores = low_back(jnp.einsum('rhk,shk->hrs', queries, keys_heads, precision=precise) * HD ** (-0.5))
    key_positions = jnp.arange(keys_heads.shape[0], dtype=jnp.int32)
    allowed = key_positions[None, None, :] <= positions[None, :, None]
    weights_soft = jax.nn.softmax(jnp.where(allowed, scores, masked_score), axis=-1)
    mixed_values = jnp.einsum('hrs,shk->rhk', low(weights_soft), values_heads, precision=precise)
    attended = low_back(low(mixed_values.reshape(row_count, HEADS * HD)))
    return jnp.dot(attended, output_matrix, precision=precise)

def expert_mlp(slot_rows, gate_up_matrix, down_matrix):
    gate_pre = low_back(jnp.dot(slot_rows, gate_up_matrix[0], precision=precise))
    up_value = low_back(jnp.dot(slot_rows, gate_up_matrix[1], precision=precise))
    hidden_units = low(jax.nn.silu(gate_pre) * up_value)
    return jnp.dot(hidden_units, down_matrix, precision=precise)

def forward(params, routes_att, routes_mlp, att_tables, mlp_tables):
    tokens, norm_in, norm_mid, router_att, router_mlp, kv_weight, query_weight, output_weight, gate_up_weight, down_weight = params
    seqs, length, model_width = tokens.shape
    att_target, att_retained, att_slot_token, att_filled, att_positions = att_tables
    mlp_target, mlp_retained, mlp_slot_token, mlp_filled, mlp_positions = mlp_tables
    normed = rms_norm(tokens, norm_in)
    lowered = low(normed)
    att_gates = softmax_chosen(jnp.einsum('bsd,de->bse', lowered, router_att, precision=precise), routes_att)
    keys_all = low_back(low(jnp.einsum('bsd,df->bsf', lowered, kv_weight[0], precision=precise)))
    values_all = low_back(low(jnp.einsum('bsd,df->bsf', lowered, kv_weight[1], precision=precise)))
    att_slots = low_back(take_blocks(lowered.reshape(seqs, N_CTX, TOK, model_width), att_slot_token) * att_filled[..., None])
    expert_rows = att_slots.reshape(seqs, N_CTX, EXPERTS, CAP, model_width).transpose(0, 2, 1, 3, 4)
    expert_rows = expert_rows.reshape(seqs * EXPERTS, N_CTX * CAP, model_width)
    seq_index = jnp.repeat(jnp.arange(seqs, dtype=jnp.int32), EXPERTS)
    expert_index = jnp.tile(jnp.arange(EXPERTS, dtype=jnp.int32), seqs)

    def attend_pair(packed):
        slot_rows, positions, seq_at, expert_at = packed
        return expert_attention(slot_rows, positions, keys_all[seq_at], values_all[seq_at], query_weight[expert_at], output_weight[expert_at])
    projected = low_back(low(lax.map(jax.checkpoint(attend_pair), (expert_rows, att_positions, seq_index, expert_index))))
    returned = projected.reshape(seqs, EXPERTS, N_CTX, CAP, model_width).transpose(0, 2, 1, 3, 4)
    returned = returned.reshape(seqs, N_CTX, EXPERTS * CAP, model_width)
    att_weight = att_gates.reshape(seqs, N_CTX, TOK, TOPK) * att_retained
    hidden = tokens + combine_blocks(returned, att_target, att_weight)
    normed_mid = rms_norm(hidden, norm_mid)
    lowered_mid = low(normed_mid)
    mlp_gates = softmax_chosen(jnp.einsum('bsd,de->bse', lowered_mid, router_mlp, precision=precise), routes_mlp)
    mlp_slots = low_back(take_blocks(lowered_mid.reshape(seqs, N_CTX, TOK, model_width), mlp_slot_token) * mlp_filled[..., None])
    mlp_rows = mlp_slots.reshape(seqs, N_CTX, EXPERTS, CAP, model_width).transpose(2, 0, 1, 3, 4)
    mlp_rows = mlp_rows.reshape(EXPERTS, seqs * N_CTX * CAP, model_width)

    def mlp_expert(packed):
        slot_rows, gate_up_matrix, down_matrix = packed
        return expert_mlp(slot_rows, gate_up_matrix, down_matrix)
    mlp_out = low_back(low(lax.map(jax.checkpoint(mlp_expert), (mlp_rows, gate_up_weight, down_weight))))
    mlp_returned = mlp_out.reshape(EXPERTS, seqs, N_CTX, CAP, model_width).transpose(1, 2, 0, 3, 4)
    mlp_returned = mlp_returned.reshape(seqs, N_CTX, EXPERTS * CAP, model_width)
    mlp_weight = mlp_gates.reshape(seqs, N_CTX, TOK, TOPK) * mlp_retained
    return hidden + combine_blocks(mlp_returned, mlp_target, mlp_weight)

def reference(tokens, norm_in, norm_mid, router_att, router_mlp, kv_weight, query_weight, output_weight, gate_up_weight, down_weight, routes_att, routes_mlp, cotangent):
    att_tables = build_tables(routes_att)
    mlp_tables = build_tables(routes_mlp)
    params = (tokens.astype(jnp.float32), norm_in, norm_mid, router_att, router_mlp, kv_weight.astype(jnp.float32), query_weight.astype(jnp.float32), output_weight.astype(jnp.float32), gate_up_weight.astype(jnp.float32), down_weight.astype(jnp.float32))

    def wrapped(params):
        return forward(params, routes_att, routes_mlp, att_tables, mlp_tables)
    result, pullback = jax.vjp(wrapped, params)
    grads, = pullback(cotangent.astype(jnp.float32))
    return (result.astype(jnp.bfloat16), grads[0], grads[1], grads[2], grads[3], grads[4], grads[5], grads[6], grads[7], grads[8], grads[9])
```

```python
from functools import partial

import jax
import jax.numpy as jnp
from jax import lax
from jax.experimental import pallas as pl
from jax.experimental.pallas import tpu as pltpu
from jax.sharding import PartitionSpec as P

MESH = pl.DeviceIdType.MESH
HD = 128
CTX = 8
TP = 8
FSDP = 2
VLIM = 61 * 1024 * 1024
epsilon = 1e-06
masked_score = -1e30
f32 = jnp.float32
bf16 = jnp.bfloat16
DMA = pltpu.SemaphoreType.DMA
VM = pltpu.VMEM


def vmem(n):
    return [pl.BlockSpec(memory_space=pltpu.VMEM)] * n


def anywhere(n):
    return [pl.BlockSpec(memory_space=pl.ANY)] * n


def params(cid=None):
    if cid is None:
        return pltpu.CompilerParams(vmem_limit_bytes=VLIM)
    return pltpu.CompilerParams(collective_id=cid, has_side_effects=True, vmem_limit_bytes=VLIM)


def cost(us):
    return pl.CostEstimate(flops=0, bytes_accessed=int(us * 3.2e6), transcendentals=0)


def sds(shape, dtype):
    return jax.ShapeDtypeStruct(shape, dtype)


def nt(a, b):
    return lax.dot_general(a, b, (((1,), (1,)), ((), ())), preferred_element_type=f32)


def tn(a, b):
    return lax.dot_general(a, b, (((0,), (0,)), ((), ())), preferred_element_type=f32)


def nn(a, b):
    return jnp.dot(a, b, preferred_element_type=f32)


def wide(v):
    return v.astype(f32)


class Place:
    def __init__(self):
        self.f, self.c, self.t = lax.axis_index("fsdp"), lax.axis_index("ctx"), lax.axis_index("tp")
        self.x, self.k = self.t // 2, lax.rem(self.t, 2)
        self.xl, self.xr, self.xo = (lax.rem(self.x + i, 4) for i in (3, 1, 2))
        self.right, self.left = {"tp": self.xr * 2 + self.k}, {"tp": self.xl * 2 + self.k}
        self.sib = {"tp": self.x * 2 + 1 - self.k}
        self.zh, self.y = self.c // 4, lax.rem(self.c, 4)
        self.z = self.zh * 2 + self.f
        self.up, self.down = ({"ctx": self.zh * 4 + lax.rem(self.y + i, 4)} for i in (1, 3))
        self.across = {"ctx": lax.rem(self.c + 4, CTX)}
        self.partner = {"fsdp": 1 - self.f}
        self.above, self.below = (self.at_z(lax.rem(self.z + i, 4)) for i in (1, 3))

    def at_z(self, z):
        return {"fsdp": lax.rem(z, 2), "ctx": (z // 2) * 4 + self.y}

    def ctx_peers(self):
        return [{"ctx": lax.rem(self.c + j, CTX)} for j in range(1, CTX)]

    def tp_near(self):
        return [self.right, self.left, self.sib]

    def z_near(self):
        return [self.above, self.below]


def greet(peers):
    barrier = pltpu.get_barrier_semaphore()
    for axes in peers:
        pl.semaphore_signal(barrier, inc=1, device_id=axes, device_id_type=MESH)
    pl.semaphore_wait(barrier, len(peers))


class Net:
    def __init__(self, send, recv):
        self.send, self.recv, self.used, self.open = send, recv, 0, []

    def go(self, src, dst, axes):
        i = self.used
        self.used += 1
        d = pltpu.make_async_remote_copy(
            src_ref=src, dst_ref=dst, send_sem=self.send.at[i], recv_sem=self.recv.at[i],
            device_id=axes, device_id_type=MESH,
        )
        d.start()
        self.open.append(d)
        return d

    def drain(self):
        for d in self.open:
            d.wait_send()
        self.open = []


class Ring:
    def __init__(self, net, view, me, plus, minus):
        self.net, self.view, self.plus, self.minus = net, view, plus, minus
        self.me, self.low, self.high, self.far = me, lax.rem(me + 3, 4), lax.rem(me + 1, 4), lax.rem(me + 2, 4)

    def hop1(self, src=None):
        src = self.view(self.me, None) if src is None else src
        self.a = self.net.go(src, self.view(self.me, None), self.plus)
        self.b = self.net.go(src, self.view(self.me, None), self.minus)

    def hop2_low(self):
        self.a.wait_recv()
        self.a = self.net.go(self.view(self.low, 0), self.view(self.low, 0), self.plus)

    def hop2_high(self):
        self.b.wait_recv()
        self.b = self.net.go(self.view(self.high, 1), self.view(self.high, 1), self.minus)

    def hop2(self):
        self.hop2_low()
        self.hop2_high()

    def hop3(self):
        self.a.wait_recv()
        self.b.wait_recv()


class RingSum:
    def __init__(self, net, own, stage, land, me, plus, minus):
        self.net, self.own, self.stage, self.land, self.plus, self.minus = net, own, stage, land, plus, minus
        self.me, self.low, self.high, self.far = me, lax.rem(me + 3, 4), lax.rem(me + 1, 4), lax.rem(me + 2, 4)

    def put(self, position, part, value):
        r = self.stage(position, part)
        r[...] = value.astype(r.dtype)
        return r

    def hop1(self):
        self.a = self.net.go(self.put(self.far, 0, self.own(self.far, 0)), self.land("a"), self.plus)
        self.b = self.net.go(self.put(self.far, 1, self.own(self.far, 1)), self.land("b"), self.minus)

    def hop2(self):
        self.a.wait_recv()
        self.put(self.high, 0, self.own(self.high, 0) + wide(self.land("a")[...]))
        self.put(self.high, 1, self.own(self.high, 1))
        self.a = self.net.go(self.stage(self.high, None), self.land("l"), self.plus)
        self.b.wait_recv()
        self.put(self.low, 1, self.own(self.low, 1) + wide(self.land("b")[...]))
        self.put(self.low, 0, self.own(self.low, 0))
        self.b = self.net.go(self.stage(self.low, None), self.land("r"), self.minus)

    def hop3(self):
        self.a.wait_recv()
        self.b.wait_recv()
        return self.own(self.me, None) + wide(self.land("l")[...]) + wide(self.land("r")[...])


def part_of(part, size):
    half = size // 2
    return pl.ds(0, size) if part is None else pl.ds(part * half, half)


class Dispatch:
    def __init__(self, net, at, x_ref, o_ref, exchange=True):
        self.net, self.at, self.x_ref, self.o_ref, self.exchange = net, at, x_ref, o_ref, exchange
        self.n, self.rows, self.w = x_ref.shape

    def view(self, block, tt, part=None):
        half = self.rows // 2
        lo, size = (0, self.rows) if part is None else (part * half, half)
        row = pl.multiple_of(block * self.rows + lo, 16)
        return self.o_ref.at[pl.ds(row, size), pl.ds(pl.multiple_of(tt * self.w, self.w), self.w)]

    def start(self):
        c, n = self.at.c, self.n
        if self.exchange:
            self.blocks = [lax.rem(c + n - j, n) for j in range(n)]
            self.moves = [None]
            for j in range(1, n):
                e = lax.rem(c + j, n)
                self.moves.append(self.net.go(self.x_ref.at[e], self.view(c, self.at.t), {"ctx": e}))
            self.view(c, self.at.t)[...] = self.x_ref[c]
        else:
            self.blocks, self.moves = list(range(n)), [None] * n
            for j in range(n):
                self.view(j, self.at.t)[...] = self.x_ref[j]

    def sibling(self, b, tt):
        return self.net.go(self.view(b, tt), self.view(b, tt), self.at.sib)

    def hop1(self):
        at = self.at
        self.rings, self.sibs = [], []
        for b, move in zip(self.blocks, self.moves):
            if move is not None:
                move.wait_recv()
            ring = Ring(self.net, lambda xx, part, b=b: self.view(b, xx * 2 + at.k, part), at.x, at.right, at.left)
            ring.hop1()
            self.rings.append(ring)
            self.sibs.append(self.sibling(b, at.t))

    def hop2(self):
        at = self.at
        for b, ring in zip(self.blocks, self.rings):
            ring.hop2_low()
            self.sibs.append(self.sibling(b, at.xl * 2 + at.k))
            ring.hop2_high()
            self.sibs.append(self.sibling(b, at.xr * 2 + at.k))

    def hop3(self):
        at = self.at
        for b, ring in zip(self.blocks, self.rings):
            ring.hop3()
            self.sibs.append(self.sibling(b, at.xo * 2 + at.k))

    def finish(self):
        for s in self.sibs:
            s.wait_recv()

    COPIES = 8 * 9 + 7


class Collect:
    def __init__(self, net, at, p_ref, o_ref, sibbuf, abuf, bbuf, lbuf, rbuf, fbuf, exchange=True):
        self.net, self.at, self.p, self.o, self.exchange = net, at, p_ref, o_ref, exchange
        self.sibbuf, self.fbuf = sibbuf, fbuf
        self.lands = {"a": abuf, "b": bbuf, "l": lbuf, "r": rbuf}
        _, _, self.n, self.rows, self.w = p_ref.shape
        n, c = self.n, at.c
        self.blocks = [lax.rem(c + j, n) for j in range(1, n)] + [c] if exchange else list(range(n))

    def start(self, which=None):
        at = self.at
        self.sibs = [self.net.go(self.p.at[1 - at.k, :, b], self.sibbuf.at[:, b], at.sib) for b in self.blocks]

    def own(self, b, xx, part):
        s = part_of(part, self.rows)
        return wide(self.p[self.at.k, xx, b, s]) + wide(self.sibbuf[xx, b, s])

    def hop1(self):
        at = self.at
        self.rings = []
        for b, sib in zip(self.blocks, self.sibs):
            sib.wait_recv()
            ring = RingSum(
                self.net,
                partial(self.own, b),
                lambda xx, part, b=b: self.fbuf.at[xx, b, part_of(part, self.rows)],
                lambda name, b=b: self.lands[name].at[b],
                at.x, at.right, at.left,
            )
            ring.hop1()
            self.rings.append(ring)

    def hop2(self):
        for ring in self.rings:
            ring.hop2()

    def hop3(self):
        at = self.at
        self.moves = []
        for j, (b, ring) in enumerate(zip(self.blocks, self.rings)):
            total = ring.hop3()
            if self.exchange and j < self.n - 1:
                self.fbuf[at.x, b] = total.astype(self.fbuf.dtype)
                self.moves.append(self.net.go(self.fbuf.at[at.x, b], self.o.at[at.c, pl.ds(0, self.rows)], {"ctx": b}))
            else:
                self.o[b, pl.ds(0, self.rows)] = total.astype(self.o.dtype)

    def finish(self):
        for m in self.moves:
            m.wait_recv()

    COPIES = 8 * 5 + 7

    @staticmethod
    def scratch(n, rows, w):
        return [
            VM((4, n, rows, w), bf16), VM((n, rows // 2, w), bf16), VM((n, rows // 2, w), bf16),
            VM((n, rows, w), bf16), VM((n, rows, w), bf16), VM((4, n, rows, w), bf16),
        ]


def sems(n):
    return [DMA((n,)), DMA((n,))]


def exact(a, b):
    return jnp.dot(a, b, preferred_element_type=f32, precision=lax.Precision.HIGHEST)


def split3(v):
    high = v.astype(bf16)
    rest = v - wide(high)
    mid = rest.astype(bf16)
    return high, mid, (rest - wide(mid)).astype(bf16)


def three_rows(v):
    high, mid, low = split3(v)
    row = lax.broadcasted_iota(jnp.int32, (8, v.shape[1]), 0)
    pieces = jnp.where(row == 0, wide(high), jnp.where(row == 1, wide(mid), jnp.where(row == 2, wide(low), 0.0)))
    return pieces.astype(bf16)


def to_row_form(columns, rows):
    return columns.T[:rows]


def to_column_form(rows):
    fill = jnp.zeros((128 - rows.shape[0], rows.shape[1]), f32)
    return jnp.concatenate([rows, fill], axis=0).T


def route_columns(routes):
    row = lax.broadcasted_iota(jnp.int32, (8, routes.shape[1]), 0)
    both = jnp.where(row == 0, routes[0:1, :], jnp.where(row == 1, routes[1:2, :], 0)).astype(f32)
    columns = to_column_form(both)
    return columns[:, 0:1], columns[:, 1:2]


FIRST = 8


def hot_lanes(routes):
    lane = lax.broadcasted_iota(jnp.int32, (routes.shape[1], 128), 1).astype(f32)
    return [(lane == r + FIRST).astype(f32) for r in route_columns(routes)]


def pick_matrix(routes, cap):
    tok = routes.shape[1]
    lane = lax.broadcasted_iota(jnp.int32, (tok, 128), 1).astype(f32)
    columns = route_columns(routes)
    hot = [(lane == r).astype(f32) for r in columns]
    row = lax.broadcasted_iota(jnp.int32, (tok, tok), 0)
    col = lax.broadcasted_iota(jnp.int32, (tok, tok), 1)
    earlier = (col < row).astype(f32).astype(bf16)
    before = nn(earlier, (hot[0] + hot[1]).astype(bf16))
    slot = lax.broadcasted_iota(jnp.int32, (tok, CTX * 128), 1).astype(f32)
    out = []
    for r, o in zip(columns, hot):
        place = jnp.sum(before * o, axis=1, keepdims=True)
        target = jnp.where(place < cap, r * 128 + place, -1.0)
        out.append((slot == target).astype(f32).astype(bf16))
    return out


def pair_positions(pos_ref, g, cap):
    a, b = wide(pos_ref[2 * g]), wide(pos_ref[2 * g + 1])
    none = jnp.zeros_like(a)
    lane = lax.broadcasted_iota(jnp.int32, (a.shape[0], 256), 1)
    a = jnp.concatenate([a, none], axis=1)
    b = pltpu.roll(jnp.concatenate([b, none], axis=1), cap, 1)
    return jnp.where(lane < cap, a, b)[0:1, : 2 * cap].astype(jnp.int32)


def front_body(
    tokens, norm_in, router_t, routes_att, routes_mlp, cot, kv_w, q_own, o_own, gu_own,
    rows_att, rows_g, kv_seq, kv_full, pos_out, lowered, pick_att, pick_mlp, info, q_oth, o_oth, gu_oth,
    slots_att, slots_g, pos, send, recv,
):
    at, net = Place(), Net(send, recv)
    tok, width = tokens.shape
    kv_part, w = kv_w.shape[1:]
    cap, part = slots_att.shape[1:]

    def kvw(z, y, p):
        return kv_full.at[lax.rem(z, 2) * CTX + (z // 2) * 4 + y, part_of(p, kv_part)]

    own = kvw(at.z, at.y, None)
    own[:, :w] = kv_w[0]
    own[:, w:] = kv_w[1]
    greet(at.ctx_peers() + at.tp_near() + at.z_near())
    zring = Ring(net, lambda z, p: kvw(z, at.y, p), at.z, at.above, at.below)
    zring.hop1()
    moves = [net.go(q_own, q_oth, at.partner)]
    yrings = []

    def y_stage(z):
        ring = Ring(net, lambda y, p: kvw(z, y, p), at.y, at.up, at.down)
        ring.hop1()
        yrings.append(ring)

    y_stage(at.z)
    for i, r in enumerate(pick_matrix(routes_att[...], cap)):
        pick_att[i * tok : (i + 1) * tok, :] = r
    zring.hop2()
    y_stage(zring.low)
    y_stage(zring.high)
    x = wide(tokens[...])
    scale = lax.rsqrt(jnp.sum(x * x, axis=1, keepdims=True) / width + epsilon)
    lowered[...] = (x * scale * norm_in[...]).astype(bf16)
    mine = pl.ds(pl.multiple_of(at.t * part, part), part)
    both = pick_att[:tok, :] + pick_att[tok:, :]
    slots = tn(both, lowered[:, mine]).astype(bf16)
    for e in range(CTX):
        slots_att[e] = slots[e * 128 : e * 128 + cap]
    d_att = Dispatch(net, at, slots_att, rows_att)
    d_att.start()
    number = lax.broadcasted_iota(jnp.int32, (8, tok), 1)
    row = lax.broadcasted_iota(jnp.int32, (8, tok), 0)
    digits = jnp.where(row == 0, number // 16, jnp.where(row == 1, lax.rem(number, 16), 0)).astype(f32).astype(bf16)
    found = nn(digits, both)
    found = (found[0:1] * 16.0 + found[1:2]).astype(jnp.int32) + at.c * tok
    for e in range(CTX):
        pos[e] = jnp.broadcast_to(found[:, e * 128 : (e + 1) * 128], (8, 128))
    for j in range(1, CTX):
        e = lax.rem(at.c + j, CTX)
        moves.append(net.go(pos.at[e], pos_out.at[at.c], {"ctx": e}))
    pos_out[at.c] = pos[at.c]
    for i, r in enumerate(pick_matrix(routes_mlp[...], cap)):
        pick_mlp[i * tok : (i + 1) * tok, :] = r
    slots = tn(pick_mlp[:tok, :] + pick_mlp[tok:, :], cot[:, mine]).astype(bf16)
    for e in range(CTX):
        slots_g[e] = slots[e * 128 : e * 128 + cap]
    d_g = Dispatch(net, at, slots_g, rows_g)
    d_g.start()
    d_att.hop1()
    zring.hop3()
    y_stage(zring.far)
    logits = sum(nt(r, lowered[...]) for r in split3(router_t[...]))
    columns = to_column_form(jnp.concatenate([jnp.zeros_like(logits), logits], axis=0))
    hot = hot_lanes(routes_att[...])
    low = [jnp.sum(o * columns, axis=1, keepdims=True) for o in hot]
    lane = lax.broadcasted_iota(jnp.int32, (tok, 128), 1)
    g0 = 1.0 / (1.0 + jnp.exp(low[1] - low[0]))
    g1 = 1.0 / (1.0 + jnp.exp(low[0] - low[1]))
    info[...] = jnp.where(
        lane == 0, scale, jnp.where(lane == 1, g0, jnp.where(lane == 2, g1, columns / scale))
    )
    d_att.hop2()
    for ring in yrings:
        ring.hop2()
    d_g.hop1()
    for ring in yrings:
        ring.hop3()
    weights = kv_full[...].reshape(-1, 2 * w)
    kv_seq[at.c] = nn(lowered[...], weights).astype(bf16)
    over = net.go(kv_seq.at[at.c], kv_seq.at[at.c], at.across)

    def seq_ring(zh):
        return Ring(net, lambda y, p: kv_seq.at[zh * 4 + y, part_of(p, tok)], at.y, at.up, at.down)

    near, far = seq_ring(at.zh), seq_ring(1 - at.zh)
    near.hop1()
    moves.append(net.go(o_own, o_oth, at.partner))
    rows = gu_oth.shape[1]
    moves.append(net.go(gu_own.at[:, pl.ds(0, rows)], gu_oth, at.partner))
    d_att.hop3()
    d_g.hop2()
    over.wait_recv()
    far.hop1()
    d_att.finish()
    near.hop2()
    d_g.hop3()
    near.hop3()
    far.hop2()
    d_g.finish()
    far.hop3()
    for m in moves:
        m.wait_recv()
    net.drain()


def front(tokens, norm_in, router_t, routes_att, routes_mlp, cot, kv_w, q_own, o_own, gu_own, cap, chunk, cid):
    tok, width = tokens.shape
    part = width // TP
    _, kv_part, w = kv_w.shape
    wide_rows = sds((CTX * cap, width), bf16)
    pick = sds((2 * tok, CTX * 128), bf16)
    return pl.pallas_call(
        front_body,
        out_shape=(
            wide_rows, wide_rows, sds((CTX, tok, 2 * w), bf16), sds((FSDP * CTX, kv_part, 2 * w), bf16),
            sds((CTX, 8, 128), jnp.int32), sds((tok, width), bf16), pick, pick, sds((tok, 128), f32),
            sds(q_own.shape, bf16), sds(o_own.shape, bf16), sds((2, chunk, gu_own.shape[2]), bf16),
        ),
        in_specs=vmem(7) + anywhere(3),
        out_specs=tuple(vmem(9) + anywhere(3)),
        scratch_shapes=[VM((CTX, cap, part), bf16), VM((CTX, cap, part), bf16), VM((CTX, 8, 128), jnp.int32)]
        + sems(2 * Dispatch.COPIES + 64),
        compiler_params=params(cid),
        cost_estimate=cost(70),
    )(tokens, norm_in, router_t, routes_att, routes_mlp, cot, kv_w, q_own, o_own, gu_own)


def assemble(own, other, full, axis, f, sem):
    size = own.shape[axis]
    out = []
    for i, (src, pos) in enumerate(((own, f), (other, 1 - f))):
        s = pl.ds(pl.multiple_of(pos * size, size), size)
        dst = full.at[s] if axis == 0 else full.at[:, s]
        d = pltpu.make_async_copy(src, dst, sem.at[i])
        d.start()
        out.append(d)
    return out


def attend_body(
    cap, tok, first, rows_ref, q_own, q_oth, o_own, o_oth, kv_ref, pos_ref, gu_own,
    q_ref, att_ref, lse_ref, p_ref, gu_oth,
    wq, wo, vt_ref, local_sem, send, recv,
):
    at, net = Place(), Net(send, recv)
    heads = q_ref.shape[1] // HD
    width = heads * HD
    scale = HD ** (-0.5)
    total = q_ref.shape[0]
    load_q = assemble(q_own, q_oth, wq, 0, at.f, local_sem.at[0])
    load_o = assemble(o_own, o_oth, wo, 1, at.f, local_sem.at[1])
    greet([at.partner])
    chunk = gu_oth.shape[1]
    move = net.go(gu_own.at[:, pl.ds(first, chunk)], gu_oth, at.partner)
    for h in range(heads):
        vt_ref[h] = kv_ref[:, width + h * HD : width + (h + 1) * HD].T
    for d in load_q:
        d.wait()
    q_ref[...] = nn(rows_ref[...], wq[...]).astype(bf16)
    for d in load_o:
        d.wait()
    rows_at, keys_at = 2 * cap, 2 * tok
    for g in range(total // rows_at):
        lo = g * rows_at
        extent = (g + 1) * keys_at
        at_key = extent - keys_at
        pos = pair_positions(pos_ref, g, cap)
        for h in range(heads):
            cols = slice(h * HD, (h + 1) * HD)
            s = nt(kv_ref[:extent, cols], q_ref[lo : lo + rows_at, cols]) * scale
            ids = lax.broadcasted_iota(jnp.int32, (keys_at, rows_at), 0) + at_key
            last = jnp.where(ids <= pos, s[at_key:], masked_score)
            highest = jnp.max(last, axis=0, keepdims=True)
            if g:
                highest = jnp.maximum(highest, jnp.max(s[:at_key], axis=0, keepdims=True))
            e_last = jnp.exp(last - highest)
            sums = jnp.sum(e_last, axis=0, keepdims=True)
            mixed = nn(vt_ref[h, :, at_key:extent], e_last.astype(bf16))
            if g:
                e = jnp.exp(s[:at_key] - highest)
                sums = sums + jnp.sum(e, axis=0, keepdims=True)
                mixed = mixed + nn(vt_ref[h, :, :at_key], e.astype(bf16))
            att_ref[lo : lo + rows_at, cols] = (mixed / sums).T.astype(bf16)
            lse_ref[h : h + 1, lo : lo + rows_at] = highest + jnp.log(sums)
        out = nn(att_ref[lo : lo + rows_at, :], wo[...]).astype(bf16)
        for i in range(TP):
            for b in range(2):
                p_ref[i % 2, i // 2, 2 * g + b] = out[b * cap : (b + 1) * cap, i * width : (i + 1) * width]
    move.wait_recv()
    net.drain()


def attend(rows, q_own, q_oth, o_own, o_oth, kv, pos, gu_own, tok, cap, first, chunk, cid):
    heads = q_own.shape[1] // HD
    slots, width = rows.shape
    w = heads * HD
    return pl.pallas_call(
        partial(attend_body, cap, tok, first),
        out_shape=(
            sds((slots, w), bf16), sds((slots, w), bf16), sds((heads, slots), f32),
            sds((2, 4, slots // cap, cap, width // TP), bf16), sds((2, chunk, gu_own.shape[2]), bf16),
        ),
        in_specs=vmem(1) + anywhere(4) + vmem(2) + anywhere(1),
        out_specs=tuple(vmem(4) + anywhere(1)),
        scratch_shapes=[VM((width, w), bf16), VM((w, width), bf16), VM((heads, HD, kv.shape[0]), bf16), DMA((2, 2))] + sems(1),
        compiler_params=params(cid),
        cost_estimate=cost(25),
    )(rows, q_own, q_oth, o_own, o_oth, kv, pos, gu_own)


def all_peers(at):
    me = at.f * CTX + at.c
    out = []
    for j in range(1, FSDP * CTX):
        p = lax.rem(me + j, FSDP * CTX)
        out.append({"fsdp": p // CTX, "ctx": lax.rem(p, CTX)})
    return out


def tp_peers(at):
    return [{"tp": lax.rem(at.t + j, TP)} for j in range(1, TP)]


def tail_body(
    spans, split,
    p_ref, dkv, lowered, kv_full, mlp_ret, hidden, gates_mlp, pick_mlp, pick_att, att_picked, grad_hidden, info,
    routes, norm_in, router_t, norm_mid_grad, router_mlp_grad, tokens, *refs,
):
    count = len(spans)
    sources, refs = refs[:count], refs[count:]
    parts = list(zip(spans, sources))
    kvw_out, result, input_grad, minor_out = refs[:4]
    outs, refs = refs[4 : 4 + count], refs[4 + count :]
    bufs, refs = refs[:6], refs[6:]
    (stage_near, stage_far, ka, kb, kl, kr, fa, fb, fl, fr, over_out, over_in, kv_low,
     p2, c2_sib, c2_a, c2_b, c2_l, c2_r, c2_f,
     w_part, w_stage, w_half, w_whole, w_sum, wz_stage, wz_half, wz_whole,
     ret, kv_back, slots, x_res, x_in, small_out, small_in, minor, minor_in, minor_sum, rgrad, toks, tok_sem,
     send, recv) = refs
    at, net = Place(), Net(send, recv)
    tok, w = dkv.shape[1:]
    kv_part = kv_full.shape[1]
    part = hidden.shape[1]
    width = part * TP
    cap = mlp_ret.shape[1]
    mine = pl.ds(pl.multiple_of(at.t * part, part), part)
    load = pltpu.make_async_copy(tokens.at[:, mine], toks, tok_sem.at[0])
    load.start()
    ret[...] = jnp.zeros_like(ret)
    near_tp = tp_peers(at)
    far_all = all_peers(at)
    greet(far_all + near_tp)

    def bulk(lo, hi):
        return [net.go(span(src), out, at.partner) for (span, src), out in zip(parts[lo:hi], outs[lo:hi])]

    def seq_sum(zh, stage, lands):
        return RingSum(
            net,
            lambda y, p: wide(dkv[zh * 4 + y, part_of(p, tok)]),
            lambda y, p: stage.at[y, part_of(p, tok)],
            lambda name: lands[name],
            at.y, at.up, at.down,
        )

    moves = bulk(0, split[0])
    far = seq_sum(1 - at.zh, stage_far, {"a": fa, "b": fb, "l": fl, "r": fr})
    near = seq_sum(at.zh, stage_near, {"a": ka, "b": kb, "l": kl, "r": kr})
    far.hop1()
    near.hop1()
    col = Collect(net, at, p_ref, ret, *bufs)
    col.start()
    col.hop1()
    far.hop2()
    near.hop2()
    col.hop2()
    over_out[...] = far.hop3().astype(bf16)
    over = net.go(over_out, over_in, at.across)
    own = near.hop3()
    col.hop3()
    moves += bulk(split[0], split[1])

    for e in range(CTX):
        slots[e * 128 : e * 128 + cap, :] = mlp_ret[e]
        slots[e * 128 + cap : (e + 1) * 128, :] = jnp.zeros((128 - cap, part), bf16)
    picked = nn(pick_mlp[...], slots[...])
    gates = gates_mlp[...]
    value = hidden[...] + gates[:, 0:1] * picked[:tok] + gates[:, 1:2] * picked[tok:]
    x_res[...] = value.astype(bf16).reshape(x_res.shape)
    d_res = Dispatch(net, at, x_res, result, exchange=False)
    d_res.start()
    d_res.hop1()

    over.wait_recv()
    kv_low[...] = (own + wide(over_in[...])).astype(bf16)
    back = nt(kv_low[...], kv_full[...].reshape(-1, w)).astype(bf16)
    n2, rows2, w2 = p2.shape[2:]
    for i in range(TP):
        p2[i % 2, i // 2] = back[:, i * w2 : (i + 1) * w2].reshape(n2, rows2, w2)
    col2 = Collect(net, at, p2, kv_back, c2_sib, c2_a, c2_b, c2_l, c2_r, c2_f, exchange=False)
    col2.start()
    low = kv_low[...]
    for i in range(4):
        cols = width // 4
        block = tn(lowered[:, i * cols : (i + 1) * cols], low).astype(bf16)
        w_part[i * (cols // kv_part) : (i + 1) * (cols // kv_part)] = block.reshape(cols // kv_part, kv_part, w)
    col2.hop1()

    def index(z, y):
        return lax.rem(z, 2) * CTX + (z // 2) * 4 + y

    order = [lax.rem(at.z + i, 4) for i in (2, 1, 3, 0)]
    rings = []
    for i, z in enumerate(order):
        lands = {"a": w_half.at[i, 0], "b": w_half.at[i, 1], "l": w_whole.at[i, 0], "r": w_whole.at[i, 1]}
        rings.append(RingSum(
            net,
            lambda y, p, z=z: wide(w_part[index(z, y), part_of(p, kv_part)]),
            lambda y, p, i=i: w_stage.at[i, y, part_of(p, kv_part)],
            lambda name, lands=lands: lands[name],
            at.y, at.up, at.down,
        ))
    for ring in rings:
        ring.hop1()
    col2.hop2()
    d_res.hop2()
    for ring in rings:
        ring.hop2()
    col.finish()
    col2.hop3()

    load.wait()
    inputs = wide(toks[...])
    norm = norm_in[0:1, mine]
    gh = grad_hidden[...]
    back = nn(pick_att[...], ret[...].reshape(-1, part))
    back = back[:tok] + back[tok:] + wide(kv_back[...].reshape(tok, part))
    lane = lax.broadcasted_iota(jnp.int32, (tok, 128), 1)
    facts = info[...]
    d0 = jnp.sum(wide(att_picked[:tok, :]) * gh, axis=1, keepdims=True)
    d1 = jnp.sum(wide(att_picked[tok:, :]) * gh, axis=1, keepdims=True)
    inner = jnp.sum(back * norm * inputs, axis=1, keepdims=True)
    sums = jnp.where(lane == 0, d0, jnp.where(lane == 1, d1, jnp.where(lane == 2, inner, 0.0)))
    small_out[...] = to_row_form(sums, 8)
    smalls = [net.go(small_out, small_in.at[j], p) for j, p in enumerate(near_tp)]
    for z, ring in zip(order, rings):
        w_sum[z] = ring.hop3()
    lands = {"a": wz_half.at[0], "b": wz_half.at[1], "l": wz_whole.at[0], "r": wz_whole.at[1]}
    zsum = RingSum(
        net,
        lambda z, p: w_sum[z, part_of(p, kv_part)],
        lambda z, p: wz_stage.at[z, part_of(p, kv_part)],
        lambda name: lands[name],
        at.z, at.above, at.below,
    )
    zsum.hop1()
    total = small_out[...]
    for j, m in enumerate(smalls):
        m.wait_recv()
        total = total + small_in[j]
    sums = to_column_form(total)
    scale, g0, g1 = facts[:, 0:1], facts[:, 1:2], facts[:, 2:3]
    inner = g0 * sums[:, 0:1] + g1 * sums[:, 1:2]
    hot = hot_lanes(routes[...])
    grad_logits = hot[0] * (g0 * (sums[:, 0:1] - inner)) + hot[1] * (g1 * (sums[:, 1:2] - inner))
    grad_low = back
    for e in range(CTX):
        grad_low = grad_low + grad_logits[:, FIRST + e : FIRST + e + 1] * router_t[e : e + 1, mine]
    inner = sums[:, 2:3] + jnp.sum(grad_logits * facts, axis=1, keepdims=True)
    grad = gh + scale * (grad_low * norm) - inputs * (scale * scale * scale) * (inner / width)
    x_in[...] = grad.astype(bf16).reshape(x_in.shape)
    d_in = Dispatch(net, at, x_in, input_grad, exchange=False)
    d_in.start()
    d_in.hop1()
    rgrad[...] = sum(tn(g, lowered[:, mine]) for g in split3(grad_logits))
    norm_grad = jnp.sum(grad_low * inputs * scale, axis=0, keepdims=True)
    row = lax.broadcasted_iota(jnp.int32, (8, part), 0)
    minor[0:8, :] = jnp.where(row == 0, norm_grad, jnp.where(row == 1, norm_mid_grad[0:1, :], 0.0))
    minor[8:16, :] = rgrad[FIRST : FIRST + CTX, :]
    minor[16:24, :] = router_mlp_grad[FIRST : FIRST + CTX, :]
    minors = [net.go(minor, minor_in.at[j], p) for j, p in enumerate(far_all)]
    zsum.hop2()
    moves += bulk(split[1], count)
    d_in.hop2()
    d_res.hop3()
    total = minor[...]
    for j, m in enumerate(minors):
        m.wait_recv()
        total = total + minor_in[j]
    minor_sum[...] = total
    minors = [net.go(minor_sum, minor_out.at[at.t], p) for p in near_tp]
    minor_out[at.t] = total
    d_in.hop3()
    kvw_out[...] = zsum.hop3()
    d_res.finish()
    d_in.finish()
    col2.finish()
    for m in minors + moves:
        m.wait_recv()
    net.drain()


def tail(
    p, dkv, lowered, kv_full, mlp_ret, hidden, gates_mlp, pick_mlp, pick_att, att_picked, grad_hidden, info,
    routes, norm_in, router_t, norm_mid_grad, router_mlp_grad, tokens, bulk, split, cid,
):
    _, _, n, rows, w = p.shape
    _, tok, kw = dkv.shape
    part = kv_full.shape[1]
    n2 = 4
    rows2 = tok // n2
    width = w * TP
    spans = [b[1] for b in bulk]
    land = [VM((tok // 2, kw), bf16)] * 2 + [VM((tok, kw), bf16)] * 2
    col2 = Collect.scratch(n2, rows2, w)
    return pl.pallas_call(
        partial(tail_body, spans, split),
        out_shape=(
            sds((part, kw), f32), sds((tok, width), bf16), sds((tok, width), bf16), sds((TP, 24, w), f32),
        ) + tuple(sds(b[2], b[0].dtype) for b in bulk),
        in_specs=vmem(17) + anywhere(1 + len(bulk)),
        out_specs=tuple(vmem(4) + anywhere(len(bulk))),
        scratch_shapes=Collect.scratch(n, rows, w)
        + [VM((4, tok, kw), bf16)] * 2 + land + land
        + [VM((tok, kw), bf16)] * 3
        + [VM((2, 4, n2, rows2, w), bf16)] + col2
        + [
            VM((FSDP * CTX, part, kw), bf16), VM((4, 4, part, kw), bf16), VM((4, 2, part // 2, kw), bf16),
            VM((4, 2, part, kw), bf16), VM((4, part, kw), f32), VM((4, part, kw), bf16),
            VM((2, part // 2, kw), bf16), VM((2, part, kw), bf16),
            VM((n, 128, w), bf16), VM((n2, rows2, w), bf16), VM((n * 128, w), bf16),
            VM((n2, rows2, w), bf16), VM((n2, rows2, w), bf16), VM((8, tok), f32), VM((TP - 1, 8, tok), f32),
            VM((24, w), f32), VM((FSDP * CTX - 1, 24, w), f32), VM((24, w), f32), VM((128, w), f32),
            VM((tok, w), bf16), DMA((1,)),
        ]
        + sems(Collect.COPIES * 2 + Dispatch.COPIES * 2 + 100),
        compiler_params=params(cid),
        cost_estimate=cost(90),
    )(
        p, dkv, lowered, kv_full, mlp_ret, hidden, gates_mlp, pick_mlp, pick_att, att_picked, grad_hidden, info,
        routes, norm_in, router_t, norm_mid_grad, router_mlp_grad, tokens, *[b[0] for b in bulk],
    )


def mid_body(
    plan,
    p_att, pick_att, pick_mlp, info, routes, norm_mid_full, router_full, tokens, cot, rows_g, gu_own, gu_f, gu_a, down_own,
    att_picked, hidden, gates_out, grad_hidden, norm_grad, router_grad, grad_proj, p1, gu_sent, dd_sent,
    gu_grad, dd_grad, dd_got, gu_got,
    ret, b1_sib, b1_a, b1_b, b1_l, b1_r, fbuf,
    x_slots, X, G, W, D, gun, U, GG, GU, trans, p2, lm, small_out, small_in, small2_out, small2_in,
    sums_ref, gs_out, gs_in, sgm, sg_out, sg_in, sg_tot, sg_home, stage, toks, cots, local_sem, stage_sem, send, recv,
):
    at, net = Place(), Net(send, recv)
    tok, part = lm.shape
    ff = down_own.shape[0]
    half = down_own.shape[1]
    cap = x_slots.shape[1]
    pad = W.shape[1] - ff
    n_f, n_a = gu_f.shape[1], gu_a.shape[1]
    mine = pl.ds(pl.multiple_of(at.f * half, half), half)
    other = pl.ds(pl.multiple_of((1 - at.f) * half, half), half)
    near = tp_peers(at)
    ret[...] = jnp.zeros_like(ret)
    loads = []

    def load(src, dst):
        d = pltpu.make_async_copy(src, dst, local_sem.at[len(loads)])
        d.start()
        loads.append(d)
        return d

    here = pl.ds(pl.multiple_of(at.t * part, part), part)
    load_s = [load(tokens.at[:, here], toks), load(cot.at[:, here], cots)]
    load_g = load(rows_g, G)
    load_d = load(down_own, D.at[pl.ds(0, ff), mine])
    load_w = [
        load(gu_own, W.at[:, pl.ds(0, ff), mine]),
        load(gu_f, W.at[:, pl.ds(0, n_f), other]),
        load(gu_a, W.at[:, pl.ds(n_f, n_a), other]),
    ]
    greet(at.ctx_peers() + near + [at.partner])

    def down_piece(lo, hi):
        s = pl.ds(lo, hi - lo)
        return net.go(down_own.at[s], D.at[s, mine], at.partner)

    d_cut = plan["down"]
    down_moves = [down_piece(0, d_cut[0])]
    W[:, ff:, :] = jnp.zeros_like(W[:, ff:, :])
    D[ff:, :] = jnp.zeros_like(D[ff:, :])
    col1 = Collect(net, at, p_att, ret.at[0], b1_sib, b1_a, b1_b, b1_l, b1_r, fbuf)
    col1.start()
    col1.hop1()
    col1.hop2()
    col1.hop3()
    down_moves.append(down_piece(d_cut[0], d_cut[1]))
    col1.finish()

    lane = lax.broadcasted_iota(jnp.int32, (tok, 128), 1)
    hot = hot_lanes(routes[...])
    ga = [info[:, k : k + 1] for k in (1, 2)]
    norm = norm_mid_full[0:1, here]
    router_t = router_full[:, here]
    router = jnp.concatenate([jnp.zeros((FIRST, part), f32), router_t, jnp.zeros((128 - FIRST - CTX, part), f32)]).T
    for d in load_s:
        d.wait()
    picked = nn(pick_att[...], ret[0].reshape(-1, part))
    att_picked[...] = picked.astype(bf16)
    h = wide(toks[...]) + ga[0] * picked[:tok] + ga[1] * picked[tok:]
    hidden[...] = h
    raw = exact(h * norm, router)
    sums = jnp.where(lane == 0, jnp.sum(h * h, axis=1, keepdims=True), raw)
    small_out[...] = to_row_form(sums, 16)
    moves = [net.go(small_out, small_in.at[j], p) for j, p in enumerate(near)]
    total = small_out[...]
    for j, m in enumerate(moves):
        m.wait_recv()
        total = total + small_in[j]
    sums = to_column_form(total)
    scale = lax.rsqrt(sums[:, 0:1] / (part * TP) + epsilon)
    low = [jnp.sum(o * sums, axis=1, keepdims=True) * scale for o in hot]
    g0 = 1.0 / (1.0 + jnp.exp(low[1] - low[0]))
    g1 = 1.0 / (1.0 + jnp.exp(low[0] - low[1]))
    gates = jnp.where(lane == 0, g0, jnp.where(lane == 1, g1, jnp.where(lane == 2, scale, 0.0)))
    sums_ref[...] = sums
    gates_out[...] = gates
    lm[...] = (hidden[...] * scale * norm).astype(bf16)
    slots = tn(pick_mlp[:tok, :] + pick_mlp[tok:, :], lm[...]).astype(bf16)
    for e in range(CTX):
        x_slots[e] = slots[e * 128 : e * 128 + cap]
    d1 = Dispatch(net, at, x_slots, X)
    d1.start()
    rows2 = to_row_form(gates, 2)
    pair_row = jnp.concatenate([rows2[0:1], rows2[1:2]], axis=1)
    slot_gates = jnp.sum(nn(three_rows(pair_row), pick_mlp[...]), axis=0, keepdims=True)
    for e in range(CTX):
        gs_out[e] = jnp.broadcast_to(slot_gates[:, e * 128 : (e + 1) * 128], (8, 128))
    gs_moves = [net.go(gs_out.at[p["ctx"]], gs_in.at[at.c], p) for p in at.ctx_peers()]
    gs_in[at.c] = gs_out[at.c]
    down_moves.append(down_piece(d_cut[1], ff))
    last = pl.ds(n_f + n_a, ff - n_f - n_a)
    gu_move = net.go(gu_own.at[:, last], W.at[:, last, mine], at.partner)
    d1.hop1()
    for m in gs_moves:
        m.wait_recv()
    load_g.wait()
    for b in range(CTX):
        column = gs_in[b].T[:cap, 0:1]
        s = slice(b * cap, (b + 1) * cap)
        G[s, :] = (wide(G[s, :]) * column).astype(bf16)
    d1.hop2()
    load_d.wait()
    for m in down_moves:
        m.wait_recv()
    rows_at = 2 * cap
    groups = CTX // 2

    def group_rows(g):
        return pl.ds(pl.multiple_of(g * rows_at, rows_at), rows_at)

    @pl.loop(0, groups)
    def _(g):
        s = group_rows(g)
        gun[s, :] = nt(G[s, :], D[...])

    d1.hop3()
    d1.finish()
    for m in load_w:
        m.wait()
    gu_move.wait_recv()
    sgm[...] = jnp.zeros_like(sgm)

    def put(p_ref, g, out):
        for i in range(TP):
            for b in range(2):
                p_ref[i % 2, i // 2, 2 * g + b] = out[b * cap : (b + 1) * cap, i * part : (i + 1) * part]

    @pl.loop(0, groups)
    def _(g):
        s = group_rows(g)
        x = X[s, :]
        gate = nt(x, W[0])
        up = nt(x, W[1])
        sig = 1.0 / (1.0 + jnp.exp(-gate))
        silu = gate * sig
        units = (silu * up).astype(bf16)
        grad = gun[s, :]
        d_gate = (grad * up * (sig * (1.0 + gate * (1.0 - sig)))).astype(bf16)
        d_up = (grad * silu).astype(bf16)
        U[s, :] = units
        GG[s, :] = d_gate
        GU[s, :] = d_up
        column = jnp.sum(wide(units) * grad, axis=1, keepdims=True)
        for b in range(2):
            sgm[2 * g + b, :cap, :] = jnp.broadcast_to(column[b * cap : (b + 1) * cap], (cap, 128))
        put(p2, g, (nn(d_gate, W[0]) + nn(d_up, W[1])).astype(bf16))

    col2 = Collect(net, at, p2, ret.at[1], b1_sib, b1_a, b1_b, b1_l, b1_r, fbuf)
    net.drain()
    col2.start()
    for b in range(CTX):
        sg_out[b] = sgm[b].T[:8]
    sg_moves = [net.go(sg_out, sg_in.at[j], p) for j, p in enumerate(near)]

    @pl.loop(0, groups)
    def _(g):
        s = group_rows(g)
        put(p1, g, nn(U[s, :], D[...]).astype(bf16))

    col2.hop1()
    v = sg_out[...]
    for j, m in enumerate(sg_moves):
        m.wait_recv()
        v = v + sg_in[j]
    sg_tot[...] = v
    sg_moves = [net.go(sg_tot.at[p["ctx"]], sg_home.at[at.c], p) for p in at.ctx_peers()]
    sg_home[at.c] = sg_tot[at.c]

    cols = stage.shape[2]
    steps = half // cols
    trans[...] = U[...].T

    @pl.loop(0, steps)
    def _(i):
        src = pl.ds(pl.multiple_of((1 - at.f) * half + i * cols, cols), cols)
        dd_sent[:, pl.ds(pl.multiple_of(i * cols, cols), cols)] = nn(trans[...], G[:, src])[:ff].astype(bf16)

    cut = plan["dd"]
    got_moves = []

    def dd_piece(lo, hi):
        s = pl.ds(lo, hi - lo)
        got_moves.append(net.go(dd_sent.at[s], dd_got.at[s], at.partner))

    dd_piece(0, cut[0])
    col2.hop2()

    def own_part(matrix, dst, first):
        out = []
        for i in range(steps):
            slot = (first + i) % 2
            if first + i >= 2:
                stage_copies[first + i - 2].wait()
            src = pl.ds(pl.multiple_of(at.f * half + i * cols, cols), cols)
            stage[slot] = nn(trans[...], matrix[:, src])[:ff]
            d = pltpu.make_async_copy(stage.at[slot], dst(pl.ds(i * cols, cols)), stage_sem.at[slot])
            d.start()
            stage_copies.append(d)

    stage_copies = []
    own_part(G, lambda s: dd_grad.at[:, s], 0)
    col2.hop3()
    dd_piece(cut[0], cut[1])
    for j, grads in enumerate((GG, GU)):
        trans[...] = grads[...].T

        @pl.loop(0, steps)
        def _(i):
            src = pl.ds(pl.multiple_of((1 - at.f) * half + i * cols, cols), cols)
            gu_sent[j, :, pl.ds(pl.multiple_of(i * cols, cols), cols)] = nn(trans[...], X[:, src])[:ff].astype(bf16)

        if j == 0:
            own_part(X, lambda s: gu_grad.at[0, :, s], steps)
    col2.finish()

    lane = lax.broadcasted_iota(jnp.int32, (tok, 128), 1)
    hot = hot_lanes(routes[...])
    ga = [info[:, k : k + 1] for k in (1, 2)]
    norm = norm_mid_full[0:1, here]
    router_t = router_full[:, here]
    sums = sums_ref[...]
    gates = gates_out[...]
    scale = gates[:, 2:3]
    back = nn(pick_mlp[...], ret[1].reshape(-1, part))
    back = back[:tok] + back[tok:]
    h = hidden[...]
    inner = jnp.sum(back * norm * h, axis=1, keepdims=True)
    small2_out[...] = to_row_form(jnp.where(lane == 0, inner, 0.0), 8)
    moves = [net.go(small2_out, small2_in.at[j], p) for j, p in enumerate(near)]
    for m in sg_moves:
        m.wait_recv()
    row = jnp.concatenate([sg_home[e][0:1] for e in range(CTX)], axis=1)
    pairs = jnp.sum(nt(pick_mlp[...], three_rows(row)), axis=1, keepdims=True)
    sg = [pairs[:tok], pairs[tok:]]
    grad_logits = sum(
        o * (d - gates[:, k : k + 1] * (sg[0] + sg[1])) for k, (o, d) in enumerate(zip(hot, sg))
    )
    grad_low = back
    for e in range(CTX):
        grad_low = grad_low + grad_logits[:, FIRST + e : FIRST + e + 1] * router_t[e : e + 1, :]
    total = small2_out[...]
    for j, m in enumerate(moves):
        m.wait_recv()
        total = total + small2_in[j]
    inner = to_column_form(total)[:, 0:1] + jnp.sum(grad_logits * sums, axis=1, keepdims=True)
    gh = (
        wide(cots[...]) + scale * (grad_low * norm) - h * (scale * scale * scale) * (inner / (part * TP))
    )
    grad_hidden[...] = gh
    pair_rows = jnp.concatenate([(ga[0] * gh).astype(bf16), (ga[1] * gh).astype(bf16)], axis=0)
    slots = tn(pick_att[...], pair_rows).astype(bf16)
    for e in range(CTX):
        x_slots[e] = slots[e * 128 : e * 128 + cap]
    d2 = Dispatch(net, at, x_slots, grad_proj)
    d2.start()
    dd_piece(cut[1], ff)
    rows = gu_got.shape[1]
    got_moves.append(net.go(gu_sent.at[:, pl.ds(0, rows)], gu_got, at.partner))
    norm_grad[...] = jnp.broadcast_to(jnp.sum(grad_low * h * scale, axis=0, keepdims=True), norm_grad.shape)
    router_grad[...] = sum(tn(g, lm[...]) for g in split3(grad_logits))
    d2.hop1()
    d2.hop2()
    own_part(X, lambda s: gu_grad.at[1, :, s], 2 * steps)
    d2.hop3()
    d2.finish()
    for d in stage_copies[-2:]:
        d.wait()
    for m in got_moves:
        m.wait_recv()
    net.drain()


def mid(
    plan, p_att, pick_att, pick_mlp, info, routes, norm_mid, router_t, tokens, cot, rows_g, gu_own, gu_f, gu_a, down_own, cid,
):
    tok, width = tokens.shape
    part = width // TP
    _, _, n, cap, _ = p_att.shape
    slots, width = rows_g.shape
    ff, half = down_own.shape
    ffp = (ff + 255) // 256 * 256
    cols = 256
    bufs = Collect.scratch(n, cap, part)
    vm_out = (
        sds((2 * tok, part), bf16), sds((tok, part), f32), sds((tok, 128), f32), sds((tok, part), f32),
        sds((8, part), f32), sds((128, part), f32), sds((slots, width), bf16), sds(p_att.shape, bf16),
        sds((2, ff, half), bf16), sds((ff, half), bf16),
    )
    any_out = (sds((2, ff, half), f32), sds((ff, half), f32), sds((ff, half), bf16), sds((2, plan["gu"], half), bf16))
    return pl.pallas_call(
        partial(mid_body, plan),
        out_shape=vm_out + any_out,
        in_specs=vmem(7) + anywhere(7),
        out_specs=tuple(vmem(len(vm_out)) + anywhere(len(any_out))),
        scratch_shapes=[VM((2, n, 128, part), bf16)] + bufs
        + [
            VM((n, cap, part), bf16), VM((slots, width), bf16), VM((slots, width), bf16),
            VM((2, ffp, width), bf16), VM((ffp, width), bf16), VM((slots, ffp), f32),
            VM((slots, ffp), bf16), VM((slots, ffp), bf16), VM((slots, ffp), bf16), VM((ffp, slots), bf16),
            VM(p_att.shape, bf16), VM((tok, part), bf16),
            VM((16, tok), f32), VM((TP - 1, 16, tok), f32), VM((8, tok), f32), VM((TP - 1, 8, tok), f32),
            VM((tok, 128), f32), VM((n, 8, 128), f32), VM((n, 8, 128), f32), VM((n, 128, 128), f32),
            VM((n, 8, 128), f32), VM((TP - 1, n, 8, 128), f32), VM((n, 8, 128), f32), VM((n, 8, 128), f32),
            VM((2, ff, cols), f32), VM((tok, part), bf16), VM((tok, part), bf16), DMA((8,)), DMA((2,)),
        ]
        + sems(2 * Collect.COPIES + 2 * Dispatch.COPIES + 64),
        compiler_params=params(cid),
        cost_estimate=cost(140),
    )(
        p_att, pick_att, pick_mlp, info, routes, norm_mid, router_t, tokens, cot, rows_g, gu_own, gu_f, gu_a, down_own,
    )


def attend_back_body(
    cap, tok, span,
    grad_proj, rows_ref, q_ref, kv_ref, pos_ref, att_ref, lse_ref, p1, q_own, q_oth, o_own, o_oth, bulk_ref,
    dkv_ref, p3, mlp_ret, o_grad, q_grad, o_sent, q_sent, bulk_out,
    wq, wo, do_ref, dq_ref, kt_ref, acc_ref, b_sib, b_a, b_b, b_l, b_r, fbuf, local_sem, send, recv,
):
    at, net = Place(), Net(send, recv)
    heads = q_ref.shape[1] // HD
    width = heads * HD
    scale = HD ** (-0.5)
    total = q_ref.shape[0]
    load_o = assemble(o_own, o_oth, wo, 1, at.f, local_sem.at[0])
    load_q = assemble(q_own, q_oth, wq, 0, at.f, local_sem.at[1])
    greet(at.ctx_peers() + at.tp_near() + [at.partner])
    lo, size = span
    move = net.go(bulk_ref.at[:, pl.ds(lo, size)], bulk_out, at.partner)
    col = Collect(net, at, p1, mlp_ret, b_sib, b_a, b_b, b_l, b_r, fbuf)
    col.start()
    for h in range(heads):
        kt_ref[h] = kv_ref[:, h * HD : (h + 1) * HD].T
    for d in load_o:
        d.wait()
    do_ref[...] = nt(grad_proj[...], wo[...]).astype(bf16)
    col.hop1()
    acc_ref[...] = jnp.zeros_like(acc_ref)
    rows_at, keys_at = 2 * cap, 2 * tok
    for d in load_q:
        d.wait()
    groups = total // rows_at
    for step, g in enumerate(reversed(range(groups))):
        lo = g * rows_at
        rows = slice(lo, lo + rows_at)
        extent = (g + 1) * keys_at
        at_key = extent - keys_at
        pos = pair_positions(pos_ref, g, cap)
        for h in range(heads):
            cols = slice(h * HD, (h + 1) * HD)
            vcols = slice(width + h * HD, width + (h + 1) * HD)
            q = q_ref[rows, cols]
            do = do_ref[rows, cols]
            s = nt(kv_ref[:extent, cols], q) * scale
            lse = lse_ref[h : h + 1, rows]
            ids = lax.broadcasted_iota(jnp.int32, (keys_at, rows_at), 0) + at_key
            last = jnp.where(ids <= pos, s[at_key:], masked_score)
            s = jnp.concatenate([s[:at_key], last], axis=0) if g else last
            soft = jnp.exp(s - lse)
            dp = nt(kv_ref[:extent, vcols], do)
            inner = jnp.sum(soft * dp, axis=0, keepdims=True)
            ds = (soft * (dp - inner)).astype(bf16)
            acc_ref[:extent, vcols] += nn(soft.astype(bf16), do)
            acc_ref[:extent, cols] += nn(ds, q)
            dq_ref[rows, cols] = (nn(kt_ref[h, :, :extent], ds) * scale).T.astype(bf16)
        out = nt(dq_ref[rows, :], wq[...]).astype(bf16)
        for i in range(TP):
            for b in range(2):
                p3[i % 2, i // 2, 2 * g + b] = out[b * cap : (b + 1) * cap, i * width : (i + 1) * width]
        if step == 0:
            col.hop2()
        if step == 1:
            col.hop3()
    dkv_ref[:, :width] = (acc_ref[:, :width] * scale).astype(bf16)
    dkv_ref[:, width:] = acc_ref[:, width:].astype(bf16)
    half = o_own.shape[1]
    step_cols = 256
    att_t = att_ref[...].T
    for i in range(half // step_cols):
        here = slice(i * step_cols, (i + 1) * step_cols)
        mine = pl.ds(pl.multiple_of(at.f * half + i * step_cols, step_cols), step_cols)
        other = pl.ds(pl.multiple_of((1 - at.f) * half + i * step_cols, step_cols), step_cols)
        o_sent[:, here] = nn(att_t, grad_proj[:, other]).astype(bf16)
        o_grad[:, here] = nn(att_t, grad_proj[:, mine])
        q_sent[here, :] = tn(rows_ref[:, other], dq_ref[...]).astype(bf16)
        q_grad[here, :] = tn(rows_ref[:, mine], dq_ref[...])
    col.finish()
    move.wait_recv()
    net.drain()


def attend_back(grad_proj, rows_att, q, kv, pos, att, lse, p1, q_own, q_oth, o_own, o_oth, bulk, span, tok, cap, cid):
    heads = q.shape[1] // HD
    slots, width = rows_att.shape
    w = heads * HD
    half = width // 2
    _, _, n, _, part = p1.shape
    return pl.pallas_call(
        partial(attend_back_body, cap, tok, span),
        out_shape=(
            sds(kv.shape, bf16), sds(p1.shape, bf16), sds((n, cap, part), bf16), sds((w, half), f32),
            sds((half, w), f32), sds((w, half), bf16), sds((half, w), bf16), sds((2, span[1], bulk.shape[2]), bf16),
        ),
        in_specs=vmem(8) + anywhere(5),
        out_specs=tuple(vmem(7) + anywhere(1)),
        scratch_shapes=[
            VM((width, w), bf16), VM((w, width), bf16), VM((slots, w), bf16), VM((slots, w), bf16),
            VM((heads, HD, kv.shape[0]), bf16), VM(kv.shape, f32),
        ]
        + Collect.scratch(n, cap, part) + [DMA((2, 2))] + sems(Collect.COPIES + 1),
        compiler_params=params(cid),
        cost_estimate=cost(35),
    )(grad_proj, rows_att, q, kv, pos, att, lse, p1, q_own, q_oth, o_own, o_oth, bulk)


def local(
    tokens, norm_in, norm_mid, router_att, router_mlp, kv_weight, query_weight, output_weight,
    gate_up_weight, down_weight, routes_att, routes_mlp, cotangent,
):
    f, c = lax.axis_index("fsdp"), lax.axis_index("ctx")
    count_rows, width = tokens.shape[1:]
    capacity = count_rows * 2 // CTX
    half = width // 2
    local_width = query_weight.shape[2]
    tokens, cotangent = tokens[0], cotangent[0]
    q_own, o_own, down_own = query_weight[0], output_weight[0], down_weight[0]
    gu_own = gate_up_weight[0].transpose(0, 2, 1)
    routes_att, routes_mlp = routes_att[0].T, routes_mlp[0].T
    norm_in, norm_mid = norm_in[None], norm_mid[None]
    router_att, router_mlp = router_att.T, router_mlp.T
    hidden_count = gu_own.shape[1]
    unit = hidden_count // 44
    gu_front, gu_attend = 8 * unit, 16 * unit
    plan = {"down": (22 * unit, 36 * unit), "dd": (10 * unit, 22 * unit), "gu": 4 * unit}
    gu_back, gu_tail = 24 * unit, 14 * unit

    rows_att, rows_g, kv_seq, kv_full, positions, lowered, pick_att, pick_mlp, info, q_oth, o_oth, gu_0 = front(
        tokens, norm_in, router_att, routes_att, routes_mlp, cotangent, kv_weight, q_own, o_own, gu_own,
        capacity, gu_front, 1,
    )
    kv_seq = kv_seq.reshape(-1, 2 * local_width)
    queries, attended, log_totals, p_att, gu_1 = attend(
        rows_att, q_own, q_oth, o_own, o_oth, kv_seq, positions, gu_own, count_rows, capacity, gu_front, gu_attend, 2
    )
    (
        att_picked, hidden, gates_mlp, grad_hidden, norm_mid_grad, router_mlp_grad, grad_proj, p_mlp, gu_sent, dd_sent,
        gu_grad, dd_grad, dd_got, gu_got_0,
    ) = mid(
        plan, p_att, pick_att, pick_mlp, info, routes_mlp, norm_mid, router_mlp, tokens, cotangent,
        rows_g, gu_own, gu_0, gu_1, down_own, 3,
    )
    dkv, p_back, mlp_ret, o_grad, q_grad, o_sent, q_sent, gu_got_1 = attend_back(
        grad_proj, rows_att, queries, kv_seq, positions, attended, log_totals, p_mlp, q_own, q_oth, o_own, o_oth,
        gu_sent, (plan["gu"], gu_back), count_rows, capacity, 4,
    )
    at_tail = plan["gu"] + gu_back
    last = hidden_count - at_tail - gu_tail
    bulk = [
        (gu_sent, lambda r: r.at[:, pl.ds(at_tail, gu_tail)], (2, gu_tail, half)),
        (gu_sent, lambda r: r.at[:, pl.ds(at_tail + gu_tail, last)], (2, last, half)),
        (o_sent, lambda r: r, o_sent.shape),
        (q_sent, lambda r: r, q_sent.shape),
    ]
    kvw_grad, result, input_grad, minor, gu_got_2, gu_got_3, o_got, q_got = tail(
        p_back, dkv.reshape(CTX, count_rows, 2 * local_width), lowered, kv_full, mlp_ret, hidden, gates_mlp,
        pick_mlp, pick_att, att_picked, grad_hidden, info, routes_att, norm_in, router_att,
        norm_mid_grad, router_mlp_grad, tokens, bulk, (1, 3), 5,
    )
    me = f * CTX + c
    minor = lax.dynamic_index_in_dim(minor, me // 2, 0, keepdims=False)
    minor = lax.dynamic_slice_in_dim(minor, lax.rem(me, 2) * 128, 128, 1)
    gu_got = jnp.concatenate([gu_got_0, gu_got_1, gu_got_2, gu_got_3], axis=1)
    gate_up_grad = gu_grad + gu_got.astype(f32)
    return (
        result[None], input_grad.astype(f32)[None], minor[0], minor[1], minor[8:16].T, minor[16:24].T,
        jnp.stack([kvw_grad[:, :local_width], kvw_grad[:, local_width:]]),
        (q_grad + q_got.astype(f32))[None], (o_grad + o_got.astype(f32))[None],
        gate_up_grad.transpose(0, 2, 1)[None], (dd_grad + dd_got.astype(f32))[None],
    )


def solution(mesh):
    placed = (
        P("fsdp", "ctx", None), P(), P(), P(), P(),
        P(None, ("fsdp", "ctx"), "tp"), P("ctx", "fsdp", "tp"), P("ctx", "tp", "fsdp"),
        P("ctx", None, "fsdp", "tp"), P("ctx", "tp", "fsdp"),
        P("fsdp", "ctx", None), P("fsdp", "ctx", None), P("fsdp", "ctx", None),
    )
    return jax.shard_map(
        local,
        mesh=mesh,
        in_specs=placed,
        out_specs=(
            P("fsdp", "ctx", None), P("fsdp", "ctx", None), P(("fsdp", "ctx")), P(("fsdp", "ctx")),
            P(("fsdp", "ctx"), None), P(("fsdp", "ctx"), None), P(None, ("fsdp", "ctx"), "tp"),
            P("ctx", "fsdp", "tp"), P("ctx", "tp", "fsdp"), P("ctx", None, "fsdp", "tp"), P("ctx", "tp", "fsdp"),
        ),
        check_vma=False,
    )
```

```python
from functools import partial

import jax
import jax.numpy as jnp
from jax import lax
from jax.experimental import pallas as pl
from jax.experimental.pallas import tpu as pltpu
from jax.sharding import PartitionSpec as P

MESH = pl.DeviceIdType.MESH
HD = 128
CTX = 8
TP = 8
FSDP = 2
VLIM = 61 * 1024 * 1024
epsilon = 1e-06
masked_score = -1e30
f32 = jnp.float32
bf16 = jnp.bfloat16
DMA = pltpu.SemaphoreType.DMA
VM = pltpu.VMEM


def vmem(n):
    return [pl.BlockSpec(memory_space=pltpu.VMEM)] * n


def anywhere(n):
    return [pl.BlockSpec(memory_space=pl.ANY)] * n


def params(cid=None):
    if cid is None:
        return pltpu.CompilerParams(vmem_limit_bytes=VLIM)
    return pltpu.CompilerParams(collective_id=cid, has_side_effects=True, vmem_limit_bytes=VLIM)


def cost(us):
    return pl.CostEstimate(flops=0, bytes_accessed=int(us * 3.2e6), transcendentals=0)


def sds(shape, dtype):
    return jax.ShapeDtypeStruct(shape, dtype)


def nt(a, b):
    return lax.dot_general(a, b, (((1,), (1,)), ((), ())), preferred_element_type=f32)


def tn(a, b):
    return lax.dot_general(a, b, (((0,), (0,)), ((), ())), preferred_element_type=f32)


def nn(a, b):
    return jnp.dot(a, b, preferred_element_type=f32)


def wide(v):
    return v.astype(f32)


class Place:
    def __init__(self):
        self.f, self.c, self.t = lax.axis_index("fsdp"), lax.axis_index("ctx"), lax.axis_index("tp")
        self.x, self.k = self.t // 2, lax.rem(self.t, 2)
        self.xl, self.xr, self.xo = (lax.rem(self.x + i, 4) for i in (3, 1, 2))
        self.right, self.left = {"tp": self.xr * 2 + self.k}, {"tp": self.xl * 2 + self.k}
        self.sib = {"tp": self.x * 2 + 1 - self.k}
        self.zh, self.y = self.c // 4, lax.rem(self.c, 4)
        self.z = self.zh * 2 + self.f
        self.up, self.down = ({"ctx": self.zh * 4 + lax.rem(self.y + i, 4)} for i in (1, 3))
        self.across = {"ctx": lax.rem(self.c + 4, CTX)}
        self.partner = {"fsdp": 1 - self.f}
        self.above, self.below = (self.at_z(lax.rem(self.z + i, 4)) for i in (1, 3))

    def at_z(self, z):
        return {"fsdp": lax.rem(z, 2), "ctx": (z // 2) * 4 + self.y}

    def ctx_peers(self):
        return [{"ctx": lax.rem(self.c + j, CTX)} for j in range(1, CTX)]

    def tp_near(self):
        return [self.right, self.left, self.sib]

    def z_near(self):
        return [self.above, self.below]


def greet(peers):
    barrier = pltpu.get_barrier_semaphore()
    for axes in peers:
        pl.semaphore_signal(barrier, inc=1, device_id=axes, device_id_type=MESH)
    pl.semaphore_wait(barrier, len(peers))


def all_peers(at):
    me = at.f * CTX + at.c
    out = []
    for j in range(1, FSDP * CTX):
        p = lax.rem(me + j, FSDP * CTX)
        out.append({"fsdp": p // CTX, "ctx": lax.rem(p, CTX)})
    return out


def tp_peers(at):
    return [{"tp": lax.rem(at.t + j, TP)} for j in range(1, TP)]


class Net:
    def __init__(self, send, recv, base=0):
        self.send, self.recv, self.used, self.open = send, recv, base, []

    def go(self, src, dst, axes):
        i = self.used
        self.used += 1
        d = pltpu.make_async_remote_copy(
            src_ref=src, dst_ref=dst, send_sem=self.send.at[i], recv_sem=self.recv.at[i],
            device_id=axes, device_id_type=MESH,
        )
        d.start()
        self.open.append(d)
        return d

    def drain(self):
        for d in self.open:
            d.wait_send()
        self.open = []


class Ring:
    def __init__(self, net, view, me, plus, minus):
        self.net, self.view, self.plus, self.minus = net, view, plus, minus
        self.me, self.low, self.high, self.far = me, lax.rem(me + 3, 4), lax.rem(me + 1, 4), lax.rem(me + 2, 4)

    def hop1(self, src=None):
        src = self.view(self.me, None) if src is None else src
        self.a = self.net.go(src, self.view(self.me, None), self.plus)
        self.b = self.net.go(src, self.view(self.me, None), self.minus)

    def hop2_low(self):
        self.a.wait_recv()
        self.a = self.net.go(self.view(self.low, 0), self.view(self.low, 0), self.plus)

    def hop2_high(self):
        self.b.wait_recv()
        self.b = self.net.go(self.view(self.high, 1), self.view(self.high, 1), self.minus)

    def hop2(self):
        self.hop2_low()
        self.hop2_high()

    def hop3(self):
        self.a.wait_recv()
        self.b.wait_recv()


class RingSum:
    def __init__(self, net, own, stage, land, me, plus, minus):
        self.net, self.own, self.stage, self.land, self.plus, self.minus = net, own, stage, land, plus, minus
        self.me, self.low, self.high, self.far = me, lax.rem(me + 3, 4), lax.rem(me + 1, 4), lax.rem(me + 2, 4)

    def put(self, position, part, value):
        r = self.stage(position, part)
        r[...] = value.astype(r.dtype)
        return r

    def hop1(self):
        self.a = self.net.go(self.put(self.far, 0, self.own(self.far, 0)), self.land("a"), self.plus)
        self.b = self.net.go(self.put(self.far, 1, self.own(self.far, 1)), self.land("b"), self.minus)

    def hop2(self):
        self.a.wait_recv()
        self.put(self.high, 0, self.own(self.high, 0) + wide(self.land("a")[...]))
        self.put(self.high, 1, self.own(self.high, 1))
        self.a = self.net.go(self.stage(self.high, None), self.land("l"), self.plus)
        self.b.wait_recv()
        self.put(self.low, 1, self.own(self.low, 1) + wide(self.land("b")[...]))
        self.put(self.low, 0, self.own(self.low, 0))
        self.b = self.net.go(self.stage(self.low, None), self.land("r"), self.minus)

    def hop3(self):
        self.a.wait_recv()
        self.b.wait_recv()
        return self.own(self.me, None) + wide(self.land("l")[...]) + wide(self.land("r")[...])


class Feeder:
    def __init__(self, net, partner, items):
        self.net, self.partner, self.moves, self.queue = net, partner, [], []
        for src, dst, axis, first, rows, unit in items:
            self.queue += [(src, dst, axis, first, lo, min(unit, rows - lo)) for lo in range(0, rows, unit)]

    def feed(self, count):
        for src, dst, axis, first, lo, size in self.queue[:count]:
            s, d = pl.ds(first + lo, size), pl.ds(lo, size)
            a, b = (src.at[s], dst.at[d]) if axis == 0 else (src.at[:, s], dst.at[:, d])
            self.moves.append(self.net.go(a, b, self.partner))
        self.queue = self.queue[count:]

    def finish(self):
        assert not self.queue
        for m in self.moves:
            m.wait_recv()


class Local:
    def __init__(self, sem):
        self.sem, self.used = sem, 0

    def go(self, src, dst):
        d = pltpu.make_async_copy(src, dst, self.sem.at[self.used])
        self.used += 1
        d.start()
        return d


def part_of(part, size):
    half = size // 2
    return pl.ds(0, size) if part is None else pl.ds(part * half, half)


class Dispatch:
    def __init__(self, net, at, x_ref, o_ref, exchange=True):
        self.net, self.at, self.x_ref, self.o_ref, self.exchange = net, at, x_ref, o_ref, exchange
        self.n, self.rows, self.w = x_ref.shape

    def view(self, block, tt, part=None):
        half = self.rows // 2
        lo, size = (0, self.rows) if part is None else (part * half, half)
        row = pl.multiple_of(block * self.rows + lo, 16)
        return self.o_ref.at[pl.ds(row, size), pl.ds(pl.multiple_of(tt * self.w, self.w), self.w)]

    def start(self):
        c, n = self.at.c, self.n
        if self.exchange:
            self.blocks = [lax.rem(c + n - j, n) for j in range(n)]
            self.moves = [None]
            for j in range(1, n):
                e = lax.rem(c + j, n)
                self.moves.append(self.net.go(self.x_ref.at[e], self.view(c, self.at.t), {"ctx": e}))
            self.view(c, self.at.t)[...] = self.x_ref[c]
        else:
            self.blocks, self.moves = list(range(n)), [None] * n
            for j in range(n):
                self.view(j, self.at.t)[...] = self.x_ref[j]

    def sibling(self, b, tt):
        return self.net.go(self.view(b, tt), self.view(b, tt), self.at.sib)

    def hop1(self):
        at = self.at
        self.rings, self.sibs = [], []
        for b, move in zip(self.blocks, self.moves):
            if move is not None:
                move.wait_recv()
            ring = Ring(self.net, lambda xx, part, b=b: self.view(b, xx * 2 + at.k, part), at.x, at.right, at.left)
            ring.hop1()
            self.rings.append(ring)
            self.sibs.append(self.sibling(b, at.t))

    def hop2(self):
        at = self.at
        for b, ring in zip(self.blocks, self.rings):
            ring.hop2_low()
            self.sibs.append(self.sibling(b, at.xl * 2 + at.k))
            ring.hop2_high()
            self.sibs.append(self.sibling(b, at.xr * 2 + at.k))

    def hop3(self):
        at = self.at
        for b, ring in zip(self.blocks, self.rings):
            ring.hop3()
            self.sibs.append(self.sibling(b, at.xo * 2 + at.k))

    def finish(self):
        for s in self.sibs:
            s.wait_recv()

    COPIES = 8 * 9 + 7


class Collect:
    def __init__(
        self, net, at, p_ref, o_ref, sibbuf, abuf, bbuf, lbuf, rbuf, fbuf, exchange=True, home_net=None, total=None
    ):
        self.net, self.at, self.p, self.o, self.exchange = net, at, p_ref, o_ref, exchange
        self.home_net = net if home_net in (None, "late") else home_net
        self.total = fbuf.at[at.x] if total is None else total
        self.sibbuf, self.fbuf = sibbuf, fbuf
        self.lands = {"a": abuf, "b": bbuf, "l": lbuf, "r": rbuf}
        _, _, self.n, self.rows, self.w = p_ref.shape
        n, c = self.n, at.c
        self.late = home_net == "late"
        self.blocks = [lax.rem(c + j, n) for j in range(1, n)] + [c] if exchange and not self.late else list(range(n))
        self.sibs, self.rings, self.moves = [None] * n, [None] * n, []

    def start(self, which=None):
        at = self.at
        for j in range(self.n) if which is None else which:
            b = self.blocks[j]
            self.sibs[j] = self.net.go(self.p.at[1 - at.k, :, b], self.sibbuf.at[:, b], at.sib)

    def own(self, b, xx, part):
        s = part_of(part, self.rows)
        return wide(self.p[self.at.k, xx, b, s]) + wide(self.sibbuf[xx, b, s])

    def hop1(self, which=None):
        at = self.at
        for j in range(self.n) if which is None else which:
            b = self.blocks[j]
            self.sibs[j].wait_recv()
            ring = RingSum(
                self.net,
                partial(self.own, b),
                lambda xx, part, b=b: self.fbuf.at[xx, b, part_of(part, self.rows)],
                lambda name, b=b: self.lands[name].at[b],
                at.x, at.right, at.left,
            )
            ring.hop1()
            self.rings[j] = ring

    def hop2(self, which=None):
        for j in range(self.n) if which is None else which:
            self.rings[j].hop2()

    def hop3(self, which=None):
        for j in range(self.n) if which is None else which:
            b = self.blocks[j]
            total = self.rings[j].hop3()
            if self.late:
                self.total[b] = total.astype(self.fbuf.dtype)
            elif self.exchange and j < self.n - 1:
                self.total[b] = total.astype(self.fbuf.dtype)
                self.to_home(b)
            else:
                self.o[b, pl.ds(0, self.rows)] = total.astype(self.o.dtype)

    def to_home(self, b):
        home = self.o.at[self.at.c, pl.ds(0, self.rows)]
        self.moves.append(self.home_net.go(self.total.at[b], home, {"ctx": b}))

    def all_home(self):
        c, n = self.at.c, self.n
        for j in range(1, n):
            self.to_home(lax.rem(c + j, n))
        self.o[c, pl.ds(0, self.rows)] = self.total[c]

    def finish(self):
        for m in self.moves:
            m.wait_recv()

    COPIES = 8 * 5 + 7

    @staticmethod
    def scratch(n, rows, w):
        return [
            VM((4, n, rows, w), bf16), VM((n, rows // 2, w), bf16), VM((n, rows // 2, w), bf16),
            VM((n, rows, w), bf16), VM((n, rows, w), bf16), VM((4, n, rows, w), bf16),
        ]


def sems(n):
    return [DMA((n,)), DMA((n,))]


def exact(a, b):
    return jnp.dot(a, b, preferred_element_type=f32, precision=lax.Precision.HIGHEST)


def split3(v):
    high = v.astype(bf16)
    rest = v - wide(high)
    mid = rest.astype(bf16)
    return high, mid, (rest - wide(mid)).astype(bf16)


def three_rows(v):
    high, mid, low = split3(v)
    row = lax.broadcasted_iota(jnp.int32, (8, v.shape[1]), 0)
    pieces = jnp.where(row == 0, wide(high), jnp.where(row == 1, wide(mid), jnp.where(row == 2, wide(low), 0.0)))
    return pieces.astype(bf16)


def to_row_form(columns, rows):
    return columns.T[:rows]


def to_column_form(rows):
    fill = jnp.zeros((128 - rows.shape[0], rows.shape[1]), f32)
    return jnp.concatenate([rows, fill], axis=0).T


def route_columns(routes):
    row = lax.broadcasted_iota(jnp.int32, (8, routes.shape[1]), 0)
    both = jnp.where(row == 0, routes[0:1, :], jnp.where(row == 1, routes[1:2, :], 0)).astype(f32)
    columns = to_column_form(both)
    return columns[:, 0:1], columns[:, 1:2]


FIRST = 8


def hot_lanes(routes):
    lane = lax.broadcasted_iota(jnp.int32, (routes.shape[1], 128), 1).astype(f32)
    return [(lane == r + FIRST).astype(f32) for r in route_columns(routes)]


def pick_matrix(routes, cap):
    tok = routes.shape[1]
    lane = lax.broadcasted_iota(jnp.int32, (tok, 128), 1).astype(f32)
    columns = route_columns(routes)
    hot = [(lane == r).astype(f32) for r in columns]
    row = lax.broadcasted_iota(jnp.int32, (tok, tok), 0)
    col = lax.broadcasted_iota(jnp.int32, (tok, tok), 1)
    earlier = (col < row).astype(f32).astype(bf16)
    before = nn(earlier, (hot[0] + hot[1]).astype(bf16))
    slot = lax.broadcasted_iota(jnp.int32, (tok, CTX * 128), 1).astype(f32)
    out = []
    for r, o in zip(columns, hot):
        place = jnp.sum(before * o, axis=1, keepdims=True)
        target = jnp.where(place < cap, r * 128 + place, -1.0)
        out.append((slot == target).astype(f32).astype(bf16))
    return out


def pair_positions(pos_ref, g, cap):
    a, b = wide(pos_ref[2 * g]), wide(pos_ref[2 * g + 1])
    none = jnp.zeros_like(a)
    lane = lax.broadcasted_iota(jnp.int32, (a.shape[0], 256), 1)
    a = jnp.concatenate([a, none], axis=1)
    b = pltpu.roll(jnp.concatenate([b, none], axis=1), cap, 1)
    return jnp.where(lane < cap, a, b)[0:1, : 2 * cap].astype(jnp.int32)


def front_body(
    norm_in, router_t, routes_att, routes_mlp, kv_w, tokens, cot, q_own, o_own, gu_own,
    pos_out, slots_g, info, rows_out, seq_out, full_out, lowered_out, pick_att_out, pick_mlp_out, q_oth, o_oth, gu_oth,
    toks, cots, rows_att, kv_seq, kv_full, lowered, pick_att, pick_mlp, slots_att, pos, local_sem, send, recv,
):
    at, net, local = Place(), Net(send, recv), Local(local_sem)
    tok, width = tokens.shape
    kv_part, w = kv_w.shape[1:]
    cap, part = slots_att.shape[1:]
    mine = pl.ds(pl.multiple_of(at.t * part, part), part)
    load_t = local.go(tokens, toks)
    load_c = local.go(cot.at[:, mine], cots)

    def kvw(z, y, p):
        return kv_full.at[lax.rem(z, 2) * CTX + (z // 2) * 4 + y, part_of(p, kv_part)]

    own = kvw(at.z, at.y, None)
    for h in range(w // HD):
        for j in range(2):
            own[:, (2 * h + j) * HD : (2 * h + j + 1) * HD] = kv_w[j, :, h * HD : (h + 1) * HD]
    greet(at.ctx_peers() + at.tp_near() + at.z_near())
    zring = Ring(net, lambda z, p: kvw(z, at.y, p), at.z, at.above, at.below)
    zring.hop1()
    yrings = []

    def y_stage(z):
        ring = Ring(net, lambda y, p: kvw(z, y, p), at.y, at.up, at.down)
        ring.hop1()
        yrings.append(ring)

    y_stage(at.z)
    load_t.wait()
    x = wide(toks[...])
    scale = lax.rsqrt(jnp.sum(x * x, axis=1, keepdims=True) / width + epsilon)
    lowered[...] = (x * scale * norm_in[...]).astype(bf16)
    zring.hop2()
    y_stage(zring.low)
    y_stage(zring.high)
    for i, r in enumerate(pick_matrix(routes_att[...], cap)):
        pick_att[i * tok : (i + 1) * tok, :] = r
    both = pick_att[:tok, :] + pick_att[tok:, :]
    slots = tn(both, lowered[:, mine]).astype(bf16)
    for e in range(CTX):
        slots_att[e] = slots[e * 128 : e * 128 + cap]
    d_att = Dispatch(net, at, slots_att, rows_att)
    d_att.start()
    zring.hop3()
    y_stage(zring.far)
    number = lax.broadcasted_iota(jnp.int32, (8, tok), 1)
    row = lax.broadcasted_iota(jnp.int32, (8, tok), 0)
    digits = jnp.where(row == 0, number // 16, jnp.where(row == 1, lax.rem(number, 16), 0)).astype(f32).astype(bf16)
    found = nn(digits, both)
    found = (found[0:1] * 16.0 + found[1:2]).astype(jnp.int32) + at.c * tok
    for e in range(CTX):
        pos[e] = jnp.broadcast_to(found[:, e * 128 : (e + 1) * 128], (8, 128))
    moves = []
    for j in range(1, CTX):
        e = lax.rem(at.c + j, CTX)
        moves.append(net.go(pos.at[e], pos_out.at[at.c], {"ctx": e}))
    pos_out[at.c] = pos[at.c]
    moves.append(net.go(q_own, q_oth, at.partner))
    moves.append(net.go(o_own, o_oth, at.partner))
    saves = [local.go(lowered, lowered_out), local.go(pick_att, pick_att_out)]
    for ring in yrings[:3]:
        ring.hop2()
    d_att.hop1()
    yrings[3].hop2()
    for i, r in enumerate(pick_matrix(routes_mlp[...], cap)):
        pick_mlp[i * tok : (i + 1) * tok, :] = r
    load_c.wait()
    slots = tn(pick_mlp[:tok, :] + pick_mlp[tok:, :], cots[...]).astype(bf16)
    for e in range(CTX):
        slots_g[e] = slots[e * 128 : e * 128 + cap]
    saves.append(local.go(pick_mlp, pick_mlp_out))
    for ring in yrings:
        ring.hop3()
    weights = kv_full[...].reshape(-1, 2 * w)
    kv_seq[at.c] = nn(lowered[...], weights).astype(bf16)
    over = net.go(kv_seq.at[at.c], kv_seq.at[at.c], at.across)

    def seq_ring(zh):
        return Ring(net, lambda y, p: kv_seq.at[zh * 4 + y, part_of(p, tok)], at.y, at.up, at.down)

    near, far = seq_ring(at.zh), seq_ring(1 - at.zh)
    near.hop1()
    rows = gu_oth.shape[1]
    moves.append(net.go(gu_own.at[:, pl.ds(0, rows)], gu_oth, at.partner))
    saves.append(local.go(kv_full, full_out))
    d_att.hop2()
    logits = sum(nt(r, lowered[...]) for r in split3(router_t[...]))
    columns = to_column_form(jnp.concatenate([jnp.zeros_like(logits), logits], axis=0))
    hot = hot_lanes(routes_att[...])
    low = [jnp.sum(o * columns, axis=1, keepdims=True) for o in hot]
    lane = lax.broadcasted_iota(jnp.int32, (tok, 128), 1)
    g0 = 1.0 / (1.0 + jnp.exp(low[1] - low[0]))
    g1 = 1.0 / (1.0 + jnp.exp(low[0] - low[1]))
    info[...] = jnp.where(
        lane == 0, scale, jnp.where(lane == 1, g0, jnp.where(lane == 2, g1, columns / scale))
    )
    d_att.hop3()
    over.wait_recv()
    far.hop1()
    d_att.finish()
    saves.append(local.go(rows_att, rows_out))
    near.hop2()
    near.hop3()
    far.hop2()
    far.hop3()
    saves.append(local.go(kv_seq, seq_out))
    for m in moves:
        m.wait_recv()
    for d in saves:
        d.wait()
    net.drain()


def front(norm_in, router_t, routes_att, routes_mlp, kv_w, tokens, cot, q_own, o_own, gu_own, cap, chunk, cid):
    tok, width = tokens.shape
    part = width // TP
    _, kv_part, w = kv_w.shape
    slots = sds((CTX, cap, part), bf16)
    large = [(CTX * cap, width), (CTX, tok, 2 * w), (FSDP * CTX, kv_part, 2 * w), (tok, width)]
    large += [(2 * tok, CTX * 128)] * 2
    out = [sds((CTX, 8, 128), jnp.int32), slots, sds((tok, 128), f32)]
    out += [sds(z, bf16) for z in large]
    out += [sds(q_own.shape, bf16), sds(o_own.shape, bf16), sds((2, chunk, gu_own.shape[2]), bf16)]
    return pl.pallas_call(
        front_body,
        out_shape=tuple(out),
        in_specs=vmem(5) + anywhere(5),
        out_specs=tuple(vmem(3) + anywhere(9)),
        scratch_shapes=[VM((tok, width), bf16), VM((tok, part), bf16)] + [VM(z, bf16) for z in large]
        + [VM((CTX, cap, part), bf16), VM((CTX, 8, 128), jnp.int32), DMA((8,))]
        + sems(Dispatch.COPIES + 64),
        compiler_params=params(cid),
        cost_estimate=cost(70),
    )(norm_in, router_t, routes_att, routes_mlp, kv_w, tokens, cot, q_own, o_own, gu_own)


def assemble(own, other, full, axis, f, local):
    size = own.shape[axis]
    out = []
    for src, place in ((own, f), (other, 1 - f)):
        span = pl.ds(pl.multiple_of(place * size, size), size)
        out.append(local.go(src, full.at[span] if axis == 0 else full.at[:, span]))
    return out


def attend_body(
    cap, tok, first,
    pos_ref, slots_g, rows_any, kv_any, q_own, q_oth, o_own, o_oth, gu_own,
    q_ref, att_ref, lse_ref, home, g_out, gu_oth,
    rows_ref, kv_ref, rows_g, p_ref, wq, wo, vt_ref, b_sib, b_a, b_b, b_l, b_r, b_f, total_ref, local_sem, send, recv,
):
    at, net, local = Place(), Net(send, recv), Local(local_sem)
    heads = q_ref.shape[1] // HD
    width = heads * HD
    scale = HD ** (-0.5)
    total = q_ref.shape[0]
    load_q = assemble(q_own, q_oth, wq, 0, at.f, local) + [local.go(rows_any, rows_ref)]
    load_kv = local.go(kv_any, kv_ref)
    load_o = assemble(o_own, o_oth, wo, 1, at.f, local)
    greet(at.ctx_peers() + at.tp_near() + [at.partner])
    d_g = Dispatch(net, at, slots_g, rows_g)
    d_g.start()
    chunk = gu_oth.shape[1]
    move = net.go(gu_own.at[:, pl.ds(first, chunk)], gu_oth, at.partner)
    for d in load_q:
        d.wait()
    q_ref[...] = nn(rows_ref[...], wq[...]).astype(bf16)
    load_kv.wait()
    for h in range(heads):
        vt_ref[h] = kv_ref[:, (2 * h + 1) * HD : (2 * h + 2) * HD].T
    for d in load_o:
        d.wait()
    saves = []
    col = Collect(net, at, p_ref, home, b_sib, b_a, b_b, b_l, b_r, b_f, home_net="late", total=total_ref)
    rows_at, keys_at = 2 * cap, 2 * tok
    d_g.hop1()
    pair = lambda g: [2 * g, 2 * g + 1]
    for step, g in enumerate(reversed(range(total // rows_at))):
        lo = g * rows_at
        extent = (g + 1) * keys_at
        at_key = extent - keys_at
        pos = pair_positions(pos_ref, g, cap)
        for h in range(heads):
            cols = slice(h * HD, (h + 1) * HD)
            s = nt(kv_ref[:extent, 2 * h * HD : (2 * h + 1) * HD], q_ref[lo : lo + rows_at, cols]) * scale
            ids = lax.broadcasted_iota(jnp.int32, (keys_at, rows_at), 0) + at_key
            last = jnp.where(ids <= pos, s[at_key:], masked_score)
            highest = jnp.max(last, axis=0, keepdims=True)
            if g:
                highest = jnp.maximum(highest, jnp.max(s[:at_key], axis=0, keepdims=True))
            e_last = jnp.exp(last - highest)
            sums = jnp.sum(e_last, axis=0, keepdims=True)
            mixed = nn(vt_ref[h, :, at_key:extent], e_last.astype(bf16))
            if g:
                e = jnp.exp(s[:at_key] - highest)
                sums = sums + jnp.sum(e, axis=0, keepdims=True)
                mixed = mixed + nn(vt_ref[h, :, :at_key], e.astype(bf16))
            att_ref[lo : lo + rows_at, cols] = (mixed / sums).T.astype(bf16)
            lse_ref[h : h + 1, lo : lo + rows_at] = highest + jnp.log(sums)
        out = nn(att_ref[lo : lo + rows_at, :], wo[...]).astype(bf16)
        for i in range(TP):
            for b in range(2):
                p_ref[i % 2, i // 2, 2 * g + b] = out[b * cap : (b + 1) * cap, i * width : (i + 1) * width]
        col.start(pair(g))
        if step == 0:
            d_g.hop2()
        if step >= 1:
            col.hop1(pair(g + 1))
        if step == 2:
            d_g.hop3()
        if step >= 2:
            col.hop2(pair(g + 2))
        if step >= 3:
            col.hop3(pair(g + 3))
    col.hop1(pair(0))
    col.hop2(pair(1))
    col.hop3(pair(2))
    col.hop2(pair(0))
    col.hop3(pair(1))
    d_g.finish()
    saves.append(local.go(rows_g, g_out))
    col.hop3(pair(0))
    col.all_home()
    move.wait_recv()
    for d in saves:
        d.wait()
    col.finish()
    net.drain()


def attend(pos, slots_g, rows, kv, q_own, q_oth, o_own, o_oth, gu_own, tok, cap, first, chunk, cid):
    heads = q_own.shape[1] // HD
    slots, width = rows.shape
    w = heads * HD
    p_shape = (2, 4, slots // cap, cap, width // TP)
    return pl.pallas_call(
        partial(attend_body, cap, tok, first),
        out_shape=(
            sds((slots, w), bf16), sds((slots, w), bf16), sds((heads, slots), f32),
            sds(slots_g.shape, bf16), sds((slots, width), bf16), sds((2, chunk, gu_own.shape[2]), bf16),
        ),
        in_specs=vmem(2) + anywhere(7),
        out_specs=tuple(vmem(4) + anywhere(2)),
        scratch_shapes=[
            VM((slots, width), bf16), VM(kv.shape, bf16), VM((slots, width), bf16), VM(p_shape, bf16),
            VM((width, w), bf16), VM((w, width), bf16), VM((heads, HD, kv.shape[0]), bf16),
        ]
        + Collect.scratch(*slots_g.shape) + [VM(slots_g.shape, bf16), DMA((16,))]
        + sems(Dispatch.COPIES + Collect.COPIES + 1),
        compiler_params=params(cid),
        cost_estimate=cost(25),
    )(pos, slots_g, rows, kv, q_own, q_oth, o_own, o_oth, gu_own)


def mid_body(
    plan,
    ret_att, info, routes, norm_mid_full, router_full, pick_att_any, pick_mlp_any, tokens, cot, rows_g, gu_own, gu_f, gu_a,
    down_own,
    att_picked, hidden, gates_out, grad_hidden, norm_grad, router_grad,
    proj_out, p1_out, gu_sent_out, dd_sent_out, gu_grad, dd_grad, dd_got,
    pick_att, pick_mlp, grad_proj, p1, gu_sent, dd_sent,
    ret, b1_sib, b1_a, b1_b, b1_l, b1_r, fbuf,
    x_slots, X, G, W, D, gun, U, GG, GU, trans, p2, lm, small_out, small_in, small2_out, small2_in,
    sums_ref, gs_out, gs_in, sgm, sg_out, sg_in, sg_tot, sg_home, stage, toks, cots, mid_total, local_sem, stage_sem, send, recv,
):
    at, net = Place(), Net(send, recv)
    tok, part = lm.shape
    ff = down_own.shape[0]
    half = down_own.shape[1]
    cap = x_slots.shape[1]
    pad = W.shape[1] - ff
    n_f, n_a = gu_f.shape[1], gu_a.shape[1]
    mine = pl.ds(pl.multiple_of(at.f * half, half), half)
    other = pl.ds(pl.multiple_of((1 - at.f) * half, half), half)
    near = tp_peers(at)
    ret[...] = jnp.zeros_like(ret)
    for e in range(CTX):
        ret[0, e, : ret_att.shape[1], :] = ret_att[e]
    local = Local(local_sem)
    load = local.go
    load_a, load_m = load(pick_att_any, pick_att), load(pick_mlp_any, pick_mlp)
    here = pl.ds(pl.multiple_of(at.t * part, part), part)
    load_s = [load(tokens.at[:, here], toks), load(cot.at[:, here], cots)]
    load_g = load(rows_g, G)
    load_d = load(down_own, D.at[pl.ds(0, ff), mine])
    load_w = [
        load(gu_own, W.at[:, pl.ds(0, ff), mine]),
        load(gu_f, W.at[:, pl.ds(0, n_f), other]),
        load(gu_a, W.at[:, pl.ds(n_f, n_a), other]),
    ]
    greet(at.ctx_peers() + near + [at.partner])

    def down_piece(lo, hi):
        s = pl.ds(lo, hi - lo)
        return net.go(down_own.at[s], D.at[s, mine], at.partner)

    d_cut = plan["down"]
    down_moves = [down_piece(0, d_cut[0])]
    W[:, ff:, :] = jnp.zeros_like(W[:, ff:, :])
    D[ff:, :] = jnp.zeros_like(D[ff:, :])
    lane = lax.broadcasted_iota(jnp.int32, (tok, 128), 1)
    hot = hot_lanes(routes[...])
    ga = [info[:, k : k + 1] for k in (1, 2)]
    norm = norm_mid_full[0:1, here]
    router_t = router_full[:, here]
    router = jnp.concatenate([jnp.zeros((FIRST, part), f32), router_t, jnp.zeros((128 - FIRST - CTX, part), f32)]).T
    for d in load_s + [load_a, load_m]:
        d.wait()
    picked = nn(pick_att[...], ret[0].reshape(-1, part))
    att_picked[...] = picked.astype(bf16)
    h = wide(toks[...]) + ga[0] * picked[:tok] + ga[1] * picked[tok:]
    hidden[...] = h
    raw = exact(h * norm, router)
    sums = jnp.where(lane == 0, jnp.sum(h * h, axis=1, keepdims=True), raw)
    small_out[...] = to_row_form(sums, 16)
    moves = [net.go(small_out, small_in.at[j], p) for j, p in enumerate(near)]
    total = small_out[...]
    for j, m in enumerate(moves):
        m.wait_recv()
        total = total + small_in[j]
    sums = to_column_form(total)
    scale = lax.rsqrt(sums[:, 0:1] / (part * TP) + epsilon)
    low = [jnp.sum(o * sums, axis=1, keepdims=True) * scale for o in hot]
    g0 = 1.0 / (1.0 + jnp.exp(low[1] - low[0]))
    g1 = 1.0 / (1.0 + jnp.exp(low[0] - low[1]))
    gates = jnp.where(lane == 0, g0, jnp.where(lane == 1, g1, jnp.where(lane == 2, scale, 0.0)))
    sums_ref[...] = sums
    gates_out[...] = gates
    lm[...] = (hidden[...] * scale * norm).astype(bf16)
    slots = tn(pick_mlp[:tok, :] + pick_mlp[tok:, :], lm[...]).astype(bf16)
    for e in range(CTX):
        x_slots[e] = slots[e * 128 : e * 128 + cap]
    d1 = Dispatch(net, at, x_slots, X)
    d1.start()
    rows2 = to_row_form(gates, 2)
    pair_row = jnp.concatenate([rows2[0:1], rows2[1:2]], axis=1)
    slot_gates = jnp.sum(nn(three_rows(pair_row), pick_mlp[...]), axis=0, keepdims=True)
    for e in range(CTX):
        gs_out[e] = jnp.broadcast_to(slot_gates[:, e * 128 : (e + 1) * 128], (8, 128))
    gs_moves = [net.go(gs_out.at[p["ctx"]], gs_in.at[at.c], p) for p in at.ctx_peers()]
    gs_in[at.c] = gs_out[at.c]
    down_moves.append(down_piece(d_cut[1], ff))
    assert n_f + n_a == ff
    d1.hop1()
    for m in gs_moves:
        m.wait_recv()
    load_g.wait()
    for b in range(CTX):
        column = gs_in[b].T[:cap, 0:1]
        s = slice(b * cap, (b + 1) * cap)
        G[s, :] = (wide(G[s, :]) * column).astype(bf16)
    d1.hop2()
    load_d.wait()
    for m in down_moves:
        m.wait_recv()
    rows_at = 2 * cap
    groups = CTX // 2

    def group_rows(g):
        return pl.ds(pl.multiple_of(g * rows_at, rows_at), rows_at)

    @pl.loop(0, groups)
    def _(g):
        s = group_rows(g)
        gun[s, :] = nt(G[s, :], D[...])

    d1.hop3()
    d1.finish()
    for m in load_w:
        m.wait()
    sgm[...] = jnp.zeros_like(sgm)

    def put(p_ref, g, out):
        for i in range(TP):
            for b in range(2):
                p_ref[i % 2, i // 2, 2 * g + b] = out[b * cap : (b + 1) * cap, i * part : (i + 1) * part]

    net.drain()
    col2 = Collect(net, at, p2, ret.at[1], b1_sib, b1_a, b1_b, b1_l, b1_r, fbuf, home_net="late", total=mid_total)
    pair = lambda g: [2 * g, 2 * g + 1]
    for g in range(groups):
        s = group_rows(g)
        x = X[s, :]
        gate = nt(x, W[0])
        up = nt(x, W[1])
        sig = 1.0 / (1.0 + jnp.exp(-gate))
        silu = gate * sig
        units = (silu * up).astype(bf16)
        grad = gun[s, :]
        d_gate = (grad * up * (sig * (1.0 + gate * (1.0 - sig)))).astype(bf16)
        d_up = (grad * silu).astype(bf16)
        U[s, :] = units
        GG[s, :] = d_gate
        GU[s, :] = d_up
        column = jnp.sum(wide(units) * grad, axis=1, keepdims=True)
        for b in range(2):
            sgm[2 * g + b, :cap, :] = jnp.broadcast_to(column[b * cap : (b + 1) * cap], (cap, 128))
        put(p2, g, (nn(d_gate, W[0]) + nn(d_up, W[1])).astype(bf16))
        col2.start(pair(g))
        if g >= 1:
            col2.hop1(pair(g - 1))
        if g >= 2:
            col2.hop2(pair(g - 2))
        if g >= 3:
            col2.hop3(pair(g - 3))
    for b in range(CTX):
        sg_out[b] = sgm[b].T[:8]
    sg_moves = [net.go(sg_out, sg_in.at[j], p) for j, p in enumerate(near)]

    @pl.loop(0, groups)
    def _(g):
        s = group_rows(g)
        put(p1, g, nn(U[s, :], D[...]).astype(bf16))

    saves = [local.go(p1, p1_out)]
    col2.hop1(pair(3))
    col2.hop2(pair(2))
    col2.hop3(pair(1))
    v = sg_out[...]
    for j, m in enumerate(sg_moves):
        m.wait_recv()
        v = v + sg_in[j]
    sg_tot[...] = v
    sg_moves = [net.go(sg_tot.at[p["ctx"]], sg_home.at[at.c], p) for p in at.ctx_peers()]
    sg_home[at.c] = sg_tot[at.c]

    cols = stage.shape[2]
    steps = half // cols
    trans[...] = U[...].T

    @pl.loop(0, steps)
    def _(i):
        src = pl.ds(pl.multiple_of((1 - at.f) * half + i * cols, cols), cols)
        dd_sent[:, pl.ds(pl.multiple_of(i * cols, cols), cols)] = nn(trans[...], G[:, src])[:ff].astype(bf16)

    saves.append(local.go(dd_sent, dd_sent_out))
    cut = plan["dd"]
    feeder = Feeder(net, at.partner, [(dd_sent, dd_got, 0, 0, ff, ff // 11)])
    feeder.feed(cut[0])
    col2.hop2(pair(3))
    col2.hop3(pair(2))

    def own_part(matrix, dst, first):
        out = []
        for i in range(steps):
            slot = (first + i) % 2
            if first + i >= 2:
                stage_copies[first + i - 2].wait()
            src = pl.ds(pl.multiple_of(at.f * half + i * cols, cols), cols)
            stage[slot] = nn(trans[...], matrix[:, src])[:ff].astype(bf16)
            d = pltpu.make_async_copy(stage.at[slot], dst(pl.ds(i * cols, cols)), stage_sem.at[slot])
            d.start()
            stage_copies.append(d)

    stage_copies = []
    col2.hop3(pair(3))
    col2.all_home()
    feeder.feed(cut[1])
    own_part(G, lambda s: dd_grad.at[:, s], 0)
    for j, grads in enumerate((GG, GU)):
        trans[...] = grads[...].T

        @pl.loop(0, steps)
        def _(i):
            src = pl.ds(pl.multiple_of((1 - at.f) * half + i * cols, cols), cols)
            gu_sent[j, :, pl.ds(pl.multiple_of(i * cols, cols), cols)] = nn(trans[...], X[:, src])[:ff].astype(bf16)

        if j == 0:
            own_part(X, lambda s: gu_grad.at[0, :, s], steps)
    saves.append(local.go(gu_sent, gu_sent_out))
    col2.finish()

    lane = lax.broadcasted_iota(jnp.int32, (tok, 128), 1)
    hot = hot_lanes(routes[...])
    ga = [info[:, k : k + 1] for k in (1, 2)]
    norm = norm_mid_full[0:1, here]
    router_t = router_full[:, here]
    sums = sums_ref[...]
    gates = gates_out[...]
    scale = gates[:, 2:3]
    back = nn(pick_mlp[...], ret[1].reshape(-1, part))
    back = back[:tok] + back[tok:]
    h = hidden[...]
    inner = jnp.sum(back * norm * h, axis=1, keepdims=True)
    small2_out[...] = to_row_form(jnp.where(lane == 0, inner, 0.0), 8)
    moves = [net.go(small2_out, small2_in.at[j], p) for j, p in enumerate(near)]
    for m in sg_moves:
        m.wait_recv()
    row = jnp.concatenate([sg_home[e][0:1] for e in range(CTX)], axis=1)
    pairs = jnp.sum(nt(pick_mlp[...], three_rows(row)), axis=1, keepdims=True)
    sg = [pairs[:tok], pairs[tok:]]
    grad_logits = sum(
        o * (d - gates[:, k : k + 1] * (sg[0] + sg[1])) for k, (o, d) in enumerate(zip(hot, sg))
    )
    grad_low = back
    for e in range(CTX):
        grad_low = grad_low + grad_logits[:, FIRST + e : FIRST + e + 1] * router_t[e : e + 1, :]
    total = small2_out[...]
    for j, m in enumerate(moves):
        m.wait_recv()
        total = total + small2_in[j]
    inner = to_column_form(total)[:, 0:1] + jnp.sum(grad_logits * sums, axis=1, keepdims=True)
    gh = (
        wide(cots[...]) + scale * (grad_low * norm) - h * (scale * scale * scale) * (inner / (part * TP))
    )
    grad_hidden[...] = gh
    pair_rows = jnp.concatenate([(ga[0] * gh).astype(bf16), (ga[1] * gh).astype(bf16)], axis=0)
    slots = tn(pick_att[...], pair_rows).astype(bf16)
    for e in range(CTX):
        x_slots[e] = slots[e * 128 : e * 128 + cap]
    d2 = Dispatch(net, at, x_slots, grad_proj)
    d2.start()
    feeder.feed(cut[2])
    norm_grad[...] = jnp.broadcast_to(jnp.sum(grad_low * h * scale, axis=0, keepdims=True), norm_grad.shape)
    router_grad[...] = sum(tn(g, lm[...]) for g in split3(grad_logits))
    d2.hop1()
    d2.hop2()
    own_part(X, lambda s: gu_grad.at[1, :, s], 2 * steps)
    d2.hop3()
    d2.finish()
    saves.append(local.go(grad_proj, proj_out))
    for d in saves + stage_copies[-2:]:
        d.wait()
    feeder.finish()
    net.drain()


def mid(
    plan, ret_att, info, routes, norm_mid, router_t, pick_att, pick_mlp, tokens, cot, rows_g, gu_own, gu_f, gu_a, down_own, cid,
):
    tok, width = tokens.shape
    part = width // TP
    n, cap, _ = ret_att.shape
    p_shape = (2, 4, n, cap, part)
    slots, width = rows_g.shape
    ff, half = down_own.shape
    ffp = (ff + 255) // 256 * 256
    cols = 256
    bufs = Collect.scratch(n, cap, part)
    vm_out = (
        sds((2 * tok, part), bf16), sds((tok, part), f32), sds((tok, 128), f32), sds((tok, part), f32),
        sds((8, part), f32), sds((128, part), f32),
    )
    any_out = (
        sds((slots, width), bf16), sds(p_shape, bf16), sds((2, ff, half), bf16), sds((ff, half), bf16),
        sds((2, ff, half), bf16), sds((ff, half), bf16), sds((ff, half), bf16))
    return pl.pallas_call(
        partial(mid_body, plan),
        out_shape=vm_out + any_out,
        in_specs=vmem(5) + anywhere(9),
        out_specs=tuple(vmem(len(vm_out)) + anywhere(len(any_out))),
        scratch_shapes=[
            VM(pick_att.shape, bf16), VM(pick_att.shape, bf16), VM((slots, width), bf16),
            VM(p_shape, bf16), VM((2, ff, half), bf16), VM((ff, half), bf16), VM((2, n, 128, part), bf16),
        ]
        + bufs
        + [
            VM((n, cap, part), bf16), VM((slots, width), bf16), VM((slots, width), bf16),
            VM((2, ffp, width), bf16), VM((ffp, width), bf16), VM((slots, ffp), f32),
            VM((slots, ffp), bf16), VM((slots, ffp), bf16), VM((slots, ffp), bf16), VM((ffp, slots), bf16),
            VM(p_shape, bf16), VM((tok, part), bf16),
            VM((16, tok), f32), VM((TP - 1, 16, tok), f32), VM((8, tok), f32), VM((TP - 1, 8, tok), f32),
            VM((tok, 128), f32), VM((n, 8, 128), f32), VM((n, 8, 128), f32), VM((n, 128, 128), f32),
            VM((n, 8, 128), f32), VM((TP - 1, n, 8, 128), f32), VM((n, 8, 128), f32), VM((n, 8, 128), f32),
            VM((2, ff, cols), bf16), VM((tok, part), bf16), VM((tok, part), bf16), VM((n, cap, part), bf16), DMA((16,)), DMA((2,)),
        ]
        + sems(Collect.COPIES + 2 * Dispatch.COPIES + 80),
        compiler_params=params(cid),
        cost_estimate=cost(140),
    )(
        ret_att, info, routes, norm_mid, router_t, pick_att, pick_mlp, tokens, cot, rows_g, gu_own, gu_f, gu_a, down_own,
    )


def back_body(
    cap, tok, cuts,
    q_ref, pos_ref, att_ref, lse_ref, hidden, gates_mlp, att_picked, grad_hidden, info, routes, norm_in, router_t,
    norm_mid_grad, router_mlp_grad,
    proj_any, rows_any, kv_any, p1_any, q_own, q_oth, o_own, o_oth, full_any, lowered_any, pick_att_any, pick_mlp_any,
    tokens, gu_sent,
    kvw_out, result, input_grad, minor_out, o_grad, q_grad, gu_got, o_got, q_got,
    rows_ref, kv_ref, p_ref, wq, wo, do_ref, dq_ref, kt_ref, acc_ref, o_sent, q_sent, o_keep, q_keep,
    b_sib, b_a, b_b, b_l, b_r, b_f,
    seq_stage, seq_half, seq_whole, over_out, over_in, own_ref, kv_low,
    p2, c2_sib, c2_a, c2_b, c2_l, c2_r, c2_f,
    w_part, w_stage, w_half, w_whole, w_sum, wz_stage, wz_half, wz_whole,
    ret, mlp_ret, mlp_total, kv_back, x_res, x_in, small_out, small_in, minor, minor_in, minor_sum, rgrad, toks, lowered,
    credit, local_sem, send, recv,
):
    at, net, first_net, local = Place(), Net(send, recv, Collect.COPIES), Net(send, recv), Local(local_sem)
    heads = q_ref.shape[1] // HD
    width = heads * HD
    full_width = width * TP
    w = 2 * width
    part = width
    kv_part = full_width // (FSDP * CTX)
    scale = HD ** (-0.5)
    total = q_ref.shape[0]
    half = o_own.shape[1]
    mine = pl.ds(pl.multiple_of(at.t * part, part), part)
    load_o = assemble(o_own, o_oth, wo, 1, at.f, local) + [local.go(proj_any, rows_ref)]
    load_p = local.go(p1_any, p_ref)
    load_kv = local.go(kv_any, kv_ref)
    load_q = assemble(q_own, q_oth, wq, 0, at.f, local)
    load_t = [local.go(tokens, toks), local.go(lowered_any, lowered)]
    ret[...] = jnp.zeros_like(ret)
    mlp_ret[...] = jnp.zeros_like(mlp_ret)
    acc_ref[...] = jnp.zeros_like(acc_ref)
    near_tp = tp_peers(at)
    far_all = all_peers(at)
    greet(far_all + near_tp)

    gu_rows = gu_got.shape[1]
    unit = gu_rows // 22
    feeder = Feeder(net, at.partner, [
        (gu_sent, gu_got, 1, 0, unit * 8, unit), (o_sent, o_got, 0, 0, o_sent.shape[0], o_sent.shape[0] // 4),
        (gu_sent, gu_got.at[:, pl.ds(unit * 8, unit * 14)], 1, unit * 8, unit * 14, unit),
        (q_sent, q_got, 0, 0, q_sent.shape[0], q_sent.shape[0] // 4),
    ])
    feeder.feed(cuts[0])
    load_p.wait()
    col1 = Collect(first_net, at, p_ref, mlp_ret, b_sib, b_a, b_b, b_l, b_r, b_f, home_net=net, total=mlp_total)
    col1.start()
    for d in load_o:
        d.wait()
    do_ref[...] = nt(rows_ref[...], wo[...]).astype(bf16)
    col1.hop1()

    step_cols = 256
    steps = half // step_cols
    att_t = att_ref[...].T
    for i in range(steps):
        here = slice(i * step_cols, (i + 1) * step_cols)
        own_cols = pl.ds(pl.multiple_of(at.f * half + i * step_cols, step_cols), step_cols)
        other_cols = pl.ds(pl.multiple_of((1 - at.f) * half + i * step_cols, step_cols), step_cols)
        o_sent[:, here] = nn(att_t, rows_ref[:, other_cols]).astype(bf16)
        o_keep[:, here] = nn(att_t, rows_ref[:, own_cols])
    feeder.feed(cuts[1])
    saves = [local.go(o_keep, o_grad)]
    load_rows = local.go(rows_any, rows_ref)
    load_kv.wait()
    for h in range(heads):
        kt_ref[h] = kv_ref[:, 2 * h * HD : (2 * h + 1) * HD].T
    rows_at, keys_at = 2 * cap, 2 * tok
    key_scale = jnp.where(lax.broadcasted_iota(jnp.int32, (1, 2 * HD), 1) < HD, scale, 1.0)

    def seq_sum(h, zh):
        i = 2 * h + zh
        span = slice(2 * h * HD, 2 * (h + 1) * HD)
        lands = {"a": seq_half.at[i, 0], "b": seq_half.at[i, 1], "l": seq_whole.at[i, 0], "r": seq_whole.at[i, 1]}

        def own(y, p):
            size = tok if p is None else tok // 2
            lo = zh * 4 * tok + y * tok + (0 if p is None else p * (tok // 2))
            return acc_ref[pl.ds(pl.multiple_of(lo, 64), size), span] * key_scale

        return RingSum(
            net, own, lambda y, p: seq_stage.at[i, y, part_of(p, tok)], lambda name: lands[name],
            at.y, at.up, at.down,
        )

    seqs = [[seq_sum(h, zh) for zh in range(2)] for h in range(heads)]
    first_half = at.zh == 0
    overs = [None] * heads

    def seq_done(h, zh):
        span = slice(2 * h * HD, 2 * (h + 1) * HD)
        total_here = seqs[h][zh].hop3()
        if zh == 1:
            own_ref[:, span] = total_here
            return
        high = own_ref[:, span]
        over_out[h] = jnp.where(first_half, high, total_here).astype(bf16)
        own_ref[:, span] = jnp.where(first_half, total_here, high)
        overs[h] = net.go(over_out.at[h], over_in.at[h], at.across)

    for h in range(heads):
        cols = slice(h * HD, (h + 1) * HD)
        kcols = slice(2 * h * HD, (2 * h + 1) * HD)
        vcols = slice((2 * h + 1) * HD, (2 * h + 2) * HD)
        for g in reversed(range(total // rows_at)):
            lo = g * rows_at
            rows = slice(lo, lo + rows_at)
            extent = (g + 1) * keys_at
            at_key = extent - keys_at
            pos = pair_positions(pos_ref, g, cap)
            q = q_ref[rows, cols]
            do = do_ref[rows, cols]
            s = nt(kv_ref[:extent, kcols], q) * scale
            lse = lse_ref[h : h + 1, rows]
            ids = lax.broadcasted_iota(jnp.int32, (keys_at, rows_at), 0) + at_key
            last = jnp.where(ids <= pos, s[at_key:], masked_score)
            s = jnp.concatenate([s[:at_key], last], axis=0) if g else last
            soft = jnp.exp(s - lse)
            dp = nt(kv_ref[:extent, vcols], do)
            inner = jnp.sum(soft * dp, axis=0, keepdims=True)
            ds = (soft * (dp - inner)).astype(bf16)
            acc_ref[:extent, vcols] += nn(soft.astype(bf16), do)
            acc_ref[:extent, kcols] += nn(ds, q)
            dq_ref[rows, cols] = (nn(kt_ref[h, :, :extent], ds) * scale).T.astype(bf16)
            if h == 0 and g == 3:
                col1.hop2()
            if g == 2:
                seqs[h][1].hop1()
            if h == 0 and g == 2:
                col1.hop3()
                for axes in at.tp_near():
                    pl.semaphore_signal(credit, inc=1, device_id=axes, device_id_type=MESH)
            if g == 1:
                seqs[h][1].hop2()
            if g == 0:
                seqs[h][0].hop1()
            if h == 1 and g == 3:
                seq_done(0, 1)
                seqs[0][0].hop2()
            if h == 1 and g == 1:
                seq_done(0, 0)
                feeder.feed(cuts[2])
    load_full = local.go(full_any, kv_ref.at[pl.ds(0, full_width)])
    for d in load_q:
        d.wait()
    first_net.drain()
    for g in range(total // rows_at):
        rows = slice(g * rows_at, (g + 1) * rows_at)
        out = nt(dq_ref[rows, :], wq[...]).astype(bf16)
        for i in range(TP):
            for b in range(2):
                p_ref[i % 2, i // 2, 2 * g + b] = out[b * cap : (b + 1) * cap, i * width : (i + 1) * width]
    pl.semaphore_wait(credit, 3)
    col = Collect(net, at, p_ref, ret, b_sib, b_a, b_b, b_l, b_r, b_f)
    col.start()
    seq_done(1, 1)
    seqs[1][0].hop2()
    col.hop1()
    load_rows.wait()
    low_half = slice(0, 2 * HD)
    overs[0].wait_recv()
    kv_low[:, low_half] = (own_ref[:, low_half] + wide(over_in[0])).astype(bf16)
    seq_done(1, 0)
    feeder.feed(cuts[3])

    def index(z, y):
        return lax.rem(z, 2) * CTX + (z // 2) * 4 + y

    order = [lax.rem(at.z + i, 4) for i in (2, 1, 3, 0)]

    def weight_rings(h):
        span = slice(2 * h * HD, 2 * (h + 1) * HD)
        low = kv_low[:, span]
        for i in range(4):
            cols = full_width // 4
            block = tn(lowered[:, i * cols : (i + 1) * cols], low).astype(bf16)
            per = cols // kv_part
            w_part[h, i * per : (i + 1) * per] = block.reshape(per, kv_part, 2 * HD)
        out = []
        for i, z in enumerate(order):
            lands = {
                "a": w_half.at[h, i, 0], "b": w_half.at[h, i, 1], "l": w_whole.at[h, i, 0], "r": w_whole.at[h, i, 1]
            }
            out.append(RingSum(
                net,
                lambda y, p, z=z: wide(w_part[h, index(z, y), part_of(p, kv_part)]),
                lambda y, p, i=i: w_stage.at[h, i, y, part_of(p, kv_part)],
                lambda name, lands=lands: lands[name],
                at.y, at.up, at.down,
            ))
        for ring in out:
            ring.hop1()
        return out

    for d in load_t:
        d.wait()
    wrings = [weight_rings(0)]
    col.hop2()
    for i in range(steps):
        here = slice(i * step_cols, (i + 1) * step_cols)
        other_cols = pl.ds(pl.multiple_of((1 - at.f) * half + i * step_cols, step_cols), step_cols)
        q_sent[here, :] = tn(rows_ref[:, other_cols], dq_ref[...]).astype(bf16)
    load_full.wait()
    for ring in wrings[0]:
        ring.hop2()
    high_half = slice(2 * HD, 4 * HD)
    overs[1].wait_recv()
    kv_low[:, high_half] = (own_ref[:, high_half] + wide(over_in[1])).astype(bf16)
    back_rows = nt(kv_low[...], kv_ref[:full_width, :])
    n2, rows2, w2 = p2.shape[2:]
    for i in range(TP):
        p2[i % 2, i // 2] = back_rows[:, i * w2 : (i + 1) * w2].astype(bf16).reshape(n2, rows2, w2)
    col2 = Collect(net, at, p2, kv_back, c2_sib, c2_a, c2_b, c2_l, c2_r, c2_f, exchange=False)
    col2.start()
    inner_kv = jnp.sum(back_rows * (wide(toks[...]) * norm_in[0:1, :]), axis=1, keepdims=True)
    wrings.append(weight_rings(1))
    col.hop3()
    feeder.feed(cuts[4])
    col2.hop1()
    for i in range(steps):
        here = slice(i * step_cols, (i + 1) * step_cols)
        own_cols = pl.ds(pl.multiple_of(at.f * half + i * step_cols, step_cols), step_cols)
        q_keep[here, :] = tn(rows_ref[:, own_cols], dq_ref[...])
    saves.append(local.go(q_keep, q_grad))
    picks = full_width // 2
    load_picks = [
        local.go(pick_att_any, rows_ref.at[:, pl.ds(0, picks)]),
        local.go(pick_mlp_any, rows_ref.at[:, pl.ds(picks, picks)]),
    ]
    for ring in wrings[1]:
        ring.hop2()
    for d in load_picks:
        d.wait()
    col.finish()
    col2.hop2()

    inputs = wide(toks[:, mine])
    norm = norm_in[0:1, mine]
    gh = grad_hidden[...]
    grad_low = nn(rows_ref[:, :picks], ret[...].reshape(-1, part))
    grad_low = grad_low[:tok] + grad_low[tok:]
    lane = lax.broadcasted_iota(jnp.int32, (tok, 128), 1)
    facts = info[...]
    d0 = jnp.sum(wide(att_picked[:tok, :]) * gh, axis=1, keepdims=True)
    d1 = jnp.sum(wide(att_picked[tok:, :]) * gh, axis=1, keepdims=True)
    inner = jnp.sum(grad_low * norm * inputs, axis=1, keepdims=True) + inner_kv
    sums = jnp.where(lane == 0, d0, jnp.where(lane == 1, d1, jnp.where(lane == 2, inner, 0.0)))
    small_out[...] = to_row_form(sums, 8)
    smalls = [net.go(small_out, small_in.at[j], p) for j, p in enumerate(near_tp)]
    for h in range(heads):
        for z, ring in zip(order, wrings[h]):
            w_sum[z, :, 2 * h * HD : 2 * (h + 1) * HD] = ring.hop3()

    col1.finish()
    picked = nn(rows_ref[:, picks:], mlp_ret[...].reshape(-1, part))
    gates = gates_mlp[...]
    value = hidden[...] + gates[:, 0:1] * picked[:tok] + gates[:, 1:2] * picked[tok:]
    x_res[...] = value.astype(bf16).reshape(x_res.shape)
    d_res = Dispatch(net, at, x_res, result, exchange=False)
    lands = {"a": wz_half.at[0], "b": wz_half.at[1], "l": wz_whole.at[0], "r": wz_whole.at[1]}
    zsum = RingSum(
        net,
        lambda z, p: w_sum[z, part_of(p, kv_part)],
        lambda z, p: wz_stage.at[z, part_of(p, kv_part)],
        lambda name: lands[name],
        at.z, at.above, at.below,
    )
    zsum.hop1()
    col2.hop3()
    grad_low = grad_low + wide(kv_back[...].reshape(tok, part))
    total_row = small_out[...]
    for j, m in enumerate(smalls):
        m.wait_recv()
        total_row = total_row + small_in[j]
    sums = to_column_form(total_row)
    row_scale, g0, g1 = facts[:, 0:1], facts[:, 1:2], facts[:, 2:3]
    inner = g0 * sums[:, 0:1] + g1 * sums[:, 1:2]
    hot = hot_lanes(routes[...])
    grad_logits = hot[0] * (g0 * (sums[:, 0:1] - inner)) + hot[1] * (g1 * (sums[:, 1:2] - inner))
    for e in range(CTX):
        grad_low = grad_low + grad_logits[:, FIRST + e : FIRST + e + 1] * router_t[e : e + 1, mine]
    inner = sums[:, 2:3] + jnp.sum(grad_logits * facts, axis=1, keepdims=True)
    cubed = row_scale * row_scale * row_scale
    grad = gh + row_scale * (grad_low * norm) - inputs * cubed * (inner / full_width)
    x_in[...] = grad.astype(bf16).reshape(x_in.shape)
    d_in = Dispatch(net, at, x_in, input_grad, exchange=False)
    d_in.start()
    d_in.hop1()
    d_res.start()
    d_res.hop1()
    rgrad[...] = sum(tn(g, lowered[:, mine]) for g in split3(grad_logits))
    norm_grad = jnp.sum(grad_low * inputs * row_scale, axis=0, keepdims=True)
    row = lax.broadcasted_iota(jnp.int32, (8, part), 0)
    minor[0:8, :] = jnp.where(row == 0, norm_grad, jnp.where(row == 1, norm_mid_grad[0:1, :], 0.0))
    minor[8:16, :] = rgrad[FIRST : FIRST + CTX, :]
    minor[16:24, :] = router_mlp_grad[FIRST : FIRST + CTX, :]
    minors = [net.go(minor, minor_in.at[j], p) for j, p in enumerate(far_all)]
    zsum.hop2()
    feeder.feed(100)
    d_in.hop2()
    d_res.hop2()
    total_row = minor[...]
    for j, m in enumerate(minors):
        m.wait_recv()
        total_row = total_row + minor_in[j]
    minor_sum[...] = total_row
    minors = [net.go(minor_sum, minor_out.at[at.t], p) for p in near_tp]
    minor_out[at.t] = total_row
    d_in.hop3()
    d_res.hop3()
    kvw_out[...] = zsum.hop3()
    d_res.finish()
    d_in.finish()
    col2.finish()
    for m in minors:
        m.wait_recv()
    feeder.finish()
    for d in saves:
        d.wait()
    net.drain()


def back(small, large, cuts, tok, cap, cid):
    q = small[0]
    proj, rows, kv, p1, q_own, _, o_own, _, _, lowered, _, _, _, gu_sent = large
    slots, w = q.shape
    heads = w // HD
    width = w * TP
    kw = 2 * w
    part = width // (FSDP * CTX)
    _, _, n, _, _ = p1.shape
    n2 = 4
    rows2 = tok // n2
    ff, half = gu_sent.shape[1:]
    vm_out = (sds((part, kw), f32), sds((tok, width), bf16), sds((tok, width), bf16), sds((TP, 24, w), f32))
    any_out = (
        sds(o_own.shape, f32), sds(q_own.shape, f32), sds(gu_sent.shape, bf16),
        sds(o_own.shape, bf16), sds(q_own.shape, bf16),
    )
    out = pl.pallas_call(
        partial(back_body, cap, tok, cuts),
        out_shape=vm_out + any_out,
        in_specs=vmem(len(small)) + anywhere(len(large)),
        out_specs=tuple(vmem(len(vm_out)) + anywhere(len(any_out))),
        scratch_shapes=[
            VM((slots, width), bf16), VM(kv.shape, bf16), VM(p1.shape, bf16), VM((width, w), bf16), VM((w, width), bf16),
            VM((slots, w), bf16), VM((slots, w), bf16), VM((heads, HD, kv.shape[0]), bf16), VM(kv.shape, f32),
            VM(o_own.shape, bf16), VM(q_own.shape, bf16), VM(o_own.shape, f32), VM(q_own.shape, f32),
        ]
        + Collect.scratch(n, cap, w)
        + [
            VM((2 * heads, 4, tok, w), bf16), VM((2 * heads, 2, tok // 2, w), bf16), VM((2 * heads, 2, tok, w), bf16),
            VM((heads, tok, w), bf16), VM((heads, tok, w), bf16), VM((tok, kw), f32), VM((tok, kw), bf16),
        ]
        + [VM((2, 4, n2, rows2, w), bf16)] + Collect.scratch(n2, rows2, w)
        + [
            VM((heads, FSDP * CTX, part, w), bf16), VM((heads, 4, 4, part, w), bf16),
            VM((heads, 4, 2, part // 2, w), bf16), VM((heads, 4, 2, part, w), bf16), VM((4, part, kw), f32), VM((4, part, kw), bf16),
            VM((2, part // 2, kw), bf16), VM((2, part, kw), bf16),
            VM((n, 128, w), bf16), VM((n, 128, w), bf16), VM((n, cap, w), bf16), VM((n2, rows2, w), bf16),
            VM((n2, rows2, w), bf16), VM((n2, rows2, w), bf16), VM((8, tok), f32), VM((TP - 1, 8, tok), f32),
            VM((24, w), f32), VM((FSDP * CTX - 1, 24, w), f32), VM((24, w), f32), VM((128, w), f32),
            VM((tok, width), bf16), VM((tok, width), bf16),
            pltpu.SemaphoreType.REGULAR, DMA((20,)),
        ]
        + sems(Collect.COPIES * 3 + Dispatch.COPIES * 2 + 180),
        compiler_params=params(cid),
        cost_estimate=cost(120),
    )(*small, *large)
    kvw, result, input_grad, minor, o_grad, q_grad, gu_got, o_got, q_got = out
    return o_grad, q_grad, kvw, result, input_grad, minor, gu_got, o_got, q_got


def local(
    tokens, norm_in, norm_mid, router_att, router_mlp, kv_weight, query_weight, output_weight,
    gate_up_weight, down_weight, routes_att, routes_mlp, cotangent,
):
    f, c = lax.axis_index("fsdp"), lax.axis_index("ctx")
    count_rows, width = tokens.shape[1:]
    capacity = count_rows * 2 // CTX
    half = width // 2
    local_width = query_weight.shape[2]
    tokens, cotangent = tokens[0], cotangent[0]
    q_own, o_own, down_own = query_weight[0], output_weight[0], down_weight[0]
    gu_own = gate_up_weight[0].transpose(0, 2, 1)
    routes_att, routes_mlp = routes_att[0].T, routes_mlp[0].T
    norm_in, norm_mid = norm_in[None], norm_mid[None]
    router_att, router_mlp = router_att.T, router_mlp.T
    hidden_count = gu_own.shape[1]
    unit = hidden_count // 44
    gu_front = 19 * unit
    gu_attend = hidden_count - gu_front
    plan = {"down": (12 * unit, 12 * unit), "dd": (2, 3, 6)}
    pieces = (8, 4, 5, 3, 4)

    (
        positions, slots_g, info, rows_att, kv_seq, kv_full, lowered, pick_att, pick_mlp, q_oth, o_oth, gu_0,
    ) = front(
        norm_in, router_att, routes_att, routes_mlp, kv_weight, tokens, cotangent, q_own, o_own, gu_own,
        capacity, gu_front, 1,
    )
    kv_seq = kv_seq.reshape(-1, 2 * local_width)
    queries, attended, log_totals, ret_att, rows_g, gu_1 = attend(
        positions, slots_g, rows_att, kv_seq, q_own, q_oth, o_own, o_oth, gu_own, count_rows, capacity,
        gu_front, gu_attend, 2,
    )
    (
        att_picked, hidden, gates_mlp, grad_hidden, norm_mid_grad, router_mlp_grad, grad_proj, p_mlp, gu_sent, dd_sent,
        gu_grad, dd_grad, dd_got,
    ) = mid(
        plan, ret_att, info, routes_mlp, norm_mid, router_mlp, pick_att, pick_mlp, tokens, cotangent,
        rows_g, gu_own, gu_0, gu_1, down_own, 3,
    )
    o_grad, q_grad, kvw_grad, result, input_grad, minor, gu_got, o_got, q_got = back(
        (queries, positions, attended, log_totals, hidden, gates_mlp, att_picked, grad_hidden, info, routes_att,
         norm_in, router_att, norm_mid_grad, router_mlp_grad),
        (grad_proj, rows_att, kv_seq, p_mlp, q_own, q_oth, o_own, o_oth, kv_full.reshape(width, 2 * local_width),
         lowered, pick_att, pick_mlp, tokens, gu_sent),
        pieces, count_rows, capacity, 4,
    )
    me = f * CTX + c
    minor = lax.dynamic_index_in_dim(minor, me // 2, 0, keepdims=False)
    minor = lax.dynamic_slice_in_dim(minor, lax.rem(me, 2) * 128, 128, 1)
    kvw_grad = kvw_grad.reshape(-1, local_width // HD, 2, HD).transpose(2, 0, 1, 3).reshape(2, -1, local_width)
    gate_up_grad = gu_grad.astype(f32) + gu_got.astype(f32)
    return (
        result[None], input_grad.astype(f32)[None], minor[0], minor[1], minor[8:16].T, minor[16:24].T,
        kvw_grad,
        (q_grad + q_got.astype(f32))[None], (o_grad + o_got.astype(f32))[None],
        gate_up_grad.transpose(0, 2, 1)[None], (dd_grad.astype(f32) + dd_got.astype(f32))[None],
    )


def solution(mesh):
    placed = (
        P("fsdp", "ctx", None), P(), P(), P(), P(),
        P(None, ("fsdp", "ctx"), "tp"), P("ctx", "fsdp", "tp"), P("ctx", "tp", "fsdp"),
        P("ctx", None, "fsdp", "tp"), P("ctx", "tp", "fsdp"),
        P("fsdp", "ctx", None), P("fsdp", "ctx", None), P("fsdp", "ctx", None),
    )
    return jax.shard_map(
        local,
        mesh=mesh,
        in_specs=placed,
        out_specs=(
            P("fsdp", "ctx", None), P("fsdp", "ctx", None), P(("fsdp", "ctx")), P(("fsdp", "ctx")),
            P(("fsdp", "ctx"), None), P(("fsdp", "ctx"), None), P(None, ("fsdp", "ctx"), "tp"),
            P("ctx", "fsdp", "tp"), P("ctx", "tp", "fsdp"), P("ctx", None, "fsdp", "tp"), P("ctx", "tp", "fsdp"),
        ),
        check_vma=False,
    )
```

```python
from functools import partial

import jax
import jax.numpy as jnp
from jax import lax
from jax.experimental import pallas as pl
from jax.experimental.pallas import tpu as pltpu
from jax.sharding import PartitionSpec as P

MESH = pl.DeviceIdType.MESH
HD = 128
CTX = 8
TP = 8
FSDP = 2
VLIM = 61 * 1024 * 1024
epsilon = 1e-06
masked_score = -1e30
f32 = jnp.float32
bf16 = jnp.bfloat16
DMA = pltpu.SemaphoreType.DMA
VM = pltpu.VMEM


def vmem(n):
    return [pl.BlockSpec(memory_space=pltpu.VMEM)] * n


def anywhere(n):
    return [pl.BlockSpec(memory_space=pl.ANY)] * n


def params(cid=None):
    if cid is None:
        return pltpu.CompilerParams(vmem_limit_bytes=VLIM)
    return pltpu.CompilerParams(collective_id=cid, has_side_effects=True, vmem_limit_bytes=VLIM)


def cost(us):
    return pl.CostEstimate(flops=0, bytes_accessed=int(us * 3.2e6), transcendentals=0)


def sds(shape, dtype):
    return jax.ShapeDtypeStruct(shape, dtype)


def nt(a, b):
    return lax.dot_general(a, b, (((1,), (1,)), ((), ())), preferred_element_type=f32)


def tn(a, b):
    return lax.dot_general(a, b, (((0,), (0,)), ((), ())), preferred_element_type=f32)


def nn(a, b):
    return jnp.dot(a, b, preferred_element_type=f32)


def wide(v):
    return v.astype(f32)


class Place:
    def __init__(self):
        self.f, self.c, self.t = lax.axis_index("fsdp"), lax.axis_index("ctx"), lax.axis_index("tp")
        self.x, self.k = self.t // 2, lax.rem(self.t, 2)
        self.xl, self.xr, self.xo = (lax.rem(self.x + i, 4) for i in (3, 1, 2))
        self.right, self.left = {"tp": self.xr * 2 + self.k}, {"tp": self.xl * 2 + self.k}
        self.sib = {"tp": self.x * 2 + 1 - self.k}
        self.zh, self.y = self.c // 4, lax.rem(self.c, 4)
        self.z = self.zh * 2 + self.f
        self.up, self.down = ({"ctx": self.zh * 4 + lax.rem(self.y + i, 4)} for i in (1, 3))
        self.across = {"ctx": lax.rem(self.c + 4, CTX)}
        self.partner = {"fsdp": 1 - self.f}
        self.above, self.below = (self.at_z(lax.rem(self.z + i, 4)) for i in (1, 3))

    def at_z(self, z):
        return {"fsdp": lax.rem(z, 2), "ctx": (z // 2) * 4 + self.y}

    def ctx_peers(self):
        return [{"ctx": lax.rem(self.c + j, CTX)} for j in range(1, CTX)]

    def tp_near(self):
        return [self.right, self.left, self.sib]

    def z_near(self):
        return [self.above, self.below]


def greet(peers):
    barrier = pltpu.get_barrier_semaphore()
    for axes in peers:
        pl.semaphore_signal(barrier, inc=1, device_id=axes, device_id_type=MESH)
    pl.semaphore_wait(barrier, len(peers))


def all_peers(at):
    me = at.f * CTX + at.c
    out = []
    for j in range(1, FSDP * CTX):
        p = lax.rem(me + j, FSDP * CTX)
        out.append({"fsdp": p // CTX, "ctx": lax.rem(p, CTX)})
    return out


def tp_peers(at):
    return [{"tp": lax.rem(at.t + j, TP)} for j in range(1, TP)]


class Net:
    def __init__(self, send, recv, base=0):
        self.send, self.recv, self.used, self.open = send, recv, base, []

    def go(self, src, dst, axes):
        i = self.used
        self.used += 1
        d = pltpu.make_async_remote_copy(
            src_ref=src, dst_ref=dst, send_sem=self.send.at[i], recv_sem=self.recv.at[i],
            device_id=axes, device_id_type=MESH,
        )
        d.start()
        self.open.append(d)
        return d

    def drain(self):
        for d in self.open:
            d.wait_send()
        self.open = []


class Ring:
    def __init__(self, net, view, me, plus, minus):
        self.net, self.view, self.plus, self.minus = net, view, plus, minus
        self.me, self.low, self.high, self.far = me, lax.rem(me + 3, 4), lax.rem(me + 1, 4), lax.rem(me + 2, 4)

    def hop1(self, src=None):
        src = self.view(self.me, None) if src is None else src
        self.a = self.net.go(src, self.view(self.me, None), self.plus)
        self.b = self.net.go(src, self.view(self.me, None), self.minus)

    def hop2_low(self):
        self.a.wait_recv()
        self.a = self.net.go(self.view(self.low, 0), self.view(self.low, 0), self.plus)

    def hop2_high(self):
        self.b.wait_recv()
        self.b = self.net.go(self.view(self.high, 1), self.view(self.high, 1), self.minus)

    def hop2(self):
        self.hop2_low()
        self.hop2_high()

    def hop3(self):
        self.a.wait_recv()
        self.b.wait_recv()


class RingSum:
    def __init__(self, net, own, stage, land, me, plus, minus):
        self.net, self.own, self.stage, self.land, self.plus, self.minus = net, own, stage, land, plus, minus
        self.me, self.low, self.high, self.far = me, lax.rem(me + 3, 4), lax.rem(me + 1, 4), lax.rem(me + 2, 4)

    def put(self, position, part, value):
        r = self.stage(position, part)
        r[...] = value.astype(r.dtype)
        return r

    def hop1(self):
        self.a = self.net.go(self.put(self.far, 0, self.own(self.far, 0)), self.land("a"), self.plus)
        self.b = self.net.go(self.put(self.far, 1, self.own(self.far, 1)), self.land("b"), self.minus)

    def hop2(self):
        self.a.wait_recv()
        self.put(self.high, 0, self.own(self.high, 0) + wide(self.land("a")[...]))
        self.put(self.high, 1, self.own(self.high, 1))
        self.a = self.net.go(self.stage(self.high, None), self.land("l"), self.plus)
        self.b.wait_recv()
        self.put(self.low, 1, self.own(self.low, 1) + wide(self.land("b")[...]))
        self.put(self.low, 0, self.own(self.low, 0))
        self.b = self.net.go(self.stage(self.low, None), self.land("r"), self.minus)

    def hop3(self):
        self.a.wait_recv()
        self.b.wait_recv()
        return self.own(self.me, None) + wide(self.land("l")[...]) + wide(self.land("r")[...])


class Feeder:
    def __init__(self, net, partner, items):
        self.net, self.partner, self.moves, self.queue = net, partner, [], []
        for src, dst, axis, first, rows, unit in items:
            self.queue += [(src, dst, axis, first, lo, min(unit, rows - lo)) for lo in range(0, rows, unit)]

    def feed(self, count):
        for src, dst, axis, first, lo, size in self.queue[:count]:
            s, d = pl.ds(first + lo, size), pl.ds(lo, size)
            a, b = (src.at[s], dst.at[d]) if axis == 0 else (src.at[:, s], dst.at[:, d])
            self.moves.append(self.net.go(a, b, self.partner))
        self.queue = self.queue[count:]

    def finish(self):
        assert not self.queue
        for m in self.moves:
            m.wait_recv()


class Local:
    def __init__(self, sem):
        self.sem, self.used = sem, 0

    def go(self, src, dst):
        d = pltpu.make_async_copy(src, dst, self.sem.at[self.used])
        self.used += 1
        d.start()
        return d


def part_of(part, size):
    half = size // 2
    return pl.ds(0, size) if part is None else pl.ds(part * half, half)


class Dispatch:
    def __init__(self, net, at, x_ref, o_ref, exchange=True):
        self.net, self.at, self.x_ref, self.o_ref, self.exchange = net, at, x_ref, o_ref, exchange
        self.n, self.rows, self.w = x_ref.shape

    def view(self, block, tt, part=None):
        half = self.rows // 2
        lo, size = (0, self.rows) if part is None else (part * half, half)
        row = pl.multiple_of(block * self.rows + lo, 16)
        return self.o_ref.at[pl.ds(row, size), pl.ds(pl.multiple_of(tt * self.w, self.w), self.w)]

    def start(self):
        c, n = self.at.c, self.n
        if self.exchange:
            self.blocks = [lax.rem(c + n - j, n) for j in range(n)]
            self.moves = [None]
            for j in range(1, n):
                e = lax.rem(c + j, n)
                self.moves.append(self.net.go(self.x_ref.at[e], self.view(c, self.at.t), {"ctx": e}))
            self.view(c, self.at.t)[...] = self.x_ref[c]
        else:
            self.blocks, self.moves = list(range(n)), [None] * n
            for j in range(n):
                self.view(j, self.at.t)[...] = self.x_ref[j]

    def sibling(self, b, tt):
        return self.net.go(self.view(b, tt), self.view(b, tt), self.at.sib)

    def hop1(self):
        at = self.at
        self.rings, self.sibs = [], []
        for b, move in zip(self.blocks, self.moves):
            if move is not None:
                move.wait_recv()
            ring = Ring(self.net, lambda xx, part, b=b: self.view(b, xx * 2 + at.k, part), at.x, at.right, at.left)
            ring.hop1()
            self.rings.append(ring)
            self.sibs.append(self.sibling(b, at.t))

    def hop2(self):
        at = self.at
        for b, ring in zip(self.blocks, self.rings):
            ring.hop2_low()
            self.sibs.append(self.sibling(b, at.xl * 2 + at.k))
            ring.hop2_high()
            self.sibs.append(self.sibling(b, at.xr * 2 + at.k))

    def hop3(self):
        at = self.at
        for b, ring in zip(self.blocks, self.rings):
            ring.hop3()
            self.sibs.append(self.sibling(b, at.xo * 2 + at.k))

    def finish(self):
        for s in self.sibs:
            s.wait_recv()

    COPIES = 8 * 9 + 7


class Collect:
    def __init__(
        self, net, at, p_ref, o_ref, sibbuf, abuf, bbuf, lbuf, rbuf, fbuf, exchange=True, home_net=None, total=None
    ):
        self.net, self.at, self.p, self.o, self.exchange = net, at, p_ref, o_ref, exchange
        self.home_net = net if home_net in (None, "late") else home_net
        self.total = fbuf.at[at.x] if total is None else total
        self.sibbuf, self.fbuf = sibbuf, fbuf
        self.lands = {"a": abuf, "b": bbuf, "l": lbuf, "r": rbuf}
        _, _, self.n, self.rows, self.w = p_ref.shape
        n, c = self.n, at.c
        self.late = home_net == "late"
        self.blocks = [lax.rem(c + j, n) for j in range(1, n)] + [c] if exchange and not self.late else list(range(n))
        self.sibs, self.rings, self.moves = [None] * n, [None] * n, []

    def start(self, which=None):
        at = self.at
        for j in range(self.n) if which is None else which:
            b = self.blocks[j]
            self.sibs[j] = self.net.go(self.p.at[1 - at.k, :, b], self.sibbuf.at[:, b], at.sib)

    def own(self, b, xx, part):
        s = part_of(part, self.rows)
        return wide(self.p[self.at.k, xx, b, s]) + wide(self.sibbuf[xx, b, s])

    def hop1(self, which=None):
        at = self.at
        for j in range(self.n) if which is None else which:
            b = self.blocks[j]
            self.sibs[j].wait_recv()
            ring = RingSum(
                self.net,
                partial(self.own, b),
                lambda xx, part, b=b: self.fbuf.at[xx, b, part_of(part, self.rows)],
                lambda name, b=b: self.lands[name].at[b],
                at.x, at.right, at.left,
            )
            ring.hop1()
            self.rings[j] = ring

    def hop2(self, which=None):
        for j in range(self.n) if which is None else which:
            self.rings[j].hop2()

    def hop3(self, which=None):
        for j in range(self.n) if which is None else which:
            b = self.blocks[j]
            total = self.rings[j].hop3()
            if self.late:
                self.total[b] = total.astype(self.fbuf.dtype)
            elif self.exchange and j < self.n - 1:
                self.total[b] = total.astype(self.fbuf.dtype)
                self.to_home(b)
            else:
                self.o[b, pl.ds(0, self.rows)] = total.astype(self.o.dtype)

    def to_home(self, b):
        home = self.o.at[self.at.c, pl.ds(0, self.rows)]
        self.moves.append(self.home_net.go(self.total.at[b], home, {"ctx": b}))

    def all_home(self):
        c, n = self.at.c, self.n
        for j in range(1, n):
            self.to_home(lax.rem(c + j, n))
        self.o[c, pl.ds(0, self.rows)] = self.total[c]

    def finish(self):
        for m in self.moves:
            m.wait_recv()

    COPIES = 8 * 5 + 7

    @staticmethod
    def scratch(n, rows, w):
        return [
            VM((4, n, rows, w), bf16), VM((n, rows // 2, w), bf16), VM((n, rows // 2, w), bf16),
            VM((n, rows, w), bf16), VM((n, rows, w), bf16), VM((4, n, rows, w), bf16),
        ]


def sems(n):
    return [DMA((n,)), DMA((n,))]


def exact(a, b):
    return jnp.dot(a, b, preferred_element_type=f32, precision=lax.Precision.HIGHEST)


def split3(v):
    high = v.astype(bf16)
    rest = v - wide(high)
    mid = rest.astype(bf16)
    return high, mid, (rest - wide(mid)).astype(bf16)


def three_rows(v):
    high, mid, low = split3(v)
    row = lax.broadcasted_iota(jnp.int32, (8, v.shape[1]), 0)
    pieces = jnp.where(row == 0, wide(high), jnp.where(row == 1, wide(mid), jnp.where(row == 2, wide(low), 0.0)))
    return pieces.astype(bf16)


def to_row_form(columns, rows):
    return columns.T[:rows]


def to_column_form(rows):
    fill = jnp.zeros((128 - rows.shape[0], rows.shape[1]), f32)
    return jnp.concatenate([rows, fill], axis=0).T


def route_columns(routes):
    row = lax.broadcasted_iota(jnp.int32, (8, routes.shape[1]), 0)
    both = jnp.where(row == 0, routes[0:1, :], jnp.where(row == 1, routes[1:2, :], 0)).astype(f32)
    columns = to_column_form(both)
    return columns[:, 0:1], columns[:, 1:2]


FIRST = 8


def hot_lanes(routes):
    lane = lax.broadcasted_iota(jnp.int32, (routes.shape[1], 128), 1).astype(f32)
    return [(lane == r + FIRST).astype(f32) for r in route_columns(routes)]


def pick_matrix(routes, cap):
    tok = routes.shape[1]
    lane = lax.broadcasted_iota(jnp.int32, (tok, 128), 1).astype(f32)
    columns = route_columns(routes)
    hot = [(lane == r).astype(f32) for r in columns]
    row = lax.broadcasted_iota(jnp.int32, (tok, tok), 0)
    col = lax.broadcasted_iota(jnp.int32, (tok, tok), 1)
    earlier = (col < row).astype(f32).astype(bf16)
    before = nn(earlier, (hot[0] + hot[1]).astype(bf16))
    slot = lax.broadcasted_iota(jnp.int32, (tok, CTX * 128), 1).astype(f32)
    out = []
    for r, o in zip(columns, hot):
        place = jnp.sum(before * o, axis=1, keepdims=True)
        target = jnp.where(place < cap, r * 128 + place, -1.0)
        out.append((slot == target).astype(f32).astype(bf16))
    return out


def pair_positions(pos_ref, g, cap):
    a, b = wide(pos_ref[2 * g]), wide(pos_ref[2 * g + 1])
    none = jnp.zeros_like(a)
    lane = lax.broadcasted_iota(jnp.int32, (a.shape[0], 256), 1)
    a = jnp.concatenate([a, none], axis=1)
    b = pltpu.roll(jnp.concatenate([b, none], axis=1), cap, 1)
    return jnp.where(lane < cap, a, b)[0:1, : 2 * cap].astype(jnp.int32)


def assemble(own, other, full, axis, f, local):
    size = own.shape[axis]
    out = []
    for src, place in ((own, f), (other, 1 - f)):
        span = pl.ds(pl.multiple_of(place * size, size), size)
        out.append(local.go(src, full.at[span] if axis == 0 else full.at[:, span]))
    return out


def front_body(
    feeds, norm_in, router_t, routes_att, routes_mlp, kv_w, tokens, cot, q_own, o_own, gu_own,
    pos_out, info, q_ref, att_ref, lse_ref, home,
    rows_out, seq_out, full_out, lowered_out, pick_att_out, pick_mlp_out, g_out, q_oth, o_oth, gu_oth,
    toks, cots, rows_att, kv_seq, kv_full, lowered, pick_att, pick_mlp, slots_att, slots_g, pos,
    rows_g, p_ref, wq, wo, vt_ref, b_sib, b_a, b_b, b_l, b_r, b_f, total_ref, local_sem, send, recv,
):
    at, net, local = Place(), Net(send, recv), Local(local_sem)
    ff = gu_own.shape[1]
    feeder = Feeder(net, at.partner, [(gu_own, gu_oth, 1, 0, ff, ff // 44)])
    tok, width = tokens.shape
    kv_part, w = kv_w.shape[1:]
    cap, part = slots_att.shape[1:]
    mine = pl.ds(pl.multiple_of(at.t * part, part), part)
    load_t = local.go(tokens, toks)
    load_c = local.go(cot.at[:, mine], cots)

    def kvw(z, y, p):
        return kv_full.at[lax.rem(z, 2) * CTX + (z // 2) * 4 + y, part_of(p, kv_part)]

    own = kvw(at.z, at.y, None)
    for h in range(w // HD):
        for j in range(2):
            own[:, (2 * h + j) * HD : (2 * h + j + 1) * HD] = kv_w[j, :, h * HD : (h + 1) * HD]
    greet(at.ctx_peers() + at.tp_near() + at.z_near())
    zring = Ring(net, lambda z, p: kvw(z, at.y, p), at.z, at.above, at.below)
    zring.hop1()
    yrings = []

    def y_stage(z):
        ring = Ring(net, lambda y, p: kvw(z, y, p), at.y, at.up, at.down)
        ring.hop1()
        yrings.append(ring)

    y_stage(at.z)
    load_t.wait()
    x = wide(toks[...])
    scale = lax.rsqrt(jnp.sum(x * x, axis=1, keepdims=True) / width + epsilon)
    lowered[...] = (x * scale * norm_in[...]).astype(bf16)
    zring.hop2()
    y_stage(zring.low)
    y_stage(zring.high)
    for i, r in enumerate(pick_matrix(routes_att[...], cap)):
        pick_att[i * tok : (i + 1) * tok, :] = r
    both = pick_att[:tok, :] + pick_att[tok:, :]
    slots = tn(both, lowered[:, mine]).astype(bf16)
    for e in range(CTX):
        slots_att[e] = slots[e * 128 : e * 128 + cap]
    d_att = Dispatch(net, at, slots_att, rows_att)
    d_att.start()
    zring.hop3()
    y_stage(zring.far)
    number = lax.broadcasted_iota(jnp.int32, (8, tok), 1)
    row = lax.broadcasted_iota(jnp.int32, (8, tok), 0)
    digits = jnp.where(row == 0, number // 16, jnp.where(row == 1, lax.rem(number, 16), 0)).astype(f32).astype(bf16)
    found = nn(digits, both)
    found = (found[0:1] * 16.0 + found[1:2]).astype(jnp.int32) + at.c * tok
    for e in range(CTX):
        pos[e] = jnp.broadcast_to(found[:, e * 128 : (e + 1) * 128], (8, 128))
    moves = []
    for j in range(1, CTX):
        e = lax.rem(at.c + j, CTX)
        moves.append(net.go(pos.at[e], pos_out.at[at.c], {"ctx": e}))
    pos_out[at.c] = pos[at.c]
    q_move = net.go(q_own, q_oth, at.partner)
    o_move = net.go(o_own, o_oth, at.partner)
    saves = [local.go(lowered, lowered_out), local.go(pick_att, pick_att_out)]
    for ring in yrings[:3]:
        ring.hop2()
    d_att.hop1()
    yrings[3].hop2()
    for i, r in enumerate(pick_matrix(routes_mlp[...], cap)):
        pick_mlp[i * tok : (i + 1) * tok, :] = r
    load_c.wait()
    slots = tn(pick_mlp[:tok, :] + pick_mlp[tok:, :], cots[...]).astype(bf16)
    for e in range(CTX):
        slots_g[e] = slots[e * 128 : e * 128 + cap]
    saves.append(local.go(pick_mlp, pick_mlp_out))
    for ring in yrings:
        ring.hop3()
    weights = kv_full[...].reshape(-1, 2 * w)
    kv_seq[at.c] = nn(lowered[...], weights).astype(bf16)
    over = net.go(kv_seq.at[at.c], kv_seq.at[at.c], at.across)

    def seq_ring(zh):
        return Ring(net, lambda y, p: kv_seq.at[zh * 4 + y, part_of(p, tok)], at.y, at.up, at.down)

    near, far = seq_ring(at.zh), seq_ring(1 - at.zh)
    near.hop1()
    feeder.feed(feeds[0])
    saves.append(local.go(kv_full, full_out))
    d_att.hop2()
    logits = sum(nt(r, lowered[...]) for r in split3(router_t[...]))
    columns = to_column_form(jnp.concatenate([jnp.zeros_like(logits), logits], axis=0))
    hot = hot_lanes(routes_att[...])
    low = [jnp.sum(o * columns, axis=1, keepdims=True) for o in hot]
    lane = lax.broadcasted_iota(jnp.int32, (tok, 128), 1)
    g0 = 1.0 / (1.0 + jnp.exp(low[1] - low[0]))
    g1 = 1.0 / (1.0 + jnp.exp(low[0] - low[1]))
    info[...] = jnp.where(
        lane == 0, scale, jnp.where(lane == 1, g0, jnp.where(lane == 2, g1, columns / scale))
    )
    d_att.hop3()
    over.wait_recv()
    far.hop1()
    d_att.finish()
    saves.append(local.go(rows_att, rows_out))
    q_move.wait_recv()
    load_q = assemble(q_own, q_oth, wq, 0, at.f, local)
    near.hop2()
    o_move.wait_recv()
    load_o = assemble(o_own, o_oth, wo, 1, at.f, local)
    for d in load_q:
        d.wait()
    q_ref[...] = nn(rows_att[...], wq[...]).astype(bf16)
    near.hop3()
    far.hop2()
    d_g = Dispatch(net, at, slots_g, rows_g)
    d_g.start()
    feeder.feed(feeds[1])
    for m in moves:
        m.wait_recv()
    far.hop3()
    saves.append(local.go(kv_seq, seq_out))

    heads = q_ref.shape[1] // HD
    width = heads * HD
    scale = HD ** (-0.5)
    total = q_ref.shape[0]
    length = kv_seq.shape[0] * tok
    for h in range(heads):
        vt_ref[h] = kv_seq[:, :, (2 * h + 1) * HD : (2 * h + 2) * HD].reshape(length, HD).T
    for d in load_o:
        d.wait()
    col = Collect(net, at, p_ref, home, b_sib, b_a, b_b, b_l, b_r, b_f, home_net="late", total=total_ref)
    rows_at, keys_at = 2 * cap, 2 * tok
    d_g.hop1()
    pair = lambda g: [2 * g, 2 * g + 1]
    for step, g in enumerate(reversed(range(total // rows_at))):
        lo = g * rows_at
        extent = (g + 1) * keys_at
        at_key = extent - keys_at
        pos = pair_positions(pos_out, g, cap)
        for h in range(heads):
            cols = slice(h * HD, (h + 1) * HD)
            s = nt(kv_seq[: extent // tok, :, 2 * h * HD : (2 * h + 1) * HD].reshape(extent, HD), q_ref[lo : lo + rows_at, cols]) * scale
            ids = lax.broadcasted_iota(jnp.int32, (keys_at, rows_at), 0) + at_key
            last = jnp.where(ids <= pos, s[at_key:], masked_score)
            highest = jnp.max(last, axis=0, keepdims=True)
            if g:
                highest = jnp.maximum(highest, jnp.max(s[:at_key], axis=0, keepdims=True))
            e_last = jnp.exp(last - highest)
            sums = jnp.sum(e_last, axis=0, keepdims=True)
            mixed = nn(vt_ref[h, :, at_key:extent], e_last.astype(bf16))
            if g:
                e = jnp.exp(s[:at_key] - highest)
                sums = sums + jnp.sum(e, axis=0, keepdims=True)
                mixed = mixed + nn(vt_ref[h, :, :at_key], e.astype(bf16))
            att_ref[lo : lo + rows_at, cols] = (mixed / sums).T.astype(bf16)
            lse_ref[h : h + 1, lo : lo + rows_at] = highest + jnp.log(sums)
        out = nn(att_ref[lo : lo + rows_at, :], wo[...]).astype(bf16)
        for i in range(TP):
            for b in range(2):
                p_ref[i % 2, i // 2, 2 * g + b] = out[b * cap : (b + 1) * cap, i * width : (i + 1) * width]
        col.start(pair(g))
        if step == 0:
            d_g.hop2()
        if step >= 1:
            col.hop1(pair(g + 1))
        if step == 2:
            d_g.hop3()
        if step >= 2:
            col.hop2(pair(g + 2))
        if step >= 3:
            col.hop3(pair(g + 3))
    col.hop1(pair(0))
    col.hop2(pair(1))
    col.hop3(pair(2))
    col.hop2(pair(0))
    col.hop3(pair(1))
    d_g.finish()
    saves.append(local.go(rows_g, g_out))
    col.hop3(pair(0))
    col.all_home()
    feeder.feed(100)
    for d in saves:
        d.wait()
    col.finish()
    feeder.finish()
    net.drain()


def front(norm_in, router_t, routes_att, routes_mlp, kv_w, tokens, cot, q_own, o_own, gu_own, cap, feeds, cid):
    tok, width = tokens.shape
    part = width // TP
    _, kv_part, w = kv_w.shape
    heads = w // HD
    slots = CTX * cap
    block = (CTX, cap, part)
    large = [(slots, width), (CTX, tok, 2 * w), (FSDP * CTX, kv_part, 2 * w), (tok, width)]
    large += [(2 * tok, CTX * 128)] * 2
    out = [
        sds((CTX, 8, 128), jnp.int32), sds((tok, 128), f32), sds((slots, w), bf16), sds((slots, w), bf16),
        sds((heads, slots), f32), sds(block, bf16),
    ]
    out += [sds(z, bf16) for z in large + [(slots, width)]]
    out += [sds(q_own.shape, bf16), sds(o_own.shape, bf16), sds(gu_own.shape, bf16)]
    return pl.pallas_call(
        partial(front_body, feeds),
        out_shape=tuple(out),
        in_specs=vmem(5) + anywhere(5),
        out_specs=tuple(vmem(6) + anywhere(10)),
        scratch_shapes=[VM((tok, width), bf16), VM((tok, part), bf16)] + [VM(z, bf16) for z in large]
        + [
            VM(block, bf16), VM(block, bf16), VM((CTX, 8, 128), jnp.int32), VM((slots, width), bf16),
            VM((2, 4) + block, bf16), VM((width, w), bf16), VM((w, width), bf16), VM((heads, HD, CTX * tok), bf16),
        ]
        + Collect.scratch(*block) + [VM(block, bf16), DMA((16,))]
        + sems(2 * Dispatch.COPIES + Collect.COPIES + 120),
        compiler_params=params(cid),
        cost_estimate=cost(120),
    )(norm_in, router_t, routes_att, routes_mlp, kv_w, tokens, cot, q_own, o_own, gu_own)


def mid_body(
    plan,
    ret_att, info, routes, norm_mid_full, router_full, pick_att_any, pick_mlp_any, tokens, cot, rows_g, gu_own, gu_oth,
    down_own,
    att_picked, hidden, gates_out, grad_hidden, norm_grad, router_grad,
    proj_out, p1_out, gu_sent_out, gu_grad, dd_grad, dd_got, gu_got,
    pick_att, pick_mlp, grad_proj, p1, gu_sent, dd_sent,
    ret, b1_sib, b1_a, b1_b, b1_l, b1_r, fbuf,
    x_slots, X, G, W, D, gun, U, GG, GU, trans, p2, lm, small_out, small_in, small2_out, small2_in,
    sums_ref, gs_out, gs_in, sgm, sg_out, sg_in, sg_tot, sg_home, stage, toks, cots, mid_total, local_sem, stage_sem, send, recv,
):
    at, net = Place(), Net(send, recv)
    tok, part = lm.shape
    ff = down_own.shape[0]
    half = down_own.shape[1]
    cap = x_slots.shape[1]
    pad = W.shape[1] - ff
    mine = pl.ds(pl.multiple_of(at.f * half, half), half)
    other = pl.ds(pl.multiple_of((1 - at.f) * half, half), half)
    near = tp_peers(at)
    ret[...] = jnp.zeros_like(ret)
    for e in range(CTX):
        ret[0, e, : ret_att.shape[1], :] = ret_att[e]
    local = Local(local_sem)
    load = local.go
    load_a, load_m = load(pick_att_any, pick_att), load(pick_mlp_any, pick_mlp)
    here = pl.ds(pl.multiple_of(at.t * part, part), part)
    load_s = [load(tokens.at[:, here], toks), load(cot.at[:, here], cots)]
    load_g = load(rows_g, G)
    load_d = load(down_own, D.at[pl.ds(0, ff), mine])
    load_w = [
        load(gu_own, W.at[:, pl.ds(0, ff), mine]),
        load(gu_oth, W.at[:, pl.ds(0, ff), other]),
    ]
    greet(at.ctx_peers() + near + [at.partner])

    def down_piece(lo, hi):
        s = pl.ds(lo, hi - lo)
        return net.go(down_own.at[s], D.at[s, mine], at.partner)

    d_cut = plan["down"]
    down_moves = [down_piece(0, d_cut[0])]
    W[:, ff:, :] = jnp.zeros_like(W[:, ff:, :])
    D[ff:, :] = jnp.zeros_like(D[ff:, :])
    lane = lax.broadcasted_iota(jnp.int32, (tok, 128), 1)
    hot = hot_lanes(routes[...])
    ga = [info[:, k : k + 1] for k in (1, 2)]
    norm = norm_mid_full[0:1, here]
    router_t = router_full[:, here]
    router = jnp.concatenate([jnp.zeros((FIRST, part), f32), router_t, jnp.zeros((128 - FIRST - CTX, part), f32)]).T
    for d in load_s + [load_a, load_m]:
        d.wait()
    picked = nn(pick_att[...], ret[0].reshape(-1, part))
    att_picked[...] = picked.astype(bf16)
    h = wide(toks[...]) + ga[0] * picked[:tok] + ga[1] * picked[tok:]
    hidden[...] = h
    raw = exact(h * norm, router)
    sums = jnp.where(lane == 0, jnp.sum(h * h, axis=1, keepdims=True), raw)
    small_out[...] = to_row_form(sums, 16)
    moves = [net.go(small_out, small_in.at[j], p) for j, p in enumerate(near)]
    total = small_out[...]
    for j, m in enumerate(moves):
        m.wait_recv()
        total = total + small_in[j]
    sums = to_column_form(total)
    scale = lax.rsqrt(sums[:, 0:1] / (part * TP) + epsilon)
    low = [jnp.sum(o * sums, axis=1, keepdims=True) * scale for o in hot]
    g0 = 1.0 / (1.0 + jnp.exp(low[1] - low[0]))
    g1 = 1.0 / (1.0 + jnp.exp(low[0] - low[1]))
    gates = jnp.where(lane == 0, g0, jnp.where(lane == 1, g1, jnp.where(lane == 2, scale, 0.0)))
    sums_ref[...] = sums
    gates_out[...] = gates
    lm[...] = (hidden[...] * scale * norm).astype(bf16)
    slots = tn(pick_mlp[:tok, :] + pick_mlp[tok:, :], lm[...]).astype(bf16)
    for e in range(CTX):
        x_slots[e] = slots[e * 128 : e * 128 + cap]
    d1 = Dispatch(net, at, x_slots, X)
    d1.start()
    rows2 = to_row_form(gates, 2)
    pair_row = jnp.concatenate([rows2[0:1], rows2[1:2]], axis=1)
    slot_gates = jnp.sum(nn(three_rows(pair_row), pick_mlp[...]), axis=0, keepdims=True)
    for e in range(CTX):
        gs_out[e] = jnp.broadcast_to(slot_gates[:, e * 128 : (e + 1) * 128], (8, 128))
    gs_moves = [net.go(gs_out.at[p["ctx"]], gs_in.at[at.c], p) for p in at.ctx_peers()]
    gs_in[at.c] = gs_out[at.c]
    down_moves.append(down_piece(d_cut[1], ff))
    d1.hop1()
    for m in gs_moves:
        m.wait_recv()
    load_g.wait()
    for b in range(CTX):
        column = gs_in[b].T[:cap, 0:1]
        s = slice(b * cap, (b + 1) * cap)
        G[s, :] = (wide(G[s, :]) * column).astype(bf16)
    d1.hop2()
    load_d.wait()
    for m in down_moves:
        m.wait_recv()
    rows_at = 2 * cap
    groups = CTX // 2

    def group_rows(g):
        return pl.ds(pl.multiple_of(g * rows_at, rows_at), rows_at)

    @pl.loop(0, groups)
    def _(g):
        s = group_rows(g)
        gun[s, :] = nt(G[s, :], D[...])

    d1.hop3()
    d1.finish()
    for m in load_w:
        m.wait()
    sgm[...] = jnp.zeros_like(sgm)

    def put(p_ref, g, out):
        for i in range(TP):
            for b in range(2):
                p_ref[i % 2, i // 2, 2 * g + b] = out[b * cap : (b + 1) * cap, i * part : (i + 1) * part]

    net.drain()
    col2 = Collect(net, at, p2, ret.at[1], b1_sib, b1_a, b1_b, b1_l, b1_r, fbuf, home_net="late", total=mid_total)
    pair = lambda g: [2 * g, 2 * g + 1]
    for g in range(groups):
        s = group_rows(g)
        x = X[s, :]
        gate = nt(x, W[0])
        up = nt(x, W[1])
        sig = 1.0 / (1.0 + jnp.exp(-gate))
        silu = gate * sig
        units = (silu * up).astype(bf16)
        grad = gun[s, :]
        d_gate = (grad * up * (sig * (1.0 + gate * (1.0 - sig)))).astype(bf16)
        d_up = (grad * silu).astype(bf16)
        U[s, :] = units
        GG[s, :] = d_gate
        GU[s, :] = d_up
        column = jnp.sum(wide(units) * grad, axis=1, keepdims=True)
        for b in range(2):
            sgm[2 * g + b, :cap, :] = jnp.broadcast_to(column[b * cap : (b + 1) * cap], (cap, 128))
        put(p2, g, (nn(d_gate, W[0]) + nn(d_up, W[1])).astype(bf16))
        col2.start(pair(g))
        if g >= 1:
            col2.hop1(pair(g - 1))
        if g >= 2:
            col2.hop2(pair(g - 2))
        if g >= 3:
            col2.hop3(pair(g - 3))
    for b in range(CTX):
        sg_out[b] = sgm[b].T[:8]
    sg_moves = [net.go(sg_out, sg_in.at[j], p) for j, p in enumerate(near)]

    saves = []
    cols = stage.shape[2]
    steps = half // cols
    trans[...] = U[...].T

    @pl.loop(0, steps)
    def _(i):
        src = pl.ds(pl.multiple_of((1 - at.f) * half + i * cols, cols), cols)
        dd_sent[:, pl.ds(pl.multiple_of(i * cols, cols), cols)] = nn(trans[...], G[:, src])[:ff].astype(bf16)

    cut = plan["dd"]
    feeder = Feeder(net, at.partner, [(dd_sent, dd_got, 0, 0, ff, ff // 11)])
    rows = gu_got.shape[1]
    gu_feeder = Feeder(net, at.partner, [(gu_sent, gu_got, 1, 0, rows, ff // 22)])
    feeder.feed(cut[0])
    col2.hop1(pair(3))
    col2.hop2(pair(2))
    col2.hop3(pair(1))
    v = sg_out[...]
    for j, m in enumerate(sg_moves):
        m.wait_recv()
        v = v + sg_in[j]
    sg_tot[...] = v
    sg_moves = [net.go(sg_tot.at[p["ctx"]], sg_home.at[at.c], p) for p in at.ctx_peers()]
    sg_home[at.c] = sg_tot[at.c]

    col2.hop2(pair(3))
    col2.hop3(pair(2))

    def own_part(matrix, dst, first):
        out = []
        for i in range(steps):
            slot = (first + i) % 2
            if first + i >= 2:
                stage_copies[first + i - 2].wait()
            src = pl.ds(pl.multiple_of(at.f * half + i * cols, cols), cols)
            stage[slot] = nn(trans[...], matrix[:, src])[:ff].astype(bf16)
            d = pltpu.make_async_copy(stage.at[slot], dst(pl.ds(i * cols, cols)), stage_sem.at[slot])
            d.start()
            stage_copies.append(d)

    stage_copies = []
    col2.hop3(pair(3))
    col2.all_home()
    feeder.feed(cut[1])
    own_part(G, lambda s: dd_grad.at[:, s], 0)
    col2.finish()

    lane = lax.broadcasted_iota(jnp.int32, (tok, 128), 1)
    hot = hot_lanes(routes[...])
    ga = [info[:, k : k + 1] for k in (1, 2)]
    norm = norm_mid_full[0:1, here]
    router_t = router_full[:, here]
    sums = sums_ref[...]
    gates = gates_out[...]
    scale = gates[:, 2:3]
    back = nn(pick_mlp[...], ret[1].reshape(-1, part))
    back = back[:tok] + back[tok:]
    h = hidden[...]
    inner = jnp.sum(back * norm * h, axis=1, keepdims=True)
    small2_out[...] = to_row_form(jnp.where(lane == 0, inner, 0.0), 8)
    moves = [net.go(small2_out, small2_in.at[j], p) for j, p in enumerate(near)]
    for m in sg_moves:
        m.wait_recv()
    row = jnp.concatenate([sg_home[e][0:1] for e in range(CTX)], axis=1)
    pairs = jnp.sum(nt(pick_mlp[...], three_rows(row)), axis=1, keepdims=True)
    sg = [pairs[:tok], pairs[tok:]]
    grad_logits = sum(
        o * (d - gates[:, k : k + 1] * (sg[0] + sg[1])) for k, (o, d) in enumerate(zip(hot, sg))
    )
    grad_low = back
    for e in range(CTX):
        grad_low = grad_low + grad_logits[:, FIRST + e : FIRST + e + 1] * router_t[e : e + 1, :]
    total = small2_out[...]
    for j, m in enumerate(moves):
        m.wait_recv()
        total = total + small2_in[j]
    inner = to_column_form(total)[:, 0:1] + jnp.sum(grad_logits * sums, axis=1, keepdims=True)
    gh = (
        wide(cots[...]) + scale * (grad_low * norm) - h * (scale * scale * scale) * (inner / (part * TP))
    )
    grad_hidden[...] = gh
    pair_rows = jnp.concatenate([(ga[0] * gh).astype(bf16), (ga[1] * gh).astype(bf16)], axis=0)
    slots = tn(pick_att[...], pair_rows).astype(bf16)
    for e in range(CTX):
        x_slots[e] = slots[e * 128 : e * 128 + cap]
    d2 = Dispatch(net, at, x_slots, grad_proj)
    d2.start()
    feeder.feed(cut[2])
    norm_grad[...] = jnp.broadcast_to(jnp.sum(grad_low * h * scale, axis=0, keepdims=True), norm_grad.shape)
    router_grad[...] = sum(tn(g, lm[...]) for g in split3(grad_logits))
    for j, grads in enumerate((GG, GU)):
        trans[...] = grads[...].T

        @pl.loop(0, steps)
        def _(i):
            src = pl.ds(pl.multiple_of((1 - at.f) * half + i * cols, cols), cols)
            gu_sent[j, :, pl.ds(pl.multiple_of(i * cols, cols), cols)] = nn(trans[...], X[:, src])[:ff].astype(bf16)

        if j == 1:
            gu_feeder.feed(100)
        own_part(X, lambda s, j=j: gu_grad.at[j, :, s], (j + 1) * steps)
        if j == 0:
            d2.hop1()
    saves.append(local.go(gu_sent, gu_sent_out))
    d2.hop2()

    @pl.loop(0, groups)
    def _(g):
        s = group_rows(g)
        put(p1, g, nn(U[s, :], D[...]).astype(bf16))

    saves.append(local.go(p1, p1_out))
    d2.hop3()
    d2.finish()
    saves.append(local.go(grad_proj, proj_out))
    for d in saves + stage_copies[-2:]:
        d.wait()
    feeder.finish()
    gu_feeder.finish()
    net.drain()


def mid(
    plan, ret_att, info, routes, norm_mid, router_t, pick_att, pick_mlp, tokens, cot, rows_g, gu_own, gu_oth, down_own, cid,
):
    tok, width = tokens.shape
    part = width // TP
    n, cap, _ = ret_att.shape
    p_shape = (2, 4, n, cap, part)
    slots, width = rows_g.shape
    ff, half = down_own.shape
    ffp = (ff + 255) // 256 * 256
    cols = 256
    bufs = Collect.scratch(n, cap, part)
    vm_out = (
        sds((2 * tok, part), bf16), sds((tok, part), f32), sds((tok, 128), f32), sds((tok, part), f32),
        sds((8, part), f32), sds((128, part), f32),
    )
    any_out = (
        sds((slots, width), bf16), sds(p_shape, bf16), sds((2, ff, half), bf16),
        sds((2, ff, half), bf16), sds((ff, half), bf16), sds((ff, half), bf16), sds((2, plan["gu"], half), bf16))
    return pl.pallas_call(
        partial(mid_body, plan),
        out_shape=vm_out + any_out,
        in_specs=vmem(5) + anywhere(8),
        out_specs=tuple(vmem(len(vm_out)) + anywhere(len(any_out))),
        scratch_shapes=[
            VM(pick_att.shape, bf16), VM(pick_att.shape, bf16), VM((slots, width), bf16),
            VM(p_shape, bf16), VM((2, ff, half), bf16), VM((ff, half), bf16), VM((2, n, 128, part), bf16),
        ]
        + bufs
        + [
            VM((n, cap, part), bf16), VM((slots, width), bf16), VM((slots, width), bf16),
            VM((2, ffp, width), bf16), VM((ffp, width), bf16), VM((slots, ffp), f32),
            VM((slots, ffp), bf16), VM((slots, ffp), bf16), VM((slots, ffp), bf16), VM((ffp, slots), bf16),
            VM(p_shape, bf16), VM((tok, part), bf16),
            VM((16, tok), f32), VM((TP - 1, 16, tok), f32), VM((8, tok), f32), VM((TP - 1, 8, tok), f32),
            VM((tok, 128), f32), VM((n, 8, 128), f32), VM((n, 8, 128), f32), VM((n, 128, 128), f32),
            VM((n, 8, 128), f32), VM((TP - 1, n, 8, 128), f32), VM((n, 8, 128), f32), VM((n, 8, 128), f32),
            VM((2, ff, cols), bf16), VM((tok, part), bf16), VM((tok, part), bf16), VM((n, cap, part), bf16), DMA((16,)), DMA((2,)),
        ]
        + sems(Collect.COPIES + 2 * Dispatch.COPIES + 80),
        compiler_params=params(cid),
        cost_estimate=cost(140),
    )(
        ret_att, info, routes, norm_mid, router_t, pick_att, pick_mlp, tokens, cot, rows_g, gu_own, gu_oth, down_own,
    )


def back_body(
    cap, tok, cuts,
    q_ref, pos_ref, att_ref, lse_ref, hidden, gates_mlp, att_picked, grad_hidden, info, routes, norm_in, router_t,
    norm_mid_grad, router_mlp_grad,
    proj_any, rows_any, kv_any, p1_any, q_own, q_oth, o_own, o_oth, full_any, lowered_any, pick_att_any, pick_mlp_any,
    tokens, gu_sent,
    kvw_out, result, input_grad, minor_out, q_sent, o_grad, q_grad, gu_got, o_got,
    rows_ref, kv_ref, p_ref, wq, wo, do_ref, dq_ref, kt_ref, acc_ref, o_sent, o_keep, q_keep,
    b_sib, b_a, b_b, b_l, b_r, b_f,
    seq_stage, seq_half, seq_whole, over_out, over_in, own_ref, kv_low,
    p2, c2_sib, c2_a, c2_b, c2_l, c2_r, c2_f,
    w_part, w_stage, w_half, w_whole, w_sum, wz_stage, wz_half, wz_whole,
    ret, mlp_ret, mlp_total, kv_back, x_res, x_in, small_out, small_in, minor, minor_in, minor_sum, rgrad, toks, lowered,
    credit, local_sem, send, recv,
):
    at, net, first_net, local = Place(), Net(send, recv, Collect.COPIES), Net(send, recv), Local(local_sem)
    heads = q_ref.shape[1] // HD
    width = heads * HD
    full_width = width * TP
    w = 2 * width
    part = width
    kv_part = full_width // (FSDP * CTX)
    scale = HD ** (-0.5)
    total = q_ref.shape[0]
    half = o_own.shape[1]
    mine = pl.ds(pl.multiple_of(at.t * part, part), part)
    load_o = assemble(o_own, o_oth, wo, 1, at.f, local) + [local.go(proj_any, rows_ref)]
    load_p = local.go(p1_any, p_ref)
    load_kv = local.go(kv_any, kv_ref)
    load_q = assemble(q_own, q_oth, wq, 0, at.f, local)
    load_t = [local.go(tokens, toks), local.go(lowered_any, lowered)]
    ret[...] = jnp.zeros_like(ret)
    mlp_ret[...] = jnp.zeros_like(mlp_ret)
    acc_ref[...] = jnp.zeros_like(acc_ref)
    near_tp = tp_peers(at)
    far_all = all_peers(at)
    greet(far_all + near_tp)

    unit = gu_sent.shape[1] // 22
    gu_rows = gu_got.shape[1]
    before = gu_sent.shape[1] - gu_rows
    lead = unit * cuts[0]
    feeder = Feeder(net, at.partner, [
        (gu_sent, gu_got.at[:, pl.ds(0, lead)], 1, before, lead, unit),
        (o_sent, o_got, 0, 0, o_sent.shape[0], o_sent.shape[0] // 4),
        (gu_sent, gu_got.at[:, pl.ds(lead, gu_rows - lead)], 1, before + lead, gu_rows - lead, unit),
    ])
    feeder.feed(cuts[0])
    load_p.wait()
    col1 = Collect(first_net, at, p_ref, mlp_ret, b_sib, b_a, b_b, b_l, b_r, b_f, home_net=net, total=mlp_total)
    col1.start()
    for d in load_o:
        d.wait()
    do_ref[...] = nt(rows_ref[...], wo[...]).astype(bf16)
    col1.hop1()

    step_cols = 256
    steps = half // step_cols
    att_t = att_ref[...].T
    for i in range(steps):
        here = slice(i * step_cols, (i + 1) * step_cols)
        own_cols = pl.ds(pl.multiple_of(at.f * half + i * step_cols, step_cols), step_cols)
        other_cols = pl.ds(pl.multiple_of((1 - at.f) * half + i * step_cols, step_cols), step_cols)
        o_sent[:, here] = nn(att_t, rows_ref[:, other_cols]).astype(bf16)
        o_keep[:, here] = nn(att_t, rows_ref[:, own_cols]).astype(bf16)
    feeder.feed(cuts[1])
    saves = [local.go(o_keep, o_grad)]
    load_rows = local.go(rows_any, rows_ref)
    load_kv.wait()
    for h in range(heads):
        kt_ref[h] = kv_ref[:, 2 * h * HD : (2 * h + 1) * HD].T
    rows_at, keys_at = 2 * cap, 2 * tok
    key_scale = jnp.where(lax.broadcasted_iota(jnp.int32, (1, 2 * HD), 1) < HD, scale, 1.0)

    def seq_sum(h, zh):
        i = 2 * h + zh
        span = slice(2 * h * HD, 2 * (h + 1) * HD)
        lands = {"a": seq_half.at[i, 0], "b": seq_half.at[i, 1], "l": seq_whole.at[i, 0], "r": seq_whole.at[i, 1]}

        def own(y, p):
            size = tok if p is None else tok // 2
            lo = zh * 4 * tok + y * tok + (0 if p is None else p * (tok // 2))
            return acc_ref[pl.ds(pl.multiple_of(lo, 64), size), span] * key_scale

        return RingSum(
            net, own, lambda y, p: seq_stage.at[i, y, part_of(p, tok)], lambda name: lands[name],
            at.y, at.up, at.down,
        )

    seqs = [[seq_sum(h, zh) for zh in range(2)] for h in range(heads)]
    first_half = at.zh == 0
    overs = [None] * heads

    def seq_done(h, zh):
        span = slice(2 * h * HD, 2 * (h + 1) * HD)
        total_here = seqs[h][zh].hop3()
        if zh == 1:
            own_ref[:, span] = total_here
            return
        high = own_ref[:, span]
        over_out[h] = jnp.where(first_half, high, total_here).astype(bf16)
        own_ref[:, span] = jnp.where(first_half, total_here, high)
        overs[h] = net.go(over_out.at[h], over_in.at[h], at.across)

    for h in range(heads):
        cols = slice(h * HD, (h + 1) * HD)
        kcols = slice(2 * h * HD, (2 * h + 1) * HD)
        vcols = slice((2 * h + 1) * HD, (2 * h + 2) * HD)
        for g in reversed(range(total // rows_at)):
            lo = g * rows_at
            rows = slice(lo, lo + rows_at)
            extent = (g + 1) * keys_at
            at_key = extent - keys_at
            pos = pair_positions(pos_ref, g, cap)
            q = q_ref[rows, cols]
            do = do_ref[rows, cols]
            s = nt(kv_ref[:extent, kcols], q) * scale
            lse = lse_ref[h : h + 1, rows]
            ids = lax.broadcasted_iota(jnp.int32, (keys_at, rows_at), 0) + at_key
            last = jnp.where(ids <= pos, s[at_key:], masked_score)
            s = jnp.concatenate([s[:at_key], last], axis=0) if g else last
            soft = jnp.exp(s - lse)
            dp = nt(kv_ref[:extent, vcols], do)
            inner = jnp.sum(soft * dp, axis=0, keepdims=True)
            ds = (soft * (dp - inner)).astype(bf16)
            acc_ref[:extent, vcols] += nn(soft.astype(bf16), do)
            acc_ref[:extent, kcols] += nn(ds, q)
            dq_ref[rows, cols] = (nn(kt_ref[h, :, :extent], ds) * scale).T.astype(bf16)
            if h == 0 and g == 3:
                col1.hop2()
            if g == 2:
                seqs[h][1].hop1()
            if h == 0 and g == 2:
                col1.hop3()
                for axes in at.tp_near():
                    pl.semaphore_signal(credit, inc=1, device_id=axes, device_id_type=MESH)
            if g == 1:
                seqs[h][1].hop2()
            if g == 0:
                seqs[h][0].hop1()
            if h == 1 and g == 3:
                seq_done(0, 1)
                seqs[0][0].hop2()
            if h == 1 and g == 1:
                seq_done(0, 0)
                feeder.feed(cuts[2])
    load_full = local.go(full_any, kv_ref.at[pl.ds(0, full_width)])
    for d in load_q:
        d.wait()
    first_net.drain()
    for g in range(total // rows_at):
        rows = slice(g * rows_at, (g + 1) * rows_at)
        out = nt(dq_ref[rows, :], wq[...]).astype(bf16)
        for i in range(TP):
            for b in range(2):
                p_ref[i % 2, i // 2, 2 * g + b] = out[b * cap : (b + 1) * cap, i * width : (i + 1) * width]
    pl.semaphore_wait(credit, 3)
    col = Collect(net, at, p_ref, ret, b_sib, b_a, b_b, b_l, b_r, b_f)
    col.start()
    seq_done(1, 1)
    seqs[1][0].hop2()
    col.hop1()
    load_rows.wait()
    for i in range(steps):
        here = slice(i * step_cols, (i + 1) * step_cols)
        own_cols = pl.ds(pl.multiple_of(at.f * half + i * step_cols, step_cols), step_cols)
        other_cols = pl.ds(pl.multiple_of((1 - at.f) * half + i * step_cols, step_cols), step_cols)
        q_sent[here, :] = tn(rows_ref[:, other_cols], dq_ref[...]).astype(bf16)
        q_keep[here, :] = tn(rows_ref[:, own_cols], dq_ref[...]).astype(bf16)
    saves.append(local.go(q_keep, q_grad))
    picks = full_width // 2
    load_picks = [
        local.go(pick_att_any, rows_ref.at[:, pl.ds(0, picks)]),
        local.go(pick_mlp_any, rows_ref.at[:, pl.ds(picks, picks)]),
    ]
    low_half = slice(0, 2 * HD)
    overs[0].wait_recv()
    kv_low[:, low_half] = (own_ref[:, low_half] + wide(over_in[0])).astype(bf16)
    seq_done(1, 0)
    feeder.feed(cuts[3])

    def index(z, y):
        return lax.rem(z, 2) * CTX + (z // 2) * 4 + y

    order = [lax.rem(at.z + i, 4) for i in (2, 1, 3, 0)]

    def weight_rings(h):
        span = slice(2 * h * HD, 2 * (h + 1) * HD)
        low = kv_low[:, span]
        for i in range(4):
            cols = full_width // 4
            block = tn(lowered[:, i * cols : (i + 1) * cols], low).astype(bf16)
            per = cols // kv_part
            w_part[h, i * per : (i + 1) * per] = block.reshape(per, kv_part, 2 * HD)
        out = []
        for i, z in enumerate(order):
            lands = {
                "a": w_half.at[h, i, 0], "b": w_half.at[h, i, 1], "l": w_whole.at[h, i, 0], "r": w_whole.at[h, i, 1]
            }
            out.append(RingSum(
                net,
                lambda y, p, z=z: wide(w_part[h, index(z, y), part_of(p, kv_part)]),
                lambda y, p, i=i: w_stage.at[h, i, y, part_of(p, kv_part)],
                lambda name, lands=lands: lands[name],
                at.y, at.up, at.down,
            ))
        for ring in out:
            ring.hop1()
        return out

    for d in load_t:
        d.wait()
    wrings = [weight_rings(0)]
    col.hop2()
    load_full.wait()
    for ring in wrings[0]:
        ring.hop2()
    col1.finish()
    for d in load_picks:
        d.wait()
    picked = nn(rows_ref[:, picks:], mlp_ret[...].reshape(-1, part))
    gates = gates_mlp[...]
    value = hidden[...] + gates[:, 0:1] * picked[:tok] + gates[:, 1:2] * picked[tok:]
    x_res[...] = value.astype(bf16).reshape(x_res.shape)
    d_res = Dispatch(net, at, x_res, result, exchange=False)
    d_res.start()
    d_res.hop1()
    col.hop3()
    feeder.feed(cuts[4])
    high_half = slice(2 * HD, 4 * HD)
    overs[1].wait_recv()
    kv_low[:, high_half] = (own_ref[:, high_half] + wide(over_in[1])).astype(bf16)
    back_rows = nt(kv_low[...], kv_ref[:full_width, :])
    n2, rows2, w2 = p2.shape[2:]
    for i in range(TP):
        p2[i % 2, i // 2] = back_rows[:, i * w2 : (i + 1) * w2].astype(bf16).reshape(n2, rows2, w2)
    col2 = Collect(net, at, p2, kv_back, c2_sib, c2_a, c2_b, c2_l, c2_r, c2_f, exchange=False)
    col2.start()
    inner_kv = jnp.sum(back_rows * (wide(toks[...]) * norm_in[0:1, :]), axis=1, keepdims=True)
    wrings.append(weight_rings(1))
    col2.hop1()
    d_res.hop2()
    feeder.feed(cuts[5])
    for ring in wrings[1]:
        ring.hop2()
    col.finish()
    feeder.feed(cuts[6])
    col2.hop2()

    inputs = wide(toks[:, mine])
    norm = norm_in[0:1, mine]
    gh = grad_hidden[...]
    grad_low = nn(rows_ref[:, :picks], ret[...].reshape(-1, part))
    grad_low = grad_low[:tok] + grad_low[tok:]
    lane = lax.broadcasted_iota(jnp.int32, (tok, 128), 1)
    facts = info[...]
    d0 = jnp.sum(wide(att_picked[:tok, :]) * gh, axis=1, keepdims=True)
    d1 = jnp.sum(wide(att_picked[tok:, :]) * gh, axis=1, keepdims=True)
    inner = jnp.sum(grad_low * norm * inputs, axis=1, keepdims=True) + inner_kv
    sums = jnp.where(lane == 0, d0, jnp.where(lane == 1, d1, jnp.where(lane == 2, inner, 0.0)))
    small_out[...] = to_row_form(sums, 8)
    smalls = [net.go(small_out, small_in.at[j], p) for j, p in enumerate(near_tp)]
    for h in range(heads):
        for z, ring in zip(order, wrings[h]):
            w_sum[z, :, 2 * h * HD : 2 * (h + 1) * HD] = ring.hop3()

    lands = {"a": wz_half.at[0], "b": wz_half.at[1], "l": wz_whole.at[0], "r": wz_whole.at[1]}
    zsum = RingSum(
        net,
        lambda z, p: w_sum[z, part_of(p, kv_part)],
        lambda z, p: wz_stage.at[z, part_of(p, kv_part)],
        lambda name: lands[name],
        at.z, at.above, at.below,
    )
    zsum.hop1()
    col2.hop3()
    grad_low = grad_low + wide(kv_back[...].reshape(tok, part))
    total_row = small_out[...]
    for j, m in enumerate(smalls):
        m.wait_recv()
        total_row = total_row + small_in[j]
    sums = to_column_form(total_row)
    row_scale, g0, g1 = facts[:, 0:1], facts[:, 1:2], facts[:, 2:3]
    inner = g0 * sums[:, 0:1] + g1 * sums[:, 1:2]
    hot = hot_lanes(routes[...])
    grad_logits = hot[0] * (g0 * (sums[:, 0:1] - inner)) + hot[1] * (g1 * (sums[:, 1:2] - inner))
    for e in range(CTX):
        grad_low = grad_low + grad_logits[:, FIRST + e : FIRST + e + 1] * router_t[e : e + 1, mine]
    inner = sums[:, 2:3] + jnp.sum(grad_logits * facts, axis=1, keepdims=True)
    cubed = row_scale * row_scale * row_scale
    grad = gh + row_scale * (grad_low * norm) - inputs * cubed * (inner / full_width)
    x_in[...] = grad.astype(bf16).reshape(x_in.shape)
    d_in = Dispatch(net, at, x_in, input_grad, exchange=False)
    d_in.start()
    d_in.hop1()
    rgrad[...] = sum(tn(g, lowered[:, mine]) for g in split3(grad_logits))
    norm_grad = jnp.sum(grad_low * inputs * row_scale, axis=0, keepdims=True)
    row = lax.broadcasted_iota(jnp.int32, (8, part), 0)
    minor[0:8, :] = jnp.where(row == 0, norm_grad, jnp.where(row == 1, norm_mid_grad[0:1, :], 0.0))
    minor[8:16, :] = rgrad[FIRST : FIRST + CTX, :]
    minor[16:24, :] = router_mlp_grad[FIRST : FIRST + CTX, :]
    minors = [net.go(minor, minor_in.at[j], p) for j, p in enumerate(far_all)]
    zsum.hop2()
    feeder.feed(100)
    d_in.hop2()
    d_res.hop3()
    total_row = minor[...]
    for j, m in enumerate(minors):
        m.wait_recv()
        total_row = total_row + minor_in[j]
    minor_sum[...] = total_row
    minors = [net.go(minor_sum, minor_out.at[at.t], p) for p in near_tp]
    minor_out[at.t] = total_row
    d_in.hop3()
    kvw_out[...] = zsum.hop3()
    d_res.finish()
    d_in.finish()
    col2.finish()
    for m in minors:
        m.wait_recv()
    feeder.finish()
    for d in saves:
        d.wait()
    net.drain()


def back(small, large, cuts, gu_rows, tok, cap, cid):
    q = small[0]
    proj, rows, kv, p1, q_own, _, o_own, _, _, lowered, _, _, _, gu_sent = large
    slots, w = q.shape
    heads = w // HD
    width = w * TP
    kw = 2 * w
    part = width // (FSDP * CTX)
    _, _, n, _, _ = p1.shape
    n2 = 4
    rows2 = tok // n2
    ff, half = gu_sent.shape[1:]
    vm_out = (
        sds((part, kw), f32), sds((tok, width), bf16), sds((tok, width), bf16), sds((TP, 24, w), f32),
        sds(q_own.shape, bf16),
    )
    any_out = (
        sds(o_own.shape, bf16), sds(q_own.shape, bf16), sds((2, gu_rows, half), bf16),
        sds(o_own.shape, bf16),
    )
    out = pl.pallas_call(
        partial(back_body, cap, tok, cuts),
        out_shape=vm_out + any_out,
        in_specs=vmem(len(small)) + anywhere(len(large)),
        out_specs=tuple(vmem(len(vm_out)) + anywhere(len(any_out))),
        scratch_shapes=[
            VM((slots, width), bf16), VM(kv.shape, bf16), VM(p1.shape, bf16),
            VM((width, w), bf16), VM((w, width), bf16), VM((slots, w), bf16), VM((slots, w), bf16), VM((heads, HD, kv.shape[0]), bf16), VM(kv.shape, f32),
            VM(o_own.shape, bf16), VM(o_own.shape, bf16), VM(q_own.shape, bf16),
        ]
        + Collect.scratch(n, cap, w)
        + [
            VM((2 * heads, 4, tok, w), bf16), VM((2 * heads, 2, tok // 2, w), bf16), VM((2 * heads, 2, tok, w), bf16),
            VM((heads, tok, w), bf16), VM((heads, tok, w), bf16), VM((tok, kw), f32), VM((tok, kw), bf16),
        ]
        + [VM((2, 4, n2, rows2, w), bf16)] + Collect.scratch(n2, rows2, w)
        + [
            VM((heads, FSDP * CTX, part, w), bf16), VM((heads, 4, 4, part, w), bf16),
            VM((heads, 4, 2, part // 2, w), bf16), VM((heads, 4, 2, part, w), bf16), VM((4, part, kw), f32), VM((4, part, kw), bf16),
            VM((2, part // 2, kw), bf16), VM((2, part, kw), bf16),
            VM((n, 128, w), bf16), VM((n, 128, w), bf16), VM((n, cap, w), bf16), VM((n2, rows2, w), bf16),
            VM((n2, rows2, w), bf16), VM((n2, rows2, w), bf16), VM((8, tok), f32), VM((TP - 1, 8, tok), f32),
            VM((24, w), f32), VM((FSDP * CTX - 1, 24, w), f32), VM((24, w), f32), VM((128, w), f32),
            VM((tok, width), bf16), VM((tok, width), bf16),
            pltpu.SemaphoreType.REGULAR, DMA((20,)),
        ]
        + sems(Collect.COPIES * 3 + Dispatch.COPIES * 2 + 180),
        compiler_params=params(cid),
        cost_estimate=cost(120),
    )(*small, *large)
    kvw, result, input_grad, minor, q_sent, o_grad, q_grad, gu_got, o_got = out
    return o_grad, q_grad, kvw, result, input_grad, minor, gu_got, o_got, q_sent


def finish_body(
    gu_a, gu_b, gu_c, dd_a, dd_b, o_a, o_b, ig, res, kvw, minor,
    gu, dd, o, grad, result, kv, n_in, n_mid, r_att, r_mlp, *refs,
):
    ins, outs, (load_sem, save_sem) = refs[:8], refs[8:12], refs[12:]
    me = lax.axis_index("fsdp") * CTX + lax.axis_index("ctx")
    early = gu_b.shape[1]
    sources = (gu_a, None, dd_a, dd_b, o_a, o_b, ig)
    pieces = [(0, j, i) for j in range(2) for i in range(4)] + [(2, 0, i) for i in range(4)]
    pieces += [(4, 0, 0)] + [(6, 0, i) for i in range(2)]
    targets = {0: (gu, outs[0]), 2: (dd, outs[1]), 4: (o, outs[2]), 6: (grad, outs[3])}
    counts = {0: 4, 2: 4, 4: 1, 6: 2}

    def span(ref, k, j, i):
        rows = ref.shape[-2] // counts[k]
        s = pl.ds(i * rows, rows)
        return ref.at[j, s] if k == 0 else ref.at[s]

    loads = []
    for n, (k, j, i) in enumerate(pieces):
        both = []
        if k == 0:
            rows = ins[1].shape[1] // counts[0]
            lo, hi = i * rows, (i + 1) * rows
            for m, (src, a, b, shift) in enumerate(
                ((gu_b, lo, min(hi, early), 0), (gu_c, max(lo, early), hi, early))
            ):
                if a < b:
                    d = pltpu.make_async_copy(
                        src.at[j, pl.ds(a - shift, b - a)], ins[1].at[j, pl.ds(a, b - a)], load_sem.at[n, 1 + m]
                    )
                    d.start()
                    both.append(d)
        for m in range(1 if k in (0, 6) else 2):
            d = pltpu.make_async_copy(span(sources[k + m], k, j, i), span(ins[k + m], k, j, i), load_sem.at[n, m])
            d.start()
            both.append(d)
        loads.append(both)
    copy = pltpu.make_async_copy(res, ins[7], load_sem.at[len(pieces), 0])
    copy.start()
    w = kv.shape[2]
    for h in range(w // HD):
        for j in range(2):
            kv[j, :, h * HD : (h + 1) * HD] = kvw[:, (2 * h + j) * HD : (2 * h + j + 1) * HD]
    mine = minor[me // 2, :, pl.ds(pl.multiple_of(lax.rem(me, 2) * 128, 128), 128)]
    n_in[...] = mine[0:1]
    n_mid[...] = mine[1:2]
    r_att[...] = mine[8:16]
    r_mlp[...] = mine[16:24]
    copy.wait()
    saves = [pltpu.make_async_copy(ins[7], result, load_sem.at[len(pieces), 1])]
    saves[0].start()
    for n, (k, j, i) in enumerate(pieces):
        for d in loads[n]:
            d.wait()
        v = wide(span(ins[k], k, j, i)[...])
        if k != 6:
            v = v + wide(span(ins[k + 1], k, j, i)[...])
        dst, buf = targets[k]
        span(buf, k, j, i)[...] = v
        d = pltpu.make_async_copy(span(buf, k, j, i), span(dst, k, j, i), save_sem.at[n])
        d.start()
        saves.append(d)
    for d in saves:
        d.wait()


def finish(gu_a, gu_b, gu_c, dd_a, dd_b, o_a, o_b, ig, res, kvw, minor):
    part, kw = kvw.shape
    args = (gu_a, gu_b, gu_c, dd_a, dd_b, o_a, o_b, ig, res)
    held = (gu_a, gu_a) + args[3:]
    sums = [sds(z.shape, f32) for z in (gu_a, dd_a, o_a, ig)]
    return pl.pallas_call(
        finish_body,
        out_shape=tuple(sums) + (
            sds(res.shape, res.dtype), sds((2, part, kw // 2), f32), sds((1, part), f32), sds((1, part), f32),
            sds((CTX, part), f32), sds((CTX, part), f32),
        ),
        in_specs=anywhere(9) + vmem(2),
        out_specs=tuple(anywhere(5) + vmem(5)),
        scratch_shapes=[VM(z.shape, z.dtype) for z in held] + [VM(z.shape, f32) for z in sums]
        + [DMA((20, 3)), DMA((20,))],
        compiler_params=params(),
        cost_estimate=cost(9),
    )(*args, kvw, minor)


def local(
    tokens, norm_in, norm_mid, router_att, router_mlp, kv_weight, query_weight, output_weight,
    gate_up_weight, down_weight, routes_att, routes_mlp, cotangent,
):
    count_rows, width = tokens.shape[1:]
    capacity = count_rows * 2 // CTX
    local_width = query_weight.shape[2]
    tokens, cotangent = tokens[0], cotangent[0]
    q_own, o_own, down_own = query_weight[0], output_weight[0], down_weight[0]
    gu_own = gate_up_weight[0].transpose(0, 2, 1)
    routes_att, routes_mlp = routes_att[0].T, routes_mlp[0].T
    norm_in, norm_mid = norm_in[None], norm_mid[None]
    router_att, router_mlp = router_att.T, router_mlp.T
    hidden_count = gu_own.shape[1]
    unit = hidden_count // 44
    plan = {"down": (18 * unit, 18 * unit), "dd": (4, 5, 2), "gu": 8 * unit}
    pieces = (8, 4, 4, 2, 4, 0, 0)

    (
        positions, info, queries, attended, log_totals, ret_att,
        rows_att, kv_seq, kv_full, lowered, pick_att, pick_mlp, rows_g, q_oth, o_oth, gu_oth,
    ) = front(
        norm_in, router_att, routes_att, routes_mlp, kv_weight, tokens, cotangent, q_own, o_own, gu_own,
        capacity, (19, 22), 1,
    )
    kv_seq = kv_seq.reshape(-1, 2 * local_width)
    (
        att_picked, hidden, gates_mlp, grad_hidden, norm_mid_grad, router_mlp_grad, grad_proj, p_mlp, gu_sent,
        gu_grad, dd_grad, dd_got, gu_got_0,
    ) = mid(
        plan, ret_att, info, routes_mlp, norm_mid, router_mlp, pick_att, pick_mlp, tokens, cotangent,
        rows_g, gu_own, gu_oth, down_own, 3,
    )
    o_grad, q_grad, kvw_grad, result, input_grad, minor, gu_got, o_got, q_sent = back(
        (queries, positions, attended, log_totals, hidden, gates_mlp, att_picked, grad_hidden, info, routes_att,
         norm_in, router_att, norm_mid_grad, router_mlp_grad),
        (grad_proj, rows_att, kv_seq, p_mlp, q_own, q_oth, o_own, o_oth, kv_full.reshape(width, 2 * local_width),
         lowered, pick_att, pick_mlp, tokens, gu_sent),
        pieces, hidden_count - plan["gu"], count_rows, capacity, 4,
    )
    q_got = lax.ppermute(q_sent, "fsdp", [(0, 1), (1, 0)])
    gu_all, dd_all, o_all, input_grad, result, kvw_grad, n_in, n_mid, r_att, r_mlp = finish(
        gu_grad, gu_got_0, gu_got, dd_grad, dd_got, o_grad, o_got, input_grad, result, kvw_grad, minor
    )
    return (
        result[None], input_grad[None], n_in[0], n_mid[0], r_att.T, r_mlp.T, kvw_grad, (q_grad.astype(f32) + q_got.astype(f32))[None], o_all[None],
        gu_all.transpose(0, 2, 1)[None], dd_all[None],
    )


def solution(mesh):
    placed = (
        P("fsdp", "ctx", None), P(), P(), P(), P(),
        P(None, ("fsdp", "ctx"), "tp"), P("ctx", "fsdp", "tp"), P("ctx", "tp", "fsdp"),
        P("ctx", None, "fsdp", "tp"), P("ctx", "tp", "fsdp"),
        P("fsdp", "ctx", None), P("fsdp", "ctx", None), P("fsdp", "ctx", None),
    )
    return jax.shard_map(
        local,
        mesh=mesh,
        in_specs=placed,
        out_specs=(
            P("fsdp", "ctx", None), P("fsdp", "ctx", None), P(("fsdp", "ctx")), P(("fsdp", "ctx")),
            P(("fsdp", "ctx"), None), P(("fsdp", "ctx"), None), P(None, ("fsdp", "ctx"), "tp"),
            P("ctx", "fsdp", "tp"), P("ctx", "tp", "fsdp"), P("ctx", None, "fsdp", "tp"), P("ctx", "tp", "fsdp"),
        ),
        check_vma=False,
    )
```

```python
from functools import partial

import jax
import jax.numpy as jnp
from jax import lax
from jax.experimental import pallas as pl
from jax.experimental.pallas import tpu as pltpu
from jax.sharding import PartitionSpec as P

MESH = pl.DeviceIdType.MESH
HD = 128
CTX = 8
TP = 8
FSDP = 2
VLIM = 61 * 1024 * 1024
epsilon = 1e-06
masked_score = -1e30
f32 = jnp.float32
bf16 = jnp.bfloat16
DMA = pltpu.SemaphoreType.DMA
VM = pltpu.VMEM


def vmem(n):
    return [pl.BlockSpec(memory_space=pltpu.VMEM)] * n


def anywhere(n):
    return [pl.BlockSpec(memory_space=pl.ANY)] * n


def params(cid=None):
    if cid is None:
        return pltpu.CompilerParams(vmem_limit_bytes=VLIM)
    return pltpu.CompilerParams(collective_id=cid, has_side_effects=True, vmem_limit_bytes=VLIM)


def cost(us):
    return pl.CostEstimate(flops=0, bytes_accessed=int(us * 3.2e6), transcendentals=0)


def sds(shape, dtype):
    return jax.ShapeDtypeStruct(shape, dtype)


def nt(a, b):
    return lax.dot_general(a, b, (((1,), (1,)), ((), ())), preferred_element_type=f32)


def tn(a, b):
    return lax.dot_general(a, b, (((0,), (0,)), ((), ())), preferred_element_type=f32)


def nn(a, b):
    return jnp.dot(a, b, preferred_element_type=f32)


def wide(v):
    return v.astype(f32)


class Place:
    def __init__(self):
        self.f, self.c, self.t = lax.axis_index("fsdp"), lax.axis_index("ctx"), lax.axis_index("tp")
        self.x, self.k = self.t // 2, lax.rem(self.t, 2)
        self.xl, self.xr, self.xo = (lax.rem(self.x + i, 4) for i in (3, 1, 2))
        self.right, self.left = {"tp": self.xr * 2 + self.k}, {"tp": self.xl * 2 + self.k}
        self.sib = {"tp": self.x * 2 + 1 - self.k}
        self.zh, self.y = self.c // 4, lax.rem(self.c, 4)
        self.z = self.zh * 2 + self.f
        self.up, self.down = ({"ctx": self.zh * 4 + lax.rem(self.y + i, 4)} for i in (1, 3))
        self.across = {"ctx": lax.rem(self.c + 4, CTX)}
        self.partner = {"fsdp": 1 - self.f}
        self.above, self.below = (self.at_z(lax.rem(self.z + i, 4)) for i in (1, 3))

    def at_z(self, z):
        return {"fsdp": lax.rem(z, 2), "ctx": (z // 2) * 4 + self.y}

    def ctx_peers(self):
        return [{"ctx": lax.rem(self.c + j, CTX)} for j in range(1, CTX)]

    def tp_near(self):
        return [self.right, self.left, self.sib]

    def z_near(self):
        return [self.above, self.below]


def greet(peers):
    barrier = pltpu.get_barrier_semaphore()
    for axes in peers:
        pl.semaphore_signal(barrier, inc=1, device_id=axes, device_id_type=MESH)
    pl.semaphore_wait(barrier, len(peers))


def all_peers(at):
    me = at.f * CTX + at.c
    out = []
    for j in range(1, FSDP * CTX):
        p = lax.rem(me + j, FSDP * CTX)
        out.append({"fsdp": p // CTX, "ctx": lax.rem(p, CTX)})
    return out


def tp_peers(at):
    return [{"tp": lax.rem(at.t + j, TP)} for j in range(1, TP)]


class Net:
    def __init__(self, send, recv, base=0):
        self.send, self.recv, self.used, self.open = send, recv, base, []

    def go(self, src, dst, axes):
        i = self.used
        self.used += 1
        d = pltpu.make_async_remote_copy(
            src_ref=src, dst_ref=dst, send_sem=self.send.at[i], recv_sem=self.recv.at[i],
            device_id=axes, device_id_type=MESH,
        )
        d.start()
        self.open.append(d)
        return d

    def drain(self):
        for d in self.open:
            d.wait_send()
        self.open = []


class Ring:
    def __init__(self, net, view, me, plus, minus):
        self.net, self.view, self.plus, self.minus = net, view, plus, minus
        self.me, self.low, self.high, self.far = me, lax.rem(me + 3, 4), lax.rem(me + 1, 4), lax.rem(me + 2, 4)

    def hop1(self, src=None):
        src = self.view(self.me, None) if src is None else src
        self.a = self.net.go(src, self.view(self.me, None), self.plus)
        self.b = self.net.go(src, self.view(self.me, None), self.minus)

    def hop2_low(self):
        self.a.wait_recv()
        self.a = self.net.go(self.view(self.low, 0), self.view(self.low, 0), self.plus)

    def hop2_high(self):
        self.b.wait_recv()
        self.b = self.net.go(self.view(self.high, 1), self.view(self.high, 1), self.minus)

    def hop2(self):
        self.hop2_low()
        self.hop2_high()

    def hop3(self):
        self.a.wait_recv()
        self.b.wait_recv()


class RingSum:
    def __init__(self, net, own, stage, land, me, plus, minus):
        self.net, self.own, self.stage, self.land, self.plus, self.minus = net, own, stage, land, plus, minus
        self.me, self.low, self.high, self.far = me, lax.rem(me + 3, 4), lax.rem(me + 1, 4), lax.rem(me + 2, 4)

    def put(self, position, part, value):
        r = self.stage(position, part)
        r[...] = value.astype(r.dtype)
        return r

    def hop1(self):
        self.a = self.net.go(self.put(self.far, 0, self.own(self.far, 0)), self.land("a"), self.plus)
        self.b = self.net.go(self.put(self.far, 1, self.own(self.far, 1)), self.land("b"), self.minus)

    def hop2(self):
        self.a.wait_recv()
        self.put(self.high, 0, self.own(self.high, 0) + wide(self.land("a")[...]))
        self.put(self.high, 1, self.own(self.high, 1))
        self.a = self.net.go(self.stage(self.high, None), self.land("l"), self.plus)
        self.b.wait_recv()
        self.put(self.low, 1, self.own(self.low, 1) + wide(self.land("b")[...]))
        self.put(self.low, 0, self.own(self.low, 0))
        self.b = self.net.go(self.stage(self.low, None), self.land("r"), self.minus)

    def hop3(self):
        self.a.wait_recv()
        self.b.wait_recv()
        return self.own(self.me, None) + wide(self.land("l")[...]) + wide(self.land("r")[...])


class Feeder:
    def __init__(self, net, partner, items):
        self.net, self.partner, self.moves, self.queue = net, partner, [], []
        for src, dst, axis, first, rows, unit in items:
            self.queue += [(src, dst, axis, first, lo, min(unit, rows - lo)) for lo in range(0, rows, unit)]

    def feed(self, count):
        for src, dst, axis, first, lo, size in self.queue[:count]:
            s, d = pl.ds(first + lo, size), pl.ds(lo, size)
            a, b = (src.at[s], dst.at[d]) if axis == 0 else (src.at[:, s], dst.at[:, d])
            self.moves.append(self.net.go(a, b, self.partner))
        self.queue = self.queue[count:]

    def finish(self):
        assert not self.queue
        for m in self.moves:
            m.wait_recv()


class Local:
    def __init__(self, sem):
        self.sem, self.used = sem, 0

    def go(self, src, dst):
        d = pltpu.make_async_copy(src, dst, self.sem.at[self.used])
        self.used += 1
        d.start()
        return d


def part_of(part, size):
    half = size // 2
    return pl.ds(0, size) if part is None else pl.ds(part * half, half)


class Dispatch:
    def __init__(self, net, at, x_ref, o_ref, exchange=True):
        self.net, self.at, self.x_ref, self.o_ref, self.exchange = net, at, x_ref, o_ref, exchange
        self.n, self.rows, self.w = x_ref.shape

    def view(self, block, tt, part=None):
        half = self.rows // 2
        lo, size = (0, self.rows) if part is None else (part * half, half)
        row = pl.multiple_of(block * self.rows + lo, 16)
        return self.o_ref.at[pl.ds(row, size), pl.ds(pl.multiple_of(tt * self.w, self.w), self.w)]

    def start(self):
        c, n = self.at.c, self.n
        if self.exchange:
            self.blocks = [lax.rem(c + n - j, n) for j in range(n)]
            self.moves = [None]
            for j in range(1, n):
                e = lax.rem(c + j, n)
                self.moves.append(self.net.go(self.x_ref.at[e], self.view(c, self.at.t), {"ctx": e}))
            self.view(c, self.at.t)[...] = self.x_ref[c]
        else:
            self.blocks, self.moves = list(range(n)), [None] * n
            for j in range(n):
                self.view(j, self.at.t)[...] = self.x_ref[j]

    def sibling(self, b, tt):
        return self.net.go(self.view(b, tt), self.view(b, tt), self.at.sib)

    def hop1(self):
        at = self.at
        self.rings, self.sibs = [], []
        for b, move in zip(self.blocks, self.moves):
            if move is not None:
                move.wait_recv()
            ring = Ring(self.net, lambda xx, part, b=b: self.view(b, xx * 2 + at.k, part), at.x, at.right, at.left)
            ring.hop1()
            self.rings.append(ring)
            self.sibs.append(self.sibling(b, at.t))

    def hop2(self):
        at = self.at
        for b, ring in zip(self.blocks, self.rings):
            ring.hop2_low()
            self.sibs.append(self.sibling(b, at.xl * 2 + at.k))
            ring.hop2_high()
            self.sibs.append(self.sibling(b, at.xr * 2 + at.k))

    def hop3(self):
        at = self.at
        for b, ring in zip(self.blocks, self.rings):
            ring.hop3()
            self.sibs.append(self.sibling(b, at.xo * 2 + at.k))

    def finish(self):
        for s in self.sibs:
            s.wait_recv()

    COPIES = 8 * 9 + 7


class Collect:
    def __init__(
        self, net, at, p_ref, o_ref, sibbuf, abuf, bbuf, lbuf, rbuf, fbuf, exchange=True, home_net=None, total=None
    ):
        self.net, self.at, self.p, self.o, self.exchange = net, at, p_ref, o_ref, exchange
        self.home_net = net if home_net in (None, "late") else home_net
        self.total = fbuf.at[at.x] if total is None else total
        self.sibbuf, self.fbuf = sibbuf, fbuf
        self.lands = {"a": abuf, "b": bbuf, "l": lbuf, "r": rbuf}
        _, _, self.n, self.rows, self.w = p_ref.shape
        n, c = self.n, at.c
        self.late = home_net == "late"
        self.blocks = [lax.rem(c + j, n) for j in range(1, n)] + [c] if exchange and not self.late else list(range(n))
        self.sibs, self.rings, self.moves = [None] * n, [None] * n, []

    def start(self, which=None):
        at = self.at
        for j in range(self.n) if which is None else which:
            b = self.blocks[j]
            self.sibs[j] = self.net.go(self.p.at[1 - at.k, :, b], self.sibbuf.at[:, b], at.sib)

    def own(self, b, xx, part):
        s = part_of(part, self.rows)
        return wide(self.p[self.at.k, xx, b, s]) + wide(self.sibbuf[xx, b, s])

    def hop1(self, which=None):
        at = self.at
        for j in range(self.n) if which is None else which:
            b = self.blocks[j]
            self.sibs[j].wait_recv()
            ring = RingSum(
                self.net,
                partial(self.own, b),
                lambda xx, part, b=b: self.fbuf.at[xx, b, part_of(part, self.rows)],
                lambda name, b=b: self.lands[name].at[b],
                at.x, at.right, at.left,
            )
            ring.hop1()
            self.rings[j] = ring

    def hop2(self, which=None):
        for j in range(self.n) if which is None else which:
            self.rings[j].hop2()

    def hop3(self, which=None):
        for j in range(self.n) if which is None else which:
            b = self.blocks[j]
            total = self.rings[j].hop3()
            if self.late:
                self.total[b] = total.astype(self.fbuf.dtype)
            elif self.exchange and j < self.n - 1:
                self.total[b] = total.astype(self.fbuf.dtype)
                self.to_home(b)
            else:
                self.o[b, pl.ds(0, self.rows)] = total.astype(self.o.dtype)

    def to_home(self, b):
        home = self.o.at[self.at.c, pl.ds(0, self.rows)]
        self.moves.append(self.home_net.go(self.total.at[b], home, {"ctx": b}))

    def all_home(self):
        c, n = self.at.c, self.n
        for j in range(1, n):
            self.to_home(lax.rem(c + j, n))
        self.o[c, pl.ds(0, self.rows)] = self.total[c]

    def finish(self):
        for m in self.moves:
            m.wait_recv()

    COPIES = 8 * 5 + 7

    @staticmethod
    def scratch(n, rows, w):
        return [
            VM((4, n, rows, w), bf16), VM((n, rows // 2, w), bf16), VM((n, rows // 2, w), bf16),
            VM((n, rows, w), bf16), VM((n, rows, w), bf16), VM((4, n, rows, w), bf16),
        ]


def sems(n):
    return [DMA((n,)), DMA((n,))]


def exact(a, b):
    return jnp.dot(a, b, preferred_element_type=f32, precision=lax.Precision.HIGHEST)


def split3(v):
    high = v.astype(bf16)
    rest = v - wide(high)
    mid = rest.astype(bf16)
    return high, mid, (rest - wide(mid)).astype(bf16)


def three_rows(v):
    high, mid, low = split3(v)
    row = lax.broadcasted_iota(jnp.int32, (8, v.shape[1]), 0)
    pieces = jnp.where(row == 0, wide(high), jnp.where(row == 1, wide(mid), jnp.where(row == 2, wide(low), 0.0)))
    return pieces.astype(bf16)


def to_row_form(columns, rows):
    return columns.T[:rows]


def to_column_form(rows):
    fill = jnp.zeros((128 - rows.shape[0], rows.shape[1]), f32)
    return jnp.concatenate([rows, fill], axis=0).T


def route_columns(routes):
    row = lax.broadcasted_iota(jnp.int32, (8, routes.shape[1]), 0)
    both = jnp.where(row == 0, routes[0:1, :], jnp.where(row == 1, routes[1:2, :], 0)).astype(f32)
    columns = to_column_form(both)
    return columns[:, 0:1], columns[:, 1:2]


FIRST = 8


def hot_lanes(routes):
    lane = lax.broadcasted_iota(jnp.int32, (routes.shape[1], 128), 1).astype(f32)
    return [(lane == r + FIRST).astype(f32) for r in route_columns(routes)]


def pick_matrix(routes, cap):
    tok = routes.shape[1]
    lane = lax.broadcasted_iota(jnp.int32, (tok, 128), 1).astype(f32)
    columns = route_columns(routes)
    hot = [(lane == r).astype(f32) for r in columns]
    row = lax.broadcasted_iota(jnp.int32, (tok, tok), 0)
    col = lax.broadcasted_iota(jnp.int32, (tok, tok), 1)
    earlier = (col < row).astype(f32).astype(bf16)
    before = nn(earlier, (hot[0] + hot[1]).astype(bf16))
    slot = lax.broadcasted_iota(jnp.int32, (tok, CTX * 128), 1).astype(f32)
    out = []
    for r, o in zip(columns, hot):
        place = jnp.sum(before * o, axis=1, keepdims=True)
        target = jnp.where(place < cap, r * 128 + place, -1.0)
        out.append((slot == target).astype(f32).astype(bf16))
    return out


def pair_positions(pos_ref, g, cap):
    a, b = wide(pos_ref[2 * g]), wide(pos_ref[2 * g + 1])
    none = jnp.zeros_like(a)
    lane = lax.broadcasted_iota(jnp.int32, (a.shape[0], 256), 1)
    a = jnp.concatenate([a, none], axis=1)
    b = pltpu.roll(jnp.concatenate([b, none], axis=1), cap, 1)
    return jnp.where(lane < cap, a, b)[0:1, : 2 * cap].astype(jnp.int32)


def assemble(own, other, full, axis, f, local):
    size = own.shape[axis]
    out = []
    for src, place in ((own, f), (other, 1 - f)):
        span = pl.ds(pl.multiple_of(place * size, size), size)
        out.append(local.go(src, full.at[span] if axis == 0 else full.at[:, span]))
    return out


def front_body(
    feeds, norm_in, router_t, routes_att, routes_mlp, kv_w, tokens, cot, q_own, o_own, gu_own,
    pos_out, info, q_ref, att_ref, lse_ref, home,
    rows_out, seq_out, full_out, lowered_out, pick_att_out, pick_mlp_out, g_out, q_oth, o_oth, gu_oth,
    toks, cots, rows_att, kv_seq, kv_full, lowered, pick_att, pick_mlp, slots_att, slots_g, pos,
    rows_g, p_ref, wq, wo, vt_ref, b_sib, b_a, b_b, b_l, b_r, b_f, total_ref, local_sem, send, recv,
):
    at, net, local = Place(), Net(send, recv), Local(local_sem)
    unit = gu_own.shape[1] // 44
    feeder = Feeder(net, at.partner, [(gu_own, gu_oth, 1, 0, gu_oth.shape[1], unit)])
    tok, width = tokens.shape
    kv_part, w = kv_w.shape[1:]
    cap, part = slots_att.shape[1:]
    mine = pl.ds(pl.multiple_of(at.t * part, part), part)
    load_t = local.go(tokens, toks)
    load_c = local.go(cot.at[:, mine], cots)

    def kvw(z, y, p):
        return kv_full.at[lax.rem(z, 2) * CTX + (z // 2) * 4 + y, part_of(p, kv_part)]

    own = kvw(at.z, at.y, None)
    for h in range(w // HD):
        for j in range(2):
            own[:, (2 * h + j) * HD : (2 * h + j + 1) * HD] = kv_w[j, :, h * HD : (h + 1) * HD]
    greet(at.ctx_peers() + at.tp_near() + at.z_near())
    zring = Ring(net, lambda z, p: kvw(z, at.y, p), at.z, at.above, at.below)
    zring.hop1()
    yrings = []

    def y_stage(z):
        ring = Ring(net, lambda y, p: kvw(z, y, p), at.y, at.up, at.down)
        ring.hop1()
        yrings.append(ring)

    y_stage(at.z)
    load_t.wait()
    x = wide(toks[...])
    scale = lax.rsqrt(jnp.sum(x * x, axis=1, keepdims=True) / width + epsilon)
    lowered[...] = (x * scale * norm_in[...]).astype(bf16)
    zring.hop2()
    y_stage(zring.low)
    y_stage(zring.high)
    for i, r in enumerate(pick_matrix(routes_att[...], cap)):
        pick_att[i * tok : (i + 1) * tok, :] = r
    both = pick_att[:tok, :] + pick_att[tok:, :]
    slots = tn(both, lowered[:, mine]).astype(bf16)
    for e in range(CTX):
        slots_att[e] = slots[e * 128 : e * 128 + cap]
    d_att = Dispatch(net, at, slots_att, rows_att)
    d_att.start()
    zring.hop3()
    y_stage(zring.far)
    number = lax.broadcasted_iota(jnp.int32, (8, tok), 1)
    row = lax.broadcasted_iota(jnp.int32, (8, tok), 0)
    digits = jnp.where(row == 0, number // 16, jnp.where(row == 1, lax.rem(number, 16), 0)).astype(f32).astype(bf16)
    found = nn(digits, both)
    found = (found[0:1] * 16.0 + found[1:2]).astype(jnp.int32) + at.c * tok
    for e in range(CTX):
        pos[e] = jnp.broadcast_to(found[:, e * 128 : (e + 1) * 128], (8, 128))
    moves = []
    for j in range(1, CTX):
        e = lax.rem(at.c + j, CTX)
        moves.append(net.go(pos.at[e], pos_out.at[at.c], {"ctx": e}))
    pos_out[at.c] = pos[at.c]
    q_move = net.go(q_own, q_oth, at.partner)
    saves = [local.go(lowered, lowered_out), local.go(pick_att, pick_att_out)]
    for ring in yrings[:3]:
        ring.hop2()
    d_att.hop1()
    yrings[3].hop2()
    for i, r in enumerate(pick_matrix(routes_mlp[...], cap)):
        pick_mlp[i * tok : (i + 1) * tok, :] = r
    load_c.wait()
    slots = tn(pick_mlp[:tok, :] + pick_mlp[tok:, :], cots[...]).astype(bf16)
    for e in range(CTX):
        slots_g[e] = slots[e * 128 : e * 128 + cap]
    saves.append(local.go(pick_mlp, pick_mlp_out))
    for ring in yrings:
        ring.hop3()
    weights = kv_full[...].reshape(-1, 2 * w)
    kv_seq[at.c] = nn(lowered[...], weights).astype(bf16)
    over = net.go(kv_seq.at[at.c], kv_seq.at[at.c], at.across)

    def seq_ring(zh):
        return Ring(net, lambda y, p: kv_seq.at[zh * 4 + y, part_of(p, tok)], at.y, at.up, at.down)

    near, far = seq_ring(at.zh), seq_ring(1 - at.zh)
    near.hop1()
    o_move = net.go(o_own, o_oth, at.partner)
    feeder.feed(feeds[0])
    saves.append(local.go(kv_full, full_out))
    d_att.hop2()
    logits = sum(nt(r, lowered[...]) for r in split3(router_t[...]))
    columns = to_column_form(jnp.concatenate([jnp.zeros_like(logits), logits], axis=0))
    hot = hot_lanes(routes_att[...])
    low = [jnp.sum(o * columns, axis=1, keepdims=True) for o in hot]
    lane = lax.broadcasted_iota(jnp.int32, (tok, 128), 1)
    g0 = 1.0 / (1.0 + jnp.exp(low[1] - low[0]))
    g1 = 1.0 / (1.0 + jnp.exp(low[0] - low[1]))
    info[...] = jnp.where(
        lane == 0, scale, jnp.where(lane == 1, g0, jnp.where(lane == 2, g1, columns / scale))
    )
    d_att.hop3()
    over.wait_recv()
    far.hop1()
    d_att.finish()
    saves.append(local.go(rows_att, rows_out))
    q_move.wait_recv()
    load_q = assemble(q_own, q_oth, wq, 0, at.f, local)
    near.hop2()
    o_move.wait_recv()
    load_o = assemble(o_own, o_oth, wo, 1, at.f, local)
    for d in load_q:
        d.wait()
    q_ref[...] = nn(rows_att[...], wq[...]).astype(bf16)
    near.hop3()
    far.hop2()
    d_g = Dispatch(net, at, slots_g, rows_g)
    d_g.start()
    feeder.feed(feeds[1])
    for m in moves:
        m.wait_recv()
    far.hop3()
    saves.append(local.go(kv_seq, seq_out))

    heads = q_ref.shape[1] // HD
    width = heads * HD
    scale = HD ** (-0.5)
    total = q_ref.shape[0]
    length = kv_seq.shape[0] * tok
    for h in range(heads):
        vt_ref[h] = kv_seq[:, :, (2 * h + 1) * HD : (2 * h + 2) * HD].reshape(length, HD).T
    for d in load_o:
        d.wait()
    col = Collect(net, at, p_ref, home, b_sib, b_a, b_b, b_l, b_r, b_f, home_net="late", total=total_ref)
    rows_at, keys_at = 2 * cap, 2 * tok
    pair = lambda g: [2 * g, 2 * g + 1]
    for step, g in enumerate(reversed(range(total // rows_at))):
        lo = g * rows_at
        extent = (g + 1) * keys_at
        at_key = extent - keys_at
        pos = pair_positions(pos_out, g, cap)
        for h in range(heads):
            cols = slice(h * HD, (h + 1) * HD)
            s = nt(kv_seq[: extent // tok, :, 2 * h * HD : (2 * h + 1) * HD].reshape(extent, HD), q_ref[lo : lo + rows_at, cols]) * scale
            ids = lax.broadcasted_iota(jnp.int32, (keys_at, rows_at), 0) + at_key
            last = jnp.where(ids <= pos, s[at_key:], masked_score)
            highest = jnp.max(last, axis=0, keepdims=True)
            if g:
                highest = jnp.maximum(highest, jnp.max(s[:at_key], axis=0, keepdims=True))
            e_last = jnp.exp(last - highest)
            sums = jnp.sum(e_last, axis=0, keepdims=True)
            mixed = nn(vt_ref[h, :, at_key:extent], e_last.astype(bf16))
            if g:
                e = jnp.exp(s[:at_key] - highest)
                sums = sums + jnp.sum(e, axis=0, keepdims=True)
                mixed = mixed + nn(vt_ref[h, :, :at_key], e.astype(bf16))
            att_ref[lo : lo + rows_at, cols] = (mixed / sums).T.astype(bf16)
            lse_ref[h : h + 1, lo : lo + rows_at] = highest + jnp.log(sums)
        out = nn(att_ref[lo : lo + rows_at, :], wo[...]).astype(bf16)
        for i in range(TP):
            for b in range(2):
                p_ref[i % 2, i // 2, 2 * g + b] = out[b * cap : (b + 1) * cap, i * width : (i + 1) * width]
        col.start(pair(g))
        if step == 0:
            d_g.hop1()
        if step == 2:
            d_g.hop2()
        if step >= 1:
            col.hop1(pair(g + 1))
        if step >= 2:
            col.hop2(pair(g + 2))
        if step >= 3:
            col.hop3(pair(g + 3))
    col.hop1(pair(0))
    col.hop2(pair(1))
    col.hop3(pair(2))
    col.hop2(pair(0))
    col.hop3(pair(1))
    d_g.hop3()
    d_g.finish()
    saves.append(local.go(rows_g, g_out))
    col.hop3(pair(0))
    col.all_home()
    feeder.feed(100)
    for d in saves:
        d.wait()
    col.finish()
    feeder.finish()
    net.drain()


def front(norm_in, router_t, routes_att, routes_mlp, kv_w, tokens, cot, q_own, o_own, gu_own, cap, feeds, gu_rows, cid):
    tok, width = tokens.shape
    part = width // TP
    _, kv_part, w = kv_w.shape
    heads = w // HD
    slots = CTX * cap
    block = (CTX, cap, part)
    large = [(slots, width), (CTX, tok, 2 * w), (FSDP * CTX, kv_part, 2 * w), (tok, width)]
    large += [(2 * tok, CTX * 128)] * 2
    out = [
        sds((CTX, 8, 128), jnp.int32), sds((tok, 128), f32), sds((slots, w), bf16), sds((slots, w), bf16),
        sds((heads, slots), f32), sds(block, bf16),
    ]
    out += [sds(z, bf16) for z in large + [(slots, width)]]
    out += [sds(q_own.shape, bf16), sds(o_own.shape, bf16), sds((2, gu_rows, gu_own.shape[2]), bf16)]
    return pl.pallas_call(
        partial(front_body, feeds),
        out_shape=tuple(out),
        in_specs=vmem(5) + anywhere(5),
        out_specs=tuple(vmem(6) + anywhere(10)),
        scratch_shapes=[VM((tok, width), bf16), VM((tok, part), bf16)] + [VM(z, bf16) for z in large]
        + [
            VM(block, bf16), VM(block, bf16), VM((CTX, 8, 128), jnp.int32), VM((slots, width), bf16),
            VM((2, 4) + block, bf16), VM((width, w), bf16), VM((w, width), bf16), VM((heads, HD, CTX * tok), bf16),
        ]
        + Collect.scratch(*block) + [VM(block, bf16), DMA((16,))]
        + sems(2 * Dispatch.COPIES + Collect.COPIES + 120),
        compiler_params=params(cid),
        cost_estimate=cost(120),
    )(norm_in, router_t, routes_att, routes_mlp, kv_w, tokens, cot, q_own, o_own, gu_own)


def mid_body(
    plan,
    ret_att, info, routes, norm_mid_full, router_full, pick_att_any, pick_mlp_any, tokens, cot, rows_g, gu_own, gu_oth,
    down_own,
    att_picked, hidden, gates_out, grad_hidden, norm_grad, router_grad,
    proj_out, p1_out, gu_sent_out, gu_grad, dd_grad, dd_got, gu_got,
    pick_att, pick_mlp, grad_proj, p1, gu_sent, dd_sent,
    ret, b1_sib, b1_a, b1_b, b1_l, b1_r, fbuf,
    x_slots, X, G, W, D, gun, U, GG, GU, trans, p2, lm, small_out, small_in, small2_out, small2_in,
    sums_ref, gs_out, gs_in, sgm, sg_out, sg_in, sg_tot, sg_home, stage, toks, cots, mid_total, local_sem, stage_sem, send, recv,
):
    at, net = Place(), Net(send, recv)
    tok, part = lm.shape
    ff = down_own.shape[0]
    half = down_own.shape[1]
    cap = x_slots.shape[1]
    pad = W.shape[1] - ff
    mine = pl.ds(pl.multiple_of(at.f * half, half), half)
    other = pl.ds(pl.multiple_of((1 - at.f) * half, half), half)
    near = tp_peers(at)
    ret[...] = jnp.zeros_like(ret)
    for e in range(CTX):
        ret[0, e, : ret_att.shape[1], :] = ret_att[e]
    local = Local(local_sem)
    load = local.go
    load_a, load_m = load(pick_att_any, pick_att), load(pick_mlp_any, pick_mlp)
    here = pl.ds(pl.multiple_of(at.t * part, part), part)
    load_s = [load(tokens.at[:, here], toks), load(cot.at[:, here], cots)]
    load_g = load(rows_g, G)
    load_d = load(down_own, D.at[pl.ds(0, ff), mine])
    load_w = [
        load(gu_own, W.at[:, pl.ds(0, ff), mine]),
        load(gu_oth, W.at[:, pl.ds(0, gu_oth.shape[1]), other]),
    ]
    greet(at.ctx_peers() + near + [at.partner])

    def down_piece(lo, hi):
        s = pl.ds(lo, hi - lo)
        return net.go(down_own.at[s], D.at[s, mine], at.partner)

    d_cut = plan["down"]
    down_moves = [down_piece(0, d_cut[0])]
    W[:, ff:, :] = jnp.zeros_like(W[:, ff:, :])
    D[ff:, :] = jnp.zeros_like(D[ff:, :])
    lane = lax.broadcasted_iota(jnp.int32, (tok, 128), 1)
    hot = hot_lanes(routes[...])
    ga = [info[:, k : k + 1] for k in (1, 2)]
    norm = norm_mid_full[0:1, here]
    router_t = router_full[:, here]
    router = jnp.concatenate([jnp.zeros((FIRST, part), f32), router_t, jnp.zeros((128 - FIRST - CTX, part), f32)]).T
    for d in load_s + [load_a, load_m]:
        d.wait()
    picked = nn(pick_att[...], ret[0].reshape(-1, part))
    att_picked[...] = picked.astype(bf16)
    h = wide(toks[...]) + ga[0] * picked[:tok] + ga[1] * picked[tok:]
    hidden[...] = h
    raw = exact(h * norm, router)
    sums = jnp.where(lane == 0, jnp.sum(h * h, axis=1, keepdims=True), raw)
    small_out[...] = to_row_form(sums, 16)
    moves = [net.go(small_out, small_in.at[j], p) for j, p in enumerate(near)]
    total = small_out[...]
    for j, m in enumerate(moves):
        m.wait_recv()
        total = total + small_in[j]
    sums = to_column_form(total)
    scale = lax.rsqrt(sums[:, 0:1] / (part * TP) + epsilon)
    low = [jnp.sum(o * sums, axis=1, keepdims=True) * scale for o in hot]
    g0 = 1.0 / (1.0 + jnp.exp(low[1] - low[0]))
    g1 = 1.0 / (1.0 + jnp.exp(low[0] - low[1]))
    gates = jnp.where(lane == 0, g0, jnp.where(lane == 1, g1, jnp.where(lane == 2, scale, 0.0)))
    sums_ref[...] = sums
    gates_out[...] = gates
    lm[...] = (hidden[...] * scale * norm).astype(bf16)
    slots = tn(pick_mlp[:tok, :] + pick_mlp[tok:, :], lm[...]).astype(bf16)
    for e in range(CTX):
        x_slots[e] = slots[e * 128 : e * 128 + cap]
    d1 = Dispatch(net, at, x_slots, X)
    d1.start()
    rows2 = to_row_form(gates, 2)
    pair_row = jnp.concatenate([rows2[0:1], rows2[1:2]], axis=1)
    slot_gates = jnp.sum(nn(three_rows(pair_row), pick_mlp[...]), axis=0, keepdims=True)
    for e in range(CTX):
        gs_out[e] = jnp.broadcast_to(slot_gates[:, e * 128 : (e + 1) * 128], (8, 128))
    gs_moves = [net.go(gs_out.at[p["ctx"]], gs_in.at[at.c], p) for p in at.ctx_peers()]
    gs_in[at.c] = gs_out[at.c]
    down_moves.append(down_piece(d_cut[1], ff))
    rest = pl.ds(gu_oth.shape[1], ff - gu_oth.shape[1])
    gu_move = net.go(gu_own.at[:, rest], W.at[:, rest, mine], at.partner)
    d1.hop1()
    for m in gs_moves:
        m.wait_recv()
    load_g.wait()
    for b in range(CTX):
        column = gs_in[b].T[:cap, 0:1]
        s = slice(b * cap, (b + 1) * cap)
        G[s, :] = (wide(G[s, :]) * column).astype(bf16)
    d1.hop2()
    load_d.wait()
    for m in down_moves:
        m.wait_recv()
    rows_at = 2 * cap
    groups = CTX // 2

    def group_rows(g):
        return pl.ds(pl.multiple_of(g * rows_at, rows_at), rows_at)

    @pl.loop(0, groups)
    def _(g):
        s = group_rows(g)
        gun[s, :] = nt(G[s, :], D[...])

    d1.hop3()
    d1.finish()
    for m in load_w:
        m.wait()
    gu_move.wait_recv()
    sgm[...] = jnp.zeros_like(sgm)

    def put(p_ref, g, out):
        for i in range(TP):
            for b in range(2):
                p_ref[i % 2, i // 2, 2 * g + b] = out[b * cap : (b + 1) * cap, i * part : (i + 1) * part]

    net.drain()
    col2 = Collect(net, at, p2, ret.at[1], b1_sib, b1_a, b1_b, b1_l, b1_r, fbuf, home_net="late", total=mid_total)
    pair = lambda g: [2 * g, 2 * g + 1]
    for g in range(groups):
        s = group_rows(g)
        x = X[s, :]
        gate = nt(x, W[0])
        up = nt(x, W[1])
        sig = 1.0 / (1.0 + jnp.exp(-gate))
        silu = gate * sig
        units = (silu * up).astype(bf16)
        grad = gun[s, :]
        d_gate = (grad * up * (sig * (1.0 + gate * (1.0 - sig)))).astype(bf16)
        d_up = (grad * silu).astype(bf16)
        U[s, :] = units
        GG[s, :] = d_gate
        GU[s, :] = d_up
        column = jnp.sum(wide(units) * grad, axis=1, keepdims=True)
        for b in range(2):
            sgm[2 * g + b, :cap, :] = jnp.broadcast_to(column[b * cap : (b + 1) * cap], (cap, 128))
        put(p2, g, (nn(d_gate, W[0]) + nn(d_up, W[1])).astype(bf16))
        col2.start(pair(g))
        if g >= 1:
            col2.hop1(pair(g - 1))
        if g >= 2:
            col2.hop2(pair(g - 2))
        if g >= 3:
            col2.hop3(pair(g - 3))
    for b in range(CTX):
        sg_out[b] = sgm[b].T[:8]
    sg_moves = [net.go(sg_out, sg_in.at[j], p) for j, p in enumerate(near)]

    saves = []
    cols = stage.shape[2]
    steps = half // cols
    trans[...] = U[...].T

    @pl.loop(0, steps)
    def _(i):
        src = pl.ds(pl.multiple_of((1 - at.f) * half + i * cols, cols), cols)
        dd_sent[:, pl.ds(pl.multiple_of(i * cols, cols), cols)] = nn(trans[...], G[:, src])[:ff].astype(bf16)

    cut = plan["dd"]
    feeder = Feeder(net, at.partner, [(dd_sent, dd_got, 0, 0, ff, ff // 11)])
    rows = gu_got.shape[1]
    gu_feeder = Feeder(net, at.partner, [(gu_sent, gu_got, 1, 0, rows, ff // 22)])
    feeder.feed(cut[0])
    col2.hop1(pair(3))
    col2.hop2(pair(2))
    col2.hop3(pair(1))
    v = sg_out[...]
    for j, m in enumerate(sg_moves):
        m.wait_recv()
        v = v + sg_in[j]
    sg_tot[...] = v
    sg_moves = [net.go(sg_tot.at[p["ctx"]], sg_home.at[at.c], p) for p in at.ctx_peers()]
    sg_home[at.c] = sg_tot[at.c]

    col2.hop2(pair(3))
    col2.hop3(pair(2))

    def own_part(matrix, dst, first):
        out = []
        for i in range(steps):
            slot = (first + i) % 2
            if first + i >= 2:
                stage_copies[first + i - 2].wait()
            src = pl.ds(pl.multiple_of(at.f * half + i * cols, cols), cols)
            stage[slot] = nn(trans[...], matrix[:, src])[:ff].astype(bf16)
            d = pltpu.make_async_copy(stage.at[slot], dst(pl.ds(i * cols, cols)), stage_sem.at[slot])
            d.start()
            stage_copies.append(d)

    stage_copies = []
    col2.hop3(pair(3))
    col2.all_home()
    feeder.feed(cut[1])
    own_part(G, lambda s: dd_grad.at[:, s], 0)
    col2.finish()

    lane = lax.broadcasted_iota(jnp.int32, (tok, 128), 1)
    hot = hot_lanes(routes[...])
    ga = [info[:, k : k + 1] for k in (1, 2)]
    norm = norm_mid_full[0:1, here]
    router_t = router_full[:, here]
    sums = sums_ref[...]
    gates = gates_out[...]
    scale = gates[:, 2:3]
    back = nn(pick_mlp[...], ret[1].reshape(-1, part))
    back = back[:tok] + back[tok:]
    h = hidden[...]
    inner = jnp.sum(back * norm * h, axis=1, keepdims=True)
    small2_out[...] = to_row_form(jnp.where(lane == 0, inner, 0.0), 8)
    moves = [net.go(small2_out, small2_in.at[j], p) for j, p in enumerate(near)]
    for m in sg_moves:
        m.wait_recv()
    row = jnp.concatenate([sg_home[e][0:1] for e in range(CTX)], axis=1)
    pairs = jnp.sum(nt(pick_mlp[...], three_rows(row)), axis=1, keepdims=True)
    sg = [pairs[:tok], pairs[tok:]]
    grad_logits = sum(
        o * (d - gates[:, k : k + 1] * (sg[0] + sg[1])) for k, (o, d) in enumerate(zip(hot, sg))
    )
    grad_low = back
    for e in range(CTX):
        grad_low = grad_low + grad_logits[:, FIRST + e : FIRST + e + 1] * router_t[e : e + 1, :]
    total = small2_out[...]
    for j, m in enumerate(moves):
        m.wait_recv()
        total = total + small2_in[j]
    inner = to_column_form(total)[:, 0:1] + jnp.sum(grad_logits * sums, axis=1, keepdims=True)
    gh = (
        wide(cots[...]) + scale * (grad_low * norm) - h * (scale * scale * scale) * (inner / (part * TP))
    )
    grad_hidden[...] = gh
    pair_rows = jnp.concatenate([(ga[0] * gh).astype(bf16), (ga[1] * gh).astype(bf16)], axis=0)
    slots = tn(pick_att[...], pair_rows).astype(bf16)
    for e in range(CTX):
        x_slots[e] = slots[e * 128 : e * 128 + cap]
    d2 = Dispatch(net, at, x_slots, grad_proj)
    d2.start()
    feeder.feed(cut[2])
    norm_grad[...] = jnp.broadcast_to(jnp.sum(grad_low * h * scale, axis=0, keepdims=True), norm_grad.shape)
    router_grad[...] = sum(tn(g, lm[...]) for g in split3(grad_logits))
    for j, grads in enumerate((GG, GU)):
        trans[...] = grads[...].T

        @pl.loop(0, steps)
        def _(i):
            src = pl.ds(pl.multiple_of((1 - at.f) * half + i * cols, cols), cols)
            gu_sent[j, :, pl.ds(pl.multiple_of(i * cols, cols), cols)] = nn(trans[...], X[:, src])[:ff].astype(bf16)

        if j == 1:
            gu_feeder.feed(100)
        own_part(X, lambda s, j=j: gu_grad.at[j, :, s], (j + 1) * steps)
        if j == 0:
            d2.hop1()
    saves.append(local.go(gu_sent, gu_sent_out))
    d2.hop2()

    @pl.loop(0, groups)
    def _(g):
        s = group_rows(g)
        put(p1, g, nn(U[s, :], D[...]).astype(bf16))

    saves.append(local.go(p1, p1_out))
    d2.hop3()
    d2.finish()
    saves.append(local.go(grad_proj, proj_out))
    for d in saves + stage_copies[-2:]:
        d.wait()
    feeder.finish()
    gu_feeder.finish()
    net.drain()


def mid(
    plan, ret_att, info, routes, norm_mid, router_t, pick_att, pick_mlp, tokens, cot, rows_g, gu_own, gu_oth, down_own, cid,
):
    tok, width = tokens.shape
    part = width // TP
    n, cap, _ = ret_att.shape
    p_shape = (2, 4, n, cap, part)
    slots, width = rows_g.shape
    ff, half = down_own.shape
    ffp = (ff + 255) // 256 * 256
    cols = 256
    bufs = Collect.scratch(n, cap, part)
    vm_out = (
        sds((2 * tok, part), bf16), sds((tok, part), f32), sds((tok, 128), f32), sds((tok, part), f32),
        sds((8, part), f32), sds((128, part), f32),
    )
    any_out = (
        sds((slots, width), bf16), sds(p_shape, bf16), sds((2, ff, half), bf16),
        sds((2, ff, half), bf16), sds((ff, half), bf16), sds((ff, half), bf16), sds((2, plan["gu"], half), bf16))
    return pl.pallas_call(
        partial(mid_body, plan),
        out_shape=vm_out + any_out,
        in_specs=vmem(5) + anywhere(8),
        out_specs=tuple(vmem(len(vm_out)) + anywhere(len(any_out))),
        scratch_shapes=[
            VM(pick_att.shape, bf16), VM(pick_att.shape, bf16), VM((slots, width), bf16),
            VM(p_shape, bf16), VM((2, ff, half), bf16), VM((ff, half), bf16), VM((2, n, 128, part), bf16),
        ]
        + bufs
        + [
            VM((n, cap, part), bf16), VM((slots, width), bf16), VM((slots, width), bf16),
            VM((2, ffp, width), bf16), VM((ffp, width), bf16), VM((slots, ffp), f32),
            VM((slots, ffp), bf16), VM((slots, ffp), bf16), VM((slots, ffp), bf16), VM((ffp, slots), bf16),
            VM(p_shape, bf16), VM((tok, part), bf16),
            VM((16, tok), f32), VM((TP - 1, 16, tok), f32), VM((8, tok), f32), VM((TP - 1, 8, tok), f32),
            VM((tok, 128), f32), VM((n, 8, 128), f32), VM((n, 8, 128), f32), VM((n, 128, 128), f32),
            VM((n, 8, 128), f32), VM((TP - 1, n, 8, 128), f32), VM((n, 8, 128), f32), VM((n, 8, 128), f32),
            VM((2, ff, cols), bf16), VM((tok, part), bf16), VM((tok, part), bf16), VM((n, cap, part), bf16), DMA((16,)), DMA((2,)),
        ]
        + sems(Collect.COPIES + 2 * Dispatch.COPIES + 80),
        compiler_params=params(cid),
        cost_estimate=cost(140),
    )(
        ret_att, info, routes, norm_mid, router_t, pick_att, pick_mlp, tokens, cot, rows_g, gu_own, gu_oth, down_own,
    )


def back_body(
    cap, tok, cuts,
    q_ref, pos_ref, att_ref, lse_ref, hidden, gates_mlp, att_picked, grad_hidden, info, routes, norm_in, router_t,
    norm_mid_grad, router_mlp_grad,
    proj_any, rows_any, kv_any, p1_any, q_own, q_oth, o_own, o_oth, full_any, lowered_any, pick_att_any, pick_mlp_any,
    tokens, gu_sent,
    kvw_out, result, input_grad, minor_out, q_sent, o_grad, q_grad, gu_got, o_got,
    rows_ref, kv_ref, p_ref, wq, wo, do_ref, dq_ref, kt_ref, acc_ref, o_sent, o_keep, q_keep,
    b_sib, b_a, b_b, b_l, b_r, b_f,
    seq_stage, seq_half, seq_whole, over_out, over_in, own_ref, kv_low,
    p2, c2_sib, c2_a, c2_b, c2_l, c2_r, c2_f,
    w_part, w_stage, w_half, w_whole, w_sum, wz_stage, wz_half, wz_whole,
    ret, mlp_ret, mlp_total, kv_back, x_res, x_in, small_out, small_in, minor, minor_in, minor_sum, rgrad, toks, lowered,
    credit, local_sem, send, recv,
):
    at, net, first_net, local = Place(), Net(send, recv, Collect.COPIES), Net(send, recv), Local(local_sem)
    heads = q_ref.shape[1] // HD
    width = heads * HD
    full_width = width * TP
    w = 2 * width
    part = width
    kv_part = full_width // (FSDP * CTX)
    scale = HD ** (-0.5)
    total = q_ref.shape[0]
    half = o_own.shape[1]
    mine = pl.ds(pl.multiple_of(at.t * part, part), part)
    load_o = assemble(o_own, o_oth, wo, 1, at.f, local) + [local.go(proj_any, rows_ref)]
    load_p = local.go(p1_any, p_ref)
    load_kv = local.go(kv_any, kv_ref)
    load_q = assemble(q_own, q_oth, wq, 0, at.f, local)
    load_t = [local.go(tokens, toks), local.go(lowered_any, lowered)]
    ret[...] = jnp.zeros_like(ret)
    mlp_ret[...] = jnp.zeros_like(mlp_ret)
    acc_ref[...] = jnp.zeros_like(acc_ref)
    near_tp = tp_peers(at)
    far_all = all_peers(at)
    greet(far_all + near_tp)

    unit = gu_sent.shape[1] // 22
    gu_rows = gu_got.shape[1]
    before = gu_sent.shape[1] - gu_rows
    lead = unit * cuts[0]
    feeder = Feeder(net, at.partner, [
        (gu_sent, gu_got.at[:, pl.ds(0, lead)], 1, before, lead, unit),
        (o_sent, o_got, 0, 0, o_sent.shape[0], o_sent.shape[0] // 4),
        (gu_sent, gu_got.at[:, pl.ds(lead, gu_rows - lead)], 1, before + lead, gu_rows - lead, unit),
    ])
    feeder.feed(cuts[0])
    load_p.wait()
    col1 = Collect(first_net, at, p_ref, mlp_ret, b_sib, b_a, b_b, b_l, b_r, b_f, home_net=net, total=mlp_total)
    col1.start()
    for d in load_o:
        d.wait()
    do_ref[...] = nt(rows_ref[...], wo[...]).astype(bf16)
    col1.hop1()

    step_cols = 256
    steps = half // step_cols
    att_t = att_ref[...].T
    for i in range(steps):
        here = slice(i * step_cols, (i + 1) * step_cols)
        own_cols = pl.ds(pl.multiple_of(at.f * half + i * step_cols, step_cols), step_cols)
        other_cols = pl.ds(pl.multiple_of((1 - at.f) * half + i * step_cols, step_cols), step_cols)
        o_sent[:, here] = nn(att_t, rows_ref[:, other_cols]).astype(bf16)
        o_keep[:, here] = nn(att_t, rows_ref[:, own_cols]).astype(bf16)
    feeder.feed(cuts[1])
    saves = [local.go(o_keep, o_grad)]
    load_rows = local.go(rows_any, rows_ref)
    load_kv.wait()
    for h in range(heads):
        kt_ref[h] = kv_ref[:, 2 * h * HD : (2 * h + 1) * HD].T
    rows_at, keys_at = 2 * cap, 2 * tok
    key_scale = jnp.where(lax.broadcasted_iota(jnp.int32, (1, 2 * HD), 1) < HD, scale, 1.0)

    def seq_sum(h, zh):
        i = 2 * h + zh
        span = slice(2 * h * HD, 2 * (h + 1) * HD)
        lands = {"a": seq_half.at[i, 0], "b": seq_half.at[i, 1], "l": seq_whole.at[i, 0], "r": seq_whole.at[i, 1]}

        def own(y, p):
            size = tok if p is None else tok // 2
            lo = zh * 4 * tok + y * tok + (0 if p is None else p * (tok // 2))
            return acc_ref[pl.ds(pl.multiple_of(lo, 64), size), span] * key_scale

        return RingSum(
            net, own, lambda y, p: seq_stage.at[i, y, part_of(p, tok)], lambda name: lands[name],
            at.y, at.up, at.down,
        )

    seqs = [[seq_sum(h, zh) for zh in range(2)] for h in range(heads)]
    first_half = at.zh == 0
    overs = [None] * heads

    def seq_done(h, zh):
        span = slice(2 * h * HD, 2 * (h + 1) * HD)
        total_here = seqs[h][zh].hop3()
        if zh == 1:
            own_ref[:, span] = total_here
            return
        high = own_ref[:, span]
        over_out[h] = jnp.where(first_half, high, total_here).astype(bf16)
        own_ref[:, span] = jnp.where(first_half, total_here, high)
        overs[h] = net.go(over_out.at[h], over_in.at[h], at.across)

    for h in range(heads):
        cols = slice(h * HD, (h + 1) * HD)
        kcols = slice(2 * h * HD, (2 * h + 1) * HD)
        vcols = slice((2 * h + 1) * HD, (2 * h + 2) * HD)
        for g in reversed(range(total // rows_at)):
            lo = g * rows_at
            rows = slice(lo, lo + rows_at)
            extent = (g + 1) * keys_at
            at_key = extent - keys_at
            pos = pair_positions(pos_ref, g, cap)
            q = q_ref[rows, cols]
            do = do_ref[rows, cols]
            s = nt(kv_ref[:extent, kcols], q) * scale
            lse = lse_ref[h : h + 1, rows]
            ids = lax.broadcasted_iota(jnp.int32, (keys_at, rows_at), 0) + at_key
            last = jnp.where(ids <= pos, s[at_key:], masked_score)
            s = jnp.concatenate([s[:at_key], last], axis=0) if g else last
            soft = jnp.exp(s - lse)
            dp = nt(kv_ref[:extent, vcols], do)
            inner = jnp.sum(soft * dp, axis=0, keepdims=True)
            ds = (soft * (dp - inner)).astype(bf16)
            acc_ref[:extent, vcols] += nn(soft.astype(bf16), do)
            acc_ref[:extent, kcols] += nn(ds, q)
            dq_ref[rows, cols] = (nn(kt_ref[h, :, :extent], ds) * scale).T.astype(bf16)
            if h == 0 and g == 3:
                col1.hop2()
            if g == 2:
                seqs[h][1].hop1()
            if h == 0 and g == 2:
                col1.hop3()
                for axes in at.tp_near():
                    pl.semaphore_signal(credit, inc=1, device_id=axes, device_id_type=MESH)
            if g == 1:
                seqs[h][1].hop2()
            if g == 0:
                seqs[h][0].hop1()
            if h == 1 and g == 3:
                seq_done(0, 1)
                seqs[0][0].hop2()
            if h == 1 and g == 1:
                seq_done(0, 0)
                feeder.feed(cuts[2])
    load_full = local.go(full_any, kv_ref.at[pl.ds(0, full_width)])
    for d in load_q:
        d.wait()
    first_net.drain()
    for g in range(total // rows_at):
        rows = slice(g * rows_at, (g + 1) * rows_at)
        out = nt(dq_ref[rows, :], wq[...]).astype(bf16)
        for i in range(TP):
            for b in range(2):
                p_ref[i % 2, i // 2, 2 * g + b] = out[b * cap : (b + 1) * cap, i * width : (i + 1) * width]
    pl.semaphore_wait(credit, 3)
    col = Collect(net, at, p_ref, ret, b_sib, b_a, b_b, b_l, b_r, b_f)
    col.start()
    seq_done(1, 1)
    seqs[1][0].hop2()
    col.hop1()
    load_rows.wait()
    for i in range(steps):
        here = slice(i * step_cols, (i + 1) * step_cols)
        own_cols = pl.ds(pl.multiple_of(at.f * half + i * step_cols, step_cols), step_cols)
        other_cols = pl.ds(pl.multiple_of((1 - at.f) * half + i * step_cols, step_cols), step_cols)
        q_sent[here, :] = tn(rows_ref[:, other_cols], dq_ref[...]).astype(bf16)
        q_keep[here, :] = tn(rows_ref[:, own_cols], dq_ref[...]).astype(bf16)
    saves.append(local.go(q_keep, q_grad))
    picks = full_width // 2
    load_picks = [
        local.go(pick_att_any, rows_ref.at[:, pl.ds(0, picks)]),
        local.go(pick_mlp_any, rows_ref.at[:, pl.ds(picks, picks)]),
    ]
    low_half = slice(0, 2 * HD)
    overs[0].wait_recv()
    kv_low[:, low_half] = (own_ref[:, low_half] + wide(over_in[0])).astype(bf16)
    seq_done(1, 0)
    feeder.feed(cuts[3])

    def index(z, y):
        return lax.rem(z, 2) * CTX + (z // 2) * 4 + y

    order = [lax.rem(at.z + i, 4) for i in (2, 1, 3, 0)]

    def weight_rings(h):
        span = slice(2 * h * HD, 2 * (h + 1) * HD)
        low = kv_low[:, span]
        for i in range(4):
            cols = full_width // 4
            block = tn(lowered[:, i * cols : (i + 1) * cols], low).astype(bf16)
            per = cols // kv_part
            w_part[h, i * per : (i + 1) * per] = block.reshape(per, kv_part, 2 * HD)
        out = []
        for i, z in enumerate(order):
            lands = {
                "a": w_half.at[h, i, 0], "b": w_half.at[h, i, 1], "l": w_whole.at[h, i, 0], "r": w_whole.at[h, i, 1]
            }
            out.append(RingSum(
                net,
                lambda y, p, z=z: wide(w_part[h, index(z, y), part_of(p, kv_part)]),
                lambda y, p, i=i: w_stage.at[h, i, y, part_of(p, kv_part)],
                lambda name, lands=lands: lands[name],
                at.y, at.up, at.down,
            ))
        for ring in out:
            ring.hop1()
        return out

    for d in load_t:
        d.wait()
    wrings = [weight_rings(0)]
    col.hop2()
    load_full.wait()
    for ring in wrings[0]:
        ring.hop2()
    col1.finish()
    for d in load_picks:
        d.wait()
    picked = nn(rows_ref[:, picks:], mlp_ret[...].reshape(-1, part))
    gates = gates_mlp[...]
    value = hidden[...] + gates[:, 0:1] * picked[:tok] + gates[:, 1:2] * picked[tok:]
    x_res[...] = value.astype(bf16).reshape(x_res.shape)
    d_res = Dispatch(net, at, x_res, result, exchange=False)
    d_res.start()
    d_res.hop1()
    col.hop3()
    feeder.feed(cuts[4])
    high_half = slice(2 * HD, 4 * HD)
    overs[1].wait_recv()
    kv_low[:, high_half] = (own_ref[:, high_half] + wide(over_in[1])).astype(bf16)
    back_rows = nt(kv_low[...], kv_ref[:full_width, :])
    n2, rows2, w2 = p2.shape[2:]
    for i in range(TP):
        p2[i % 2, i // 2] = back_rows[:, i * w2 : (i + 1) * w2].astype(bf16).reshape(n2, rows2, w2)
    col2 = Collect(net, at, p2, kv_back, c2_sib, c2_a, c2_b, c2_l, c2_r, c2_f, exchange=False)
    col2.start()
    inner_kv = jnp.sum(back_rows * (wide(toks[...]) * norm_in[0:1, :]), axis=1, keepdims=True)
    wrings.append(weight_rings(1))
    col2.hop1()
    d_res.hop2()
    feeder.feed(cuts[5])
    for ring in wrings[1]:
        ring.hop2()
    col.finish()
    feeder.feed(cuts[6])
    col2.hop2()

    inputs = wide(toks[:, mine])
    norm = norm_in[0:1, mine]
    gh = grad_hidden[...]
    grad_low = nn(rows_ref[:, :picks], ret[...].reshape(-1, part))
    grad_low = grad_low[:tok] + grad_low[tok:]
    lane = lax.broadcasted_iota(jnp.int32, (tok, 128), 1)
    facts = info[...]
    d0 = jnp.sum(wide(att_picked[:tok, :]) * gh, axis=1, keepdims=True)
    d1 = jnp.sum(wide(att_picked[tok:, :]) * gh, axis=1, keepdims=True)
    inner = jnp.sum(grad_low * norm * inputs, axis=1, keepdims=True) + inner_kv
    sums = jnp.where(lane == 0, d0, jnp.where(lane == 1, d1, jnp.where(lane == 2, inner, 0.0)))
    small_out[...] = to_row_form(sums, 8)
    smalls = [net.go(small_out, small_in.at[j], p) for j, p in enumerate(near_tp)]
    for h in range(heads):
        for z, ring in zip(order, wrings[h]):
            w_sum[z, :, 2 * h * HD : 2 * (h + 1) * HD] = ring.hop3()

    lands = {"a": wz_half.at[0], "b": wz_half.at[1], "l": wz_whole.at[0], "r": wz_whole.at[1]}
    zsum = RingSum(
        net,
        lambda z, p: w_sum[z, part_of(p, kv_part)],
        lambda z, p: wz_stage.at[z, part_of(p, kv_part)],
        lambda name: lands[name],
        at.z, at.above, at.below,
    )
    zsum.hop1()
    col2.hop3()
    grad_low = grad_low + wide(kv_back[...].reshape(tok, part))
    total_row = small_out[...]
    for j, m in enumerate(smalls):
        m.wait_recv()
        total_row = total_row + small_in[j]
    sums = to_column_form(total_row)
    row_scale, g0, g1 = facts[:, 0:1], facts[:, 1:2], facts[:, 2:3]
    inner = g0 * sums[:, 0:1] + g1 * sums[:, 1:2]
    hot = hot_lanes(routes[...])
    grad_logits = hot[0] * (g0 * (sums[:, 0:1] - inner)) + hot[1] * (g1 * (sums[:, 1:2] - inner))
    for e in range(CTX):
        grad_low = grad_low + grad_logits[:, FIRST + e : FIRST + e + 1] * router_t[e : e + 1, mine]
    inner = sums[:, 2:3] + jnp.sum(grad_logits * facts, axis=1, keepdims=True)
    cubed = row_scale * row_scale * row_scale
    grad = gh + row_scale * (grad_low * norm) - inputs * cubed * (inner / full_width)
    x_in[...] = grad.astype(bf16).reshape(x_in.shape)
    d_in = Dispatch(net, at, x_in, input_grad, exchange=False)
    d_in.start()
    d_in.hop1()
    rgrad[...] = sum(tn(g, lowered[:, mine]) for g in split3(grad_logits))
    norm_grad = jnp.sum(grad_low * inputs * row_scale, axis=0, keepdims=True)
    row = lax.broadcasted_iota(jnp.int32, (8, part), 0)
    minor[0:8, :] = jnp.where(row == 0, norm_grad, jnp.where(row == 1, norm_mid_grad[0:1, :], 0.0))
    minor[8:16, :] = rgrad[FIRST : FIRST + CTX, :]
    minor[16:24, :] = router_mlp_grad[FIRST : FIRST + CTX, :]
    minors = [net.go(minor, minor_in.at[j], p) for j, p in enumerate(far_all)]
    zsum.hop2()
    feeder.feed(100)
    d_in.hop2()
    d_res.hop3()
    total_row = minor[...]
    for j, m in enumerate(minors):
        m.wait_recv()
        total_row = total_row + minor_in[j]
    minor_sum[...] = total_row
    minors = [net.go(minor_sum, minor_out.at[at.t], p) for p in near_tp]
    minor_out[at.t] = total_row
    d_in.hop3()
    kvw_out[...] = zsum.hop3()
    d_res.finish()
    d_in.finish()
    col2.finish()
    for m in minors:
        m.wait_recv()
    feeder.finish()
    for d in saves:
        d.wait()
    net.drain()


def back(small, large, cuts, gu_rows, tok, cap, cid):
    q = small[0]
    proj, rows, kv, p1, q_own, _, o_own, _, _, lowered, _, _, _, gu_sent = large
    slots, w = q.shape
    heads = w // HD
    width = w * TP
    kw = 2 * w
    part = width // (FSDP * CTX)
    _, _, n, _, _ = p1.shape
    n2 = 4
    rows2 = tok // n2
    ff, half = gu_sent.shape[1:]
    vm_out = (
        sds((part, kw), f32), sds((tok, width), bf16), sds((tok, width), bf16), sds((TP, 24, w), f32),
        sds(q_own.shape, bf16),
    )
    any_out = (
        sds(o_own.shape, bf16), sds(q_own.shape, bf16), sds((2, gu_rows, half), bf16),
        sds(o_own.shape, bf16),
    )
    out = pl.pallas_call(
        partial(back_body, cap, tok, cuts),
        out_shape=vm_out + any_out,
        in_specs=vmem(len(small)) + anywhere(len(large)),
        out_specs=tuple(vmem(len(vm_out)) + anywhere(len(any_out))),
        scratch_shapes=[
            VM((slots, width), bf16), VM(kv.shape, bf16), VM(p1.shape, bf16),
            VM((width, w), bf16), VM((w, width), bf16), VM((slots, w), bf16), VM((slots, w), bf16), VM((heads, HD, kv.shape[0]), bf16), VM(kv.shape, f32),
            VM(o_own.shape, bf16), VM(o_own.shape, bf16), VM(q_own.shape, bf16),
        ]
        + Collect.scratch(n, cap, w)
        + [
            VM((2 * heads, 4, tok, w), bf16), VM((2 * heads, 2, tok // 2, w), bf16), VM((2 * heads, 2, tok, w), bf16),
            VM((heads, tok, w), bf16), VM((heads, tok, w), bf16), VM((tok, kw), f32), VM((tok, kw), bf16),
        ]
        + [VM((2, 4, n2, rows2, w), bf16)] + Collect.scratch(n2, rows2, w)
        + [
            VM((heads, FSDP * CTX, part, w), bf16), VM((heads, 4, 4, part, w), bf16),
            VM((heads, 4, 2, part // 2, w), bf16), VM((heads, 4, 2, part, w), bf16), VM((4, part, kw), f32), VM((4, part, kw), bf16),
            VM((2, part // 2, kw), bf16), VM((2, part, kw), bf16),
            VM((n, 128, w), bf16), VM((n, 128, w), bf16), VM((n, cap, w), bf16), VM((n2, rows2, w), bf16),
            VM((n2, rows2, w), bf16), VM((n2, rows2, w), bf16), VM((8, tok), f32), VM((TP - 1, 8, tok), f32),
            VM((24, w), f32), VM((FSDP * CTX - 1, 24, w), f32), VM((24, w), f32), VM((128, w), f32),
            VM((tok, width), bf16), VM((tok, width), bf16),
            pltpu.SemaphoreType.REGULAR, DMA((20,)),
        ]
        + sems(Collect.COPIES * 3 + Dispatch.COPIES * 2 + 180),
        compiler_params=params(cid),
        cost_estimate=cost(120),
    )(*small, *large)
    kvw, result, input_grad, minor, q_sent, o_grad, q_grad, gu_got, o_got = out
    return o_grad, q_grad, kvw, result, input_grad, minor, gu_got, o_got, q_sent


def finish_body(
    gu_a, gu_b, gu_c, dd_a, dd_b, o_a, o_b, ig, res, kvw, minor,
    gu, dd, o, grad, result, kv, n_in, n_mid, r_att, r_mlp, *refs,
):
    ins, outs, (load_sem, save_sem) = refs[:8], refs[8:12], refs[12:]
    me = lax.axis_index("fsdp") * CTX + lax.axis_index("ctx")
    early = gu_b.shape[1]
    sources = (gu_a, None, dd_a, dd_b, o_a, o_b, ig)
    pieces = [(0, j, i) for j in range(2) for i in range(4)] + [(2, 0, i) for i in range(4)]
    pieces += [(4, 0, 0)] + [(6, 0, i) for i in range(2)]
    targets = {0: (gu, outs[0]), 2: (dd, outs[1]), 4: (o, outs[2]), 6: (grad, outs[3])}
    counts = {0: 4, 2: 4, 4: 1, 6: 2}

    def span(ref, k, j, i):
        rows = ref.shape[-2] // counts[k]
        s = pl.ds(i * rows, rows)
        return ref.at[j, s] if k == 0 else ref.at[s]

    loads = []
    for n, (k, j, i) in enumerate(pieces):
        both = []
        if k == 0:
            rows = ins[1].shape[1] // counts[0]
            lo, hi = i * rows, (i + 1) * rows
            for m, (src, a, b, shift) in enumerate(
                ((gu_b, lo, min(hi, early), 0), (gu_c, max(lo, early), hi, early))
            ):
                if a < b:
                    d = pltpu.make_async_copy(
                        src.at[j, pl.ds(a - shift, b - a)], ins[1].at[j, pl.ds(a, b - a)], load_sem.at[n, 1 + m]
                    )
                    d.start()
                    both.append(d)
        for m in range(1 if k in (0, 6) else 2):
            d = pltpu.make_async_copy(span(sources[k + m], k, j, i), span(ins[k + m], k, j, i), load_sem.at[n, m])
            d.start()
            both.append(d)
        loads.append(both)
    copy = pltpu.make_async_copy(res, ins[7], load_sem.at[len(pieces), 0])
    copy.start()
    w = kv.shape[2]
    for h in range(w // HD):
        for j in range(2):
            kv[j, :, h * HD : (h + 1) * HD] = kvw[:, (2 * h + j) * HD : (2 * h + j + 1) * HD]
    mine = minor[me // 2, :, pl.ds(pl.multiple_of(lax.rem(me, 2) * 128, 128), 128)]
    n_in[...] = mine[0:1]
    n_mid[...] = mine[1:2]
    r_att[...] = mine[8:16]
    r_mlp[...] = mine[16:24]
    copy.wait()
    saves = [pltpu.make_async_copy(ins[7], result, load_sem.at[len(pieces), 1])]
    saves[0].start()
    for n, (k, j, i) in enumerate(pieces):
        for d in loads[n]:
            d.wait()
        v = wide(span(ins[k], k, j, i)[...])
        if k != 6:
            v = v + wide(span(ins[k + 1], k, j, i)[...])
        dst, buf = targets[k]
        span(buf, k, j, i)[...] = v
        d = pltpu.make_async_copy(span(buf, k, j, i), span(dst, k, j, i), save_sem.at[n])
        d.start()
        saves.append(d)
    for d in saves:
        d.wait()


def finish(gu_a, gu_b, gu_c, dd_a, dd_b, o_a, o_b, ig, res, kvw, minor):
    part, kw = kvw.shape
    args = (gu_a, gu_b, gu_c, dd_a, dd_b, o_a, o_b, ig, res)
    held = (gu_a, gu_a) + args[3:]
    sums = [sds(z.shape, f32) for z in (gu_a, dd_a, o_a, ig)]
    return pl.pallas_call(
        finish_body,
        out_shape=tuple(sums) + (
            sds(res.shape, res.dtype), sds((2, part, kw // 2), f32), sds((1, part), f32), sds((1, part), f32),
            sds((CTX, part), f32), sds((CTX, part), f32),
        ),
        in_specs=anywhere(9) + vmem(2),
        out_specs=tuple(anywhere(5) + vmem(5)),
        scratch_shapes=[VM(z.shape, z.dtype) for z in held] + [VM(z.shape, f32) for z in sums]
        + [DMA((20, 3)), DMA((20,))],
        compiler_params=params(),
        cost_estimate=cost(9),
    )(*args, kvw, minor)


def local(
    tokens, norm_in, norm_mid, router_att, router_mlp, kv_weight, query_weight, output_weight,
    gate_up_weight, down_weight, routes_att, routes_mlp, cotangent,
):
    count_rows, width = tokens.shape[1:]
    capacity = count_rows * 2 // CTX
    local_width = query_weight.shape[2]
    tokens, cotangent = tokens[0], cotangent[0]
    q_own, o_own, down_own = query_weight[0], output_weight[0], down_weight[0]
    gu_own = gate_up_weight[0].transpose(0, 2, 1)
    routes_att, routes_mlp = routes_att[0].T, routes_mlp[0].T
    norm_in, norm_mid = norm_in[None], norm_mid[None]
    router_att, router_mlp = router_att.T, router_mlp.T
    hidden_count = gu_own.shape[1]
    unit = hidden_count // 44
    plan = {"down": (18 * unit, 18 * unit), "dd": (4, 5, 2), "gu": 8 * unit}
    pieces = (8, 4, 4, 2, 4, 0, 0)

    (
        positions, info, queries, attended, log_totals, ret_att,
        rows_att, kv_seq, kv_full, lowered, pick_att, pick_mlp, rows_g, q_oth, o_oth, gu_oth,
    ) = front(
        norm_in, router_att, routes_att, routes_mlp, kv_weight, tokens, cotangent, q_own, o_own, gu_own,
        capacity, (14, 20), 34 * unit, 1,
    )
    kv_seq = kv_seq.reshape(-1, 2 * local_width)
    (
        att_picked, hidden, gates_mlp, grad_hidden, norm_mid_grad, router_mlp_grad, grad_proj, p_mlp, gu_sent,
        gu_grad, dd_grad, dd_got, gu_got_0,
    ) = mid(
        plan, ret_att, info, routes_mlp, norm_mid, router_mlp, pick_att, pick_mlp, tokens, cotangent,
        rows_g, gu_own, gu_oth, down_own, 3,
    )
    o_grad, q_grad, kvw_grad, result, input_grad, minor, gu_got, o_got, q_sent = back(
        (queries, positions, attended, log_totals, hidden, gates_mlp, att_picked, grad_hidden, info, routes_att,
         norm_in, router_att, norm_mid_grad, router_mlp_grad),
        (grad_proj, rows_att, kv_seq, p_mlp, q_own, q_oth, o_own, o_oth, kv_full.reshape(width, 2 * local_width),
         lowered, pick_att, pick_mlp, tokens, gu_sent),
        pieces, hidden_count - plan["gu"], count_rows, capacity, 4,
    )
    q_got = lax.ppermute(q_sent, "fsdp", [(0, 1), (1, 0)])
    gu_all, dd_all, o_all, input_grad, result, kvw_grad, n_in, n_mid, r_att, r_mlp = finish(
        gu_grad, gu_got_0, gu_got, dd_grad, dd_got, o_grad, o_got, input_grad, result, kvw_grad, minor
    )
    return (
        result[None], input_grad[None], n_in[0], n_mid[0], r_att.T, r_mlp.T, kvw_grad, (q_grad.astype(f32) + q_got.astype(f32))[None], o_all[None],
        gu_all.transpose(0, 2, 1)[None], dd_all[None],
    )


def solution(mesh):
    placed = (
        P("fsdp", "ctx", None), P(), P(), P(), P(),
        P(None, ("fsdp", "ctx"), "tp"), P("ctx", "fsdp", "tp"), P("ctx", "tp", "fsdp"),
        P("ctx", None, "fsdp", "tp"), P("ctx", "tp", "fsdp"),
        P("fsdp", "ctx", None), P("fsdp", "ctx", None), P("fsdp", "ctx", None),
    )
    return jax.shard_map(
        local,
        mesh=mesh,
        in_specs=placed,
        out_specs=(
            P("fsdp", "ctx", None), P("fsdp", "ctx", None), P(("fsdp", "ctx")), P(("fsdp", "ctx")),
            P(("fsdp", "ctx"), None), P(("fsdp", "ctx"), None), P(None, ("fsdp", "ctx"), "tp"),
            P("ctx", "fsdp", "tp"), P("ctx", "tp", "fsdp"), P("ctx", None, "fsdp", "tp"), P("ctx", "tp", "fsdp"),
        ),
        check_vma=False,
    )
```
